32 devices in a mesh: parts: 2 (over x), tile: 16 (over z, y, core).
Axes of the slice: x: 2, y: 2, z: 4, core: 2. Of those that a mesh axis runs over, the one named last changes fastest.
Arguments:
- sections: bfloat16 [4096, 2048], P(('parts', 'tile')), parts along dimension 0, may hold values from -10 to 10
- valid_mask: int32 [32, 16], P(('parts', 'tile')), parts along dimension 0, may hold values 0 or 1
- coarse_offsets: int32 [8, 2], P('parts'), parts along dimension 0, may hold values from -3 to 3
Outputs:
- aligned: bfloat16 [4096, 2048], P(('parts', 'tile')), parts along dimension 0
- node_shift: float32 [2, 32, 16], P(None, ('parts', 'tile')), parts along dimension 1
The draws below stay inside these ranges and needn't reach their ends.
There are 2 independent parts, one for each index of `parts`. The reference program is written for one: setup_inputs(seed, part) draws one part's arguments, and reference() takes and returns one part's arrays. A program takes and returns all parts, laid end to end along the dimension named above; each array names one. Nothing has to cross between parts.
All inputs are finite; a program needn't handle non-finite values. No bound on the sum of `valid_mask` on one device may be relied on, other than what follows from the above.
Results may differ from the reference program's by a relative error of at most 0.002.
Values may be sent and summed in bfloat16 or wider, within the bound.
No kernel may reach another device: no remote copies, remote signals or barrier semaphores. Data moves between devices by JAX's collectives and lax.ppermute only.
A program may use at most 64 MiB of HBM per device.

```python
import jax
import jax.numpy as jnp
from jax import lax

SECTIONS = 4
PATCH = 128
PC = 16
HALF = 4
SWEEPS = 3
TPS = 4


def draw_sections(key, part):
    row_count = TPS * PATCH
    col_count = PC * PATCH
    common_key = jax.random.fold_in(key, 11)
    own_key = jax.random.fold_in(key, 12)
    common = jax.random.normal(common_key, (row_count, col_count), jnp.float32)
    own_part = jax.random.normal(own_key, (SECTIONS, row_count, col_count), jnp.float32)
    volume = jnp.clip(0.6 * common[None] + 0.8 * own_part, -6.0, 6.0)
    return volume.reshape(SECTIONS * row_count, col_count).astype(jnp.bfloat16)


def touch_ends(drawn, stream_key, least, largest):
    spot = [jax.random.randint(jax.random.fold_in(stream_key, axis), (), 0, length) for axis, length in enumerate(drawn.shape)]
    widest = drawn.shape.index(max(drawn.shape))
    neighbour = spot[:widest] + [(spot[widest] + 1) % drawn.shape[widest]] + spot[widest + 1:]
    return drawn.at[tuple(spot)].set(least).at[tuple(neighbour)].set(largest)


def setup_inputs(seed: int = 0, part: int = 0) -> dict:
    splits = jax.random.split(jax.random.key(seed), 4)
    part_keys = jax.random.split(jax.random.fold_in(splits[3], part), 4)
    sections = draw_sections(jax.random.fold_in(jax.random.fold_in(splits[3], part), 71), part)
    valid_mask = touch_ends((jax.random.randint(part_keys[1], (SECTIONS * TPS, PC), 0, 4) < 3).astype(jnp.int32), jax.random.fold_in(part_keys[1], 1), 0, 1)
    coarse_offsets = touch_ends(jax.random.randint(part_keys[2], (SECTIONS, 2), -3, 4), jax.random.fold_in(part_keys[2], 1), -3, 3).astype(jnp.int32)
    return {"sections": sections, "valid_mask": valid_mask, "coarse_offsets": coarse_offsets}


highest = lax.Precision.HIGHEST
sharpness = 12.0
anchor_weight = 2.0

def fourier_tables(length):
    index_vector = jnp.arange(length, dtype=jnp.int32)
    phase_index = index_vector[:, None] * index_vector[None, :] % length
    angles = phase_index.astype(jnp.float32) * (2.0 * jnp.pi / length)
    return (jnp.cos(angles), -jnp.sin(angles))

def left_apply(matrix, blocks):
    return jnp.einsum('jk,...kl->...jl', matrix, blocks, precision=highest)

def right_apply(blocks, matrix):
    return jnp.einsum('...jk,kl->...jl', blocks, matrix, precision=highest)

def forward(blocks, cosine_table, sine_table):
    first_re = left_apply(cosine_table, blocks)
    first_im = left_apply(sine_table, blocks)
    out_re = right_apply(first_re, cosine_table) - right_apply(first_im, sine_table)
    out_im = right_apply(first_re, sine_table) + right_apply(first_im, cosine_table)
    return (out_re, out_im)

def centred(blocks):
    mean_level = lax.optimization_barrier(jnp.mean(blocks, axis=(-2, -1), keepdims=True))
    centre = blocks - mean_level
    spread = jnp.sqrt(lax.optimization_barrier(jnp.mean(centre * centre, axis=(-2, -1), keepdims=True)) + 1e-05)
    return (centre, mean_level, spread)

def window_tables(offset, length):
    shift_values = offset + jnp.arange(-HALF, HALF + 1, dtype=jnp.int32)
    frequency = jnp.arange(length, dtype=jnp.int32)
    phase_index = jnp.mod(shift_values[:, None] * frequency[None, :], length)
    angles = phase_index.astype(jnp.float32) * (2.0 * jnp.pi / length)
    return (jnp.cos(angles), jnp.sin(angles), shift_values.astype(jnp.float32))

def estimate_flow(own_re, own_im, own_spread, prev_re, prev_im, prev_spread, offset_pair):
    length = PATCH
    cross_re = own_re * prev_re + own_im * prev_im
    cross_im = own_im * prev_re - own_re * prev_im
    row_cos, row_sin, row_shifts = window_tables(offset_pair[0], length)
    col_cos, col_sin, col_shifts = window_tables(offset_pair[1], length)
    half_re = left_apply(row_cos, cross_re) - left_apply(row_sin, cross_im)
    half_im = left_apply(row_cos, cross_im) + left_apply(row_sin, cross_re)
    correlation = jnp.einsum('...jk,lk->...jl', half_re, col_cos, precision=highest) - jnp.einsum('...jk,lk->...jl', half_im, col_sin, precision=highest)
    similarity = correlation / (float(length) ** 4 * own_spread * prev_spread)
    weights = jnp.exp(sharpness * similarity)
    weight_sum = lax.optimization_barrier(jnp.sum(weights, axis=(-2, -1), keepdims=True))
    chance = weights / weight_sum
    flow_rows = lax.optimization_barrier(jnp.sum(chance * row_shifts[:, None], axis=(-2, -1)))
    flow_cols = lax.optimization_barrier(jnp.sum(chance * col_shifts[None, :], axis=(-2, -1)))
    return jnp.stack([flow_rows, flow_cols], axis=0)

def warp_patches(spec_re, spec_im, mean_level, shift_rows, shift_cols, cosine_table, sine_table):
    length = PATCH
    frequency = jnp.arange(length, dtype=jnp.int32)
    signed_freq = jnp.where(frequency < length // 2, frequency, frequency - length).astype(jnp.float32)
    phase_angle = 2.0 * jnp.pi / length * (signed_freq[:, None] * shift_rows[..., None, None] + signed_freq[None, :] * shift_cols[..., None, None])
    turn_cos = jnp.cos(phase_angle)
    turn_sin = jnp.sin(phase_angle)
    moved_re = spec_re * turn_cos - spec_im * turn_sin
    moved_im = spec_re * turn_sin + spec_im * turn_cos
    back_re = cosine_table
    back_im = -sine_table
    inner_re = left_apply(back_re, moved_re) - left_apply(back_im, moved_im)
    inner_im = left_apply(back_re, moved_im) + left_apply(back_im, moved_re)
    restored = right_apply(inner_re, back_re) - right_apply(inner_im, back_im)
    return restored / float(length * length) + mean_level

def relax_mesh(flow_nodes, mask_float):
    weight = anchor_weight * mask_float
    padded_ones = jnp.pad(jnp.ones_like(mask_float), 1)
    neighbour_count = padded_ones[:-2, 1:-1] + padded_ones[2:, 1:-1] + padded_ones[1:-1, :-2] + padded_ones[1:-1, 2:]
    node_shift = flow_nodes * mask_float
    for sweep_index in range(SWEEPS):
        padded = jnp.pad(node_shift, ((0, 0), (1, 1), (1, 1)))
        neighbours = padded[:, :-2, 1:-1] + padded[:, 2:, 1:-1] + padded[:, 1:-1, :-2] + padded[:, 1:-1, 2:]
        node_shift = (weight * flow_nodes + neighbours) / (weight + neighbour_count)
    return node_shift

def to_patches(strip):
    return strip.astype(jnp.float32).reshape(-1, PATCH, PC, PATCH).transpose(0, 2, 1, 3)

def from_patches(patches):
    return patches.transpose(0, 2, 1, 3).reshape(-1, PC * PATCH)

def reference(sections, valid_mask, coarse_offsets):
    half_rows = TPS // 2
    sections = jnp.roll(sections, -half_rows * PATCH, axis=0)
    valid_mask = jnp.roll(valid_mask, -half_rows, axis=0)
    cosine_table, sine_table = fourier_tables(PATCH)
    strip_rows = TPS * PATCH
    aligned_list = [sections[:strip_rows]]
    shift_list = [jnp.zeros((2, TPS, PC), jnp.float32)]
    previous = sections[:strip_rows]
    for section_index in range(1, SECTIONS):
        current = to_patches(sections[section_index * strip_rows:(section_index + 1) * strip_rows])
        own_centre, own_level, own_spread = centred(current)
        own_re, own_im = forward(own_centre, cosine_table, sine_table)
        prev_patches = to_patches(lax.optimization_barrier(previous))
        prev_centre, prev_level, prev_spread = centred(prev_patches)
        prev_re, prev_im = forward(prev_centre, cosine_table, sine_table)
        flow_nodes = estimate_flow(own_re, own_im, own_spread, prev_re, prev_im, prev_spread, coarse_offsets[section_index])
        mask_float = valid_mask[section_index * TPS:(section_index + 1) * TPS].astype(jnp.float32)
        node_shift = relax_mesh(flow_nodes, mask_float)
        warped = warp_patches(own_re, own_im, own_level, node_shift[0], node_shift[1], cosine_table, sine_table).astype(jnp.bfloat16)
        strip = from_patches(warped)
        previous = strip
        aligned_list.append(strip)
        shift_list.append(node_shift)
    aligned_all = jnp.roll(jnp.concatenate(aligned_list, axis=0), half_rows * PATCH, axis=0)
    shift_all = jnp.roll(jnp.concatenate(shift_list, axis=1), half_rows, axis=1)
    return (aligned_all, shift_all)
```

```python
import functools
import math

import jax
import jax.numpy as jnp
from jax import lax
from jax.experimental import pallas as pl
from jax.experimental.pallas import tpu as pltpu
from jax.sharding import PartitionSpec as P

SECTIONS = 4
PATCH = 128
HALF = 4
SWEEPS = 3
LANES = 128
WIDTH = 2 * HALF + 1
MASK_LANE = 64
GROUP = 2

sharpness = 12.0
anchor_weight = 2.0
f32 = jnp.float32
bf16 = jnp.bfloat16


def iota(shape, axis):
    return lax.broadcasted_iota(jnp.int32, shape, axis)


def split(value):
    high = value.astype(bf16)
    return high, (value - high.astype(f32)).astype(bf16)


def dot(lhs, rhs):
    return jnp.dot(lhs, rhs, preferred_element_type=f32)


def dot_t(lhs, rhs):
    return lax.dot_general(lhs, rhs, (((1,), (1,)), ((), ())), preferred_element_type=f32)


def sine(x):
    y = x * x
    acc = jnp.full_like(x, 1.0 / math.factorial(13))
    for order in (11, 9, 7, 5, 3, 1):
        acc = (-1.0 if order % 4 == 3 else 1.0) / math.factorial(order) + y * acc
    return x * acc


def cosine(x):
    y = x * x
    acc = jnp.full_like(x, 1.0 / math.factorial(12))
    for order in (10, 8, 6, 4, 2, 0):
        acc = (-1.0 if order % 4 == 2 else 1.0) / math.factorial(order) + y * acc
    return acc


def total(value):
    return jnp.sum(jnp.sum(value, axis=0, keepdims=True), axis=1, keepdims=True)


def tile_sum(value):
    parts = [value[r : r + 8] for r in range(0, value.shape[0], 8)]
    while len(parts) > 1:
        parts = [x + y for x, y in zip(parts[::2], parts[1::2])]
    return parts[0]


def sign_tile(shape):
    return (1 - 2 * ((iota(shape, 0) + iota(shape, 1)) % 2)).astype(f32)


def section_grid(gathered, step, rows):
    count = gathered.shape[0]
    padded = rows + 8 - rows % 8
    out = None
    for group in (step - 1, step):
        start = (group * rows + rows // 2) % count
        part = jnp.concatenate([gathered[start:], gathered[:start]], axis=0) if start else gathered
        part = part[:padded]
        out = part if out is None else out + part
    return out


def relax(grid, rows, nodes):
    shape = grid.shape
    row, lane = iota(shape, 0), iota(shape, 1)
    col = lane % nodes
    valid = (row < rows) & (lane < 2 * nodes)
    mask = pltpu.roll(grid, LANES - MASK_LANE, 1)
    one = lambda cond: jnp.where(cond, 1.0, 0.0)
    count = one(row > 0) + one(row < rows - 1) + one(col > 0) + one(col < nodes - 1)
    weight = anchor_weight * mask
    inverse = 1.0 / jnp.where(valid, weight + count, 1.0)
    pulled = weight * grid
    shift = jnp.where(valid, grid * mask, 0.0)
    for _ in range(SWEEPS):
        near = pltpu.roll(shift, 1, 0) + pltpu.roll(shift, shape[0] - 1, 0)
        near += jnp.where(col > 0, pltpu.roll(shift, 1, 1), 0.0)
        near += jnp.where(col < nodes - 1, pltpu.roll(shift, LANES - 1, 1), 0.0)
        shift = jnp.where(valid, (pulled + near) * inverse, 0.0)
    return shift


def own_row(shift, index):
    return jnp.sum(jnp.where(iota(shift.shape, 0) == index, shift, 0.0), axis=0, keepdims=True)


def kernels_of(row_shift, first, cols, nodes):
    shape = (2 * cols, LANES)
    sub, lane = iota(shape, 0), iota(shape, 1)
    is_row = sub < cols
    target = first + jnp.where(is_row, sub, sub - cols + nodes)
    shift = jnp.sum(jnp.where(lane == target, row_shift, 0.0), axis=1, keepdims=True)
    shift = jnp.broadcast_to(shift, shape)
    whole = jnp.floor(shift + 0.5)
    part = shift - whole
    steps = jnp.where(is_row, -lane, lane).astype(f32) + whole
    steps = steps - LANES * jnp.floor((steps + LANES // 2) * (1.0 / LANES))
    sign = lambda n: 1.0 - 2.0 * (n - 2.0 * jnp.floor(n * 0.5))
    swing = sine(part * math.pi)
    angle = (steps + part) * (math.pi / LANES)
    centre = (steps == 0.0) & (jnp.abs(part) < 1e-20)
    below = jnp.where(centre, 1.0, sine(angle))
    base = swing * sign(steps) * (1.0 / LANES) * cosine(angle) / below
    return jnp.where(centre, 1.0, base), swing * sign(whole)


def circulant(row):
    return pltpu.roll(jnp.broadcast_to(row, (PATCH, LANES)), 0, 1, stride=1, stride_axis=0)


def warp(patch, row_base, col_base, row_swing, col_swing, nyquist):
    row_high, row_low = split(circulant(row_base))
    col_high, col_low = split(circulant(col_base))
    inner = dot(
        jnp.concatenate([patch, patch], axis=1), jnp.concatenate([col_high, col_low], axis=0)
    )
    in_high, in_low = split(inner)
    out = dot(
        jnp.concatenate([row_high, row_low], axis=1), jnp.concatenate([in_high, in_high], axis=0)
    ) + dot(row_high, in_low)
    factor = row_swing * col_swing * nyquist * (1.0 / (PATCH * PATCH))
    return out - factor * sign_tile((PATCH, LANES))


def correlate(own, prev, base, column_offset):
    half, edge, third = PATCH // 2, 16, 3
    own32, prev32 = own.astype(f32), prev.astype(f32)
    left = []
    for i in range(third):
        amount = (PATCH + HALF - i - column_offset) % PATCH
        turned = pltpu.roll(own32, amount, 1).astype(bf16)
        left.append(jnp.concatenate([turned[:half], turned[half:]], axis=1))
    right = []
    for j in range(third):
        turned = (pltpu.roll(prev32, third * j, 1) if j else prev32).astype(bf16)
        low = jnp.concatenate([turned[PATCH - edge :], turned[: PATCH - edge]], axis=0)
        high = jnp.concatenate([turned[half - edge :], turned[: half - edge]], axis=0)
        right.append(jnp.concatenate([low, high], axis=1))
    product = dot_t(jnp.concatenate(left, axis=0), jnp.concatenate(right, axis=0))
    lane = iota((8, LANES), 1)
    sub = iota((16, LANES), 0)
    out = jnp.zeros((16, LANES), f32)
    for j in range(third):
        for i in range(third):
            block = product[i * half : (i + 1) * half, j * LANES : (j + 1) * LANES]
            band = None
            for k in range(4):
                later = (lane >= 8 * k + 32) & (lane < 8 * k + 64)
                kept = jnp.where(later, block[8 * k + 32 : 8 * k + 40], block[8 * k : 8 * k + 8])
                kept = pltpu.roll(kept, LANES - 8 * k, 1) if k else kept
                band = kept if band is None else band + kept
            band = band - base
            for step in (4, 2, 1):
                band = band + pltpu.roll(pltpu.roll(band, 8 - step, 0), LANES - step, 1)
            line = band[0:1]
            line = line + pltpu.roll(line, LANES - 32, 1)
            out = jnp.where(sub == i + third * j, line, out)
    return out


def stats(tile):
    return total(tile) * (1.0 / (PATCH * PATCH))


def chain_kernel(
    step, rows, nodes, offsets_ref, own_ref, below_ref, above_ref, mask_ref, *refs
):
    gathered_ref = refs[0] if step > 1 else None
    out_ref, score_ref, base_ref, swing_ref = refs[-4:]
    cols = nodes // 2
    count = lax.axis_size("tile")
    rotated = (lax.axis_index("tile") + count - rows // 2) % count
    group, row_index = rotated // rows, rotated % rows
    is_upper = group == step
    first = jnp.where(is_upper, cols, 0)
    if step > 1:
        shift = relax(section_grid(gathered_ref[...], step - 1, rows), rows, nodes)
        base, swing = kernels_of(own_row(shift, row_index), first, cols, nodes)
        base_ref[...] = base
        swing_ref[...] = swing
    row_offset, col_offset = offsets_ref[step, 0], offsets_ref[step, 1]
    area = float(PATCH * PATCH)

    def one(index):
        here = pl.ds(pl.multiple_of(index * PATCH, PATCH), PATCH)
        beyond = pl.ds(pl.multiple_of((index + cols) * PATCH, PATCH), PATCH)
        own = jnp.where(is_upper, own_ref[:, beyond], above_ref[:, here])
        prev = jnp.where(is_upper, below_ref[:, here], own_ref[:, here])
        own32, prev32 = own.astype(f32), prev.astype(f32)
        own_mean = stats(tile_sum(own32))
        own_var = stats(tile_sum((own32 - own_mean) * (own32 - own_mean)))
        prev_tile = tile_sum(prev32)
        prev_mean = stats(prev_tile)
        if step > 1:
            nyquist = total(prev_tile * sign_tile((8, LANES)))
            prev = warp(
                prev,
                base_ref[pl.ds(index, 1), :],
                base_ref[pl.ds(index + cols, 1), :],
                swing_ref[pl.ds(index, 1), :],
                swing_ref[pl.ds(index + cols, 1), :],
                nyquist,
            ).astype(bf16)
            prev32 = prev.astype(f32)
        centre = prev32 - prev_mean
        drift = stats(tile_sum(centre))
        prev_var = stats(tile_sum(centre * centre)) - drift * drift
        spread = jnp.sqrt((own_var + 1e-5) * (prev_var + 1e-5))
        lags = correlate(own, prev, (own_mean * (prev_mean + drift)) * (8.0 * LANES), col_offset)
        score_ref[pl.ds(index, 1)] = (lags * (sharpness / area / spread))[None]

    def body(turn, carry):
        for k in range(GROUP):
            one(turn * GROUP + k)
        return carry

    lax.fori_loop(0, cols // GROUP, body, 0)
    shape = (cols, 16, LANES)
    line, lane = iota(shape, 1), iota(shape, 2)
    row_step = 16 - lane - row_offset
    inside = (line < WIDTH) & (row_step >= -HALF) & (row_step <= HALF)
    weights = jnp.where(inside, jnp.exp(jnp.where(inside, score_ref[...], 0.0)), 0.0)
    reduce = lambda value: jnp.sum(jnp.sum(value, axis=1), axis=1, keepdims=True)
    inverse = 1.0 / reduce(weights)
    flow_row = reduce(weights * (row_step + row_offset).astype(f32)) * inverse
    flow_col = reduce(weights * (line - HALF + col_offset).astype(f32)) * inverse
    shape = (cols, LANES)
    node, lane = iota(shape, 0) + first, iota(shape, 1)
    sent = jnp.where(lane == node, flow_row, jnp.where(lane == node + nodes, flow_col, 0.0))
    sent = jnp.sum(sent, axis=0, keepdims=True)
    masks = mask_ref[...].astype(f32)
    masks = jnp.concatenate(
        [jnp.zeros((1, MASK_LANE), f32), masks, masks, jnp.zeros((1, LANES - MASK_LANE - 2 * nodes), f32)],
        axis=1,
    )
    sent = sent + jnp.where(is_upper, masks, 0.0)
    out_ref[...] = jnp.broadcast_to(sent, out_ref.shape)


def home_kernel(rows, nodes, own_ref, *refs):
    gathered_refs = refs[: SECTIONS - 1]
    out_ref, shift_ref, base_ref, swing_ref = refs[SECTIONS - 1 :]
    count = lax.axis_size("tile")
    rotated = (lax.axis_index("tile") + count - rows // 2) % count
    group, row_index = rotated // rows, rotated % rows
    grid = None
    for step in range(1, SECTIONS):
        part = section_grid(gathered_refs[step - 1][...], step, rows)
        grid = part if grid is None else jnp.where(group == step, part, grid)
    row_shift = own_row(relax(grid, rows, nodes), row_index)
    row_shift = jnp.where(group == 0, 0.0, row_shift)
    shift_ref[0, :, :] = row_shift[:, :nodes]
    shift_ref[1, :, :] = pltpu.roll(row_shift, LANES - nodes, 1)[:, :nodes]
    base, swing = kernels_of(row_shift, 0, nodes, nodes)
    base_ref[...] = base
    swing_ref[...] = swing

    def one(index):
        here = pl.ds(pl.multiple_of(index * PATCH, PATCH), PATCH)
        own = own_ref[:, here]
        nyquist = total(tile_sum(own.astype(f32)) * sign_tile((8, LANES)))
        out_ref[:, here] = warp(
            own,
            base_ref[pl.ds(index, 1), :],
            base_ref[pl.ds(index + nodes, 1), :],
            swing_ref[pl.ds(index, 1), :],
            swing_ref[pl.ds(index + nodes, 1), :],
            nyquist,
        ).astype(bf16)

    def body(turn, carry):
        for k in range(GROUP):
            one(turn * GROUP + k)
        return carry

    lax.fori_loop(0, nodes // GROUP, body, 0)


def shards(sections, valid_mask, coarse_offsets):
    count = lax.axis_size("tile")
    rows = count // SECTIONS
    nodes = valid_mask.shape[1]
    cols = nodes // 2
    width = cols * PATCH
    place = lambda group, row: (group * rows + row + rows // 2) % count

    def moved(value, pairs):
        return lax.ppermute(
            value, "tile", [(place(s, i), place(d, i)) for s, d in pairs for i in range(rows)]
        )

    left, right = sections[:, :width], sections[:, width:]
    below = moved(right, [(s, s + 1) for s in range(SECTIONS - 1)])
    above = moved(left, [(s + 1, s) for s in range(SECTIONS - 1)])

    vmem = pl.BlockSpec(memory_space=pltpu.VMEM)
    smem = pl.BlockSpec(memory_space=pltpu.SMEM)
    params = pltpu.CompilerParams(vmem_limit_bytes=16 * 2**20)
    gathered = []
    for step in range(1, SECTIONS):
        extra = gathered[-1:]
        sent = pl.pallas_call(
            functools.partial(chain_kernel, step, rows, nodes),
            out_shape=jax.ShapeDtypeStruct((count, LANES), f32),
            in_specs=[smem] + [vmem] * (4 + len(extra)),
            out_specs=vmem,
            scratch_shapes=[
                pltpu.VMEM((cols, 16, LANES), f32),
                pltpu.VMEM((2 * cols, LANES), f32),
                pltpu.VMEM((2 * cols, LANES), f32),
            ],
            compiler_params=params,
            name=f"chain{step}",
        )(coarse_offsets, sections, below, above, valid_mask, *extra)
        gathered.append(lax.all_to_all(sent, "tile", 0, 0, tiled=True))
    return pl.pallas_call(
        functools.partial(home_kernel, rows, nodes),
        out_shape=(
            jax.ShapeDtypeStruct(sections.shape, bf16),
            jax.ShapeDtypeStruct((2, 1, nodes), f32),
        ),
        in_specs=[vmem] * SECTIONS,
        out_specs=(vmem, vmem),
        scratch_shapes=[pltpu.VMEM((2 * nodes, LANES), f32)] * 2,
        compiler_params=params,
        name="home",
    )(sections, *gathered)


def solution(mesh):
    placed = (P(("parts", "tile"), None), P(("parts", "tile"), None), P("parts", None))
    return jax.shard_map(
        shards,
        mesh=mesh,
        in_specs=placed,
        out_specs=(P(("parts", "tile"), None), P(None, ("parts", "tile"), None)),
        check_vma=False,
    )
```

```python
import functools
import math

import jax
import jax.numpy as jnp
from jax import lax
from jax.experimental import pallas as pl
from jax.experimental.pallas import tpu as pltpu
from jax.sharding import PartitionSpec as P

SECTIONS = 4
PATCH = 128
HALF = 4
SWEEPS = 3
LANES = 128
WIDTH = 2 * HALF + 1
MASK_LANE = 64
GROUP = 4

sharpness = 12.0
anchor_weight = 2.0
f32 = jnp.float32
bf16 = jnp.bfloat16


def iota(shape, axis):
    return lax.broadcasted_iota(jnp.int32, shape, axis)


def split(value):
    high = value.astype(bf16)
    return high, (value - high.astype(f32)).astype(bf16)


def dot(lhs, rhs):
    return jnp.dot(lhs, rhs, preferred_element_type=f32)


def dot_t(lhs, rhs):
    return lax.dot_general(lhs, rhs, (((1,), (1,)), ((), ())), preferred_element_type=f32)


def sine(x):
    y = x * x
    acc = jnp.full_like(x, 1.0 / math.factorial(13))
    for order in (11, 9, 7, 5, 3, 1):
        acc = (-1.0 if order % 4 == 3 else 1.0) / math.factorial(order) + y * acc
    return x * acc


def cosine(x):
    y = x * x
    acc = jnp.full_like(x, 1.0 / math.factorial(12))
    for order in (10, 8, 6, 4, 2, 0):
        acc = (-1.0 if order % 4 == 2 else 1.0) / math.factorial(order) + y * acc
    return acc


def total(value):
    return jnp.sum(jnp.sum(value, axis=0, keepdims=True), axis=1, keepdims=True)


def tile_sum(value):
    parts = [value[r : r + 8] for r in range(0, value.shape[0], 8)]
    while len(parts) > 1:
        parts = [x + y for x, y in zip(parts[::2], parts[1::2])]
    return parts[0]


def sign_tile(shape):
    return (1 - 2 * ((iota(shape, 0) + iota(shape, 1)) % 2)).astype(f32)


def section_grid(gathered, step, rows):
    out = gathered[(step - 1) * rows : step * rows] + gathered[step * rows : (step + 1) * rows]
    return jnp.concatenate([out, jnp.zeros((8 - rows % 8, LANES), f32)], axis=0)


def relax(grid, rows, nodes):
    shape = grid.shape
    row, lane = iota(shape, 0), iota(shape, 1)
    col = lane % nodes
    valid = (row < rows) & (lane < 2 * nodes)
    mask = pltpu.roll(grid, LANES - MASK_LANE, 1)
    one = lambda cond: jnp.where(cond, 1.0, 0.0)
    count = one(row > 0) + one(row < rows - 1) + one(col > 0) + one(col < nodes - 1)
    weight = anchor_weight * mask
    inverse = 1.0 / jnp.where(valid, weight + count, 1.0)
    pulled = weight * grid
    shift = jnp.where(valid, grid * mask, 0.0)
    for _ in range(SWEEPS):
        near = pltpu.roll(shift, 1, 0) + pltpu.roll(shift, shape[0] - 1, 0)
        near += jnp.where(col > 0, pltpu.roll(shift, 1, 1), 0.0)
        near += jnp.where(col < nodes - 1, pltpu.roll(shift, LANES - 1, 1), 0.0)
        shift = jnp.where(valid, (pulled + near) * inverse, 0.0)
    return shift


def own_row(shift, index):
    return jnp.sum(jnp.where(iota(shift.shape, 0) == index, shift, 0.0), axis=0, keepdims=True)


def kernels_of(row_shift, first, cols, nodes):
    shape = (2 * cols, LANES)
    sub, lane = iota(shape, 0), iota(shape, 1)
    is_row = sub < cols
    target = first + jnp.where(is_row, sub, sub - cols + nodes)
    shift = jnp.sum(jnp.where(lane == target, row_shift, 0.0), axis=1, keepdims=True)
    shift = jnp.broadcast_to(shift, shape)
    whole = jnp.floor(shift + 0.5)
    part = shift - whole
    steps = jnp.where(is_row, -lane, lane).astype(f32) + whole
    steps = steps - LANES * jnp.floor((steps + LANES // 2) * (1.0 / LANES))
    sign = lambda n: 1.0 - 2.0 * (n - 2.0 * jnp.floor(n * 0.5))
    swing = sine(part * math.pi)
    angle = (steps + part) * (math.pi / LANES)
    centre = (steps == 0.0) & (jnp.abs(part) < 1e-20)
    below = jnp.where(centre, 1.0, sine(angle))
    base = swing * sign(steps) * (1.0 / LANES) * cosine(angle) / below
    return jnp.where(centre, 1.0, base), swing * sign(whole)


def circulant(row):
    return pltpu.roll(jnp.broadcast_to(row, (PATCH, LANES)), 0, 1, stride=1, stride_axis=0)


def warp(patch, row_base, col_base, row_swing, col_swing, nyquist):
    row_high, row_low = split(circulant(row_base))
    col_high, col_low = split(circulant(col_base))
    inner = dot(
        jnp.concatenate([patch, patch], axis=1), jnp.concatenate([col_high, col_low], axis=0)
    )
    in_high, in_low = split(inner)
    out = dot(
        jnp.concatenate([row_high, row_low], axis=1), jnp.concatenate([in_high, in_high], axis=0)
    ) + dot(row_high, in_low)
    factor = row_swing * col_swing * nyquist * (1.0 / (PATCH * PATCH))
    return out - factor * sign_tile((PATCH, LANES))


def correlate(own, prev, base, column_offset):
    half, edge, third = PATCH // 2, 16, 3
    own32, prev32 = own.astype(f32), prev.astype(f32)
    left = []
    for i in range(third):
        amount = (PATCH + HALF - i - column_offset) % PATCH
        turned = pltpu.roll(own32, amount, 1).astype(bf16)
        left.append(jnp.concatenate([turned[:half], turned[half:]], axis=1))
    right = []
    for j in range(third):
        turned = (pltpu.roll(prev32, third * j, 1) if j else prev32).astype(bf16)
        low = jnp.concatenate([turned[PATCH - edge :], turned[: PATCH - edge]], axis=0)
        high = jnp.concatenate([turned[half - edge :], turned[: half - edge]], axis=0)
        right.append(jnp.concatenate([low, high], axis=1))
    product = dot_t(jnp.concatenate(left, axis=0), jnp.concatenate(right, axis=0))
    lane = iota((8, LANES), 1)
    sub = iota((16, LANES), 0)
    out = jnp.zeros((16, LANES), f32)
    for j in range(third):
        for i in range(third):
            block = product[i * half : (i + 1) * half, j * LANES : (j + 1) * LANES]
            band = None
            for k in range(4):
                later = (lane >= 8 * k + 32) & (lane < 8 * k + 64)
                kept = jnp.where(later, block[8 * k + 32 : 8 * k + 40], block[8 * k : 8 * k + 8])
                kept = pltpu.roll(kept, LANES - 8 * k, 1) if k else kept
                band = kept if band is None else band + kept
            band = band - base
            for step in (4, 2, 1):
                band = band + pltpu.roll(pltpu.roll(band, 8 - step, 0), LANES - step, 1)
            line = band[0:1]
            line = line + pltpu.roll(line, LANES - 32, 1)
            out = jnp.where(sub == i + third * j, line, out)
    return out


def stats(tile):
    return total(tile) * (1.0 / (PATCH * PATCH))


def chain_kernel(
    step, rows, nodes, offsets_ref, own_ref, other_ref, mask_ref, *refs
):
    gathered_ref = refs[0] if step > 1 else None
    out_ref, score_ref, base_ref, swing_ref = refs[-4:]
    cols = nodes // 2
    count = lax.axis_size("tile")
    rotated = (lax.axis_index("tile") + count - rows // 2) % count
    group, row_index = rotated // rows, rotated % rows
    is_upper = group == step
    first = jnp.where(is_upper, cols, 0)
    if step > 1:
        shift = relax(section_grid(gathered_ref[...], step - 1, rows), rows, nodes)
        base, swing = kernels_of(own_row(shift, row_index), first, cols, nodes)
        base_ref[...] = base
        swing_ref[...] = swing
    row_offset, col_offset = offsets_ref[step, 0], offsets_ref[step, 1]
    area = float(PATCH * PATCH)

    def one(index):
        here = pl.ds(pl.multiple_of(index * PATCH, PATCH), PATCH)
        beyond = pl.ds(pl.multiple_of((index + cols) * PATCH, PATCH), PATCH)
        other = other_ref[:, here]
        own = jnp.where(is_upper, own_ref[:, beyond], other)
        prev = jnp.where(is_upper, other, own_ref[:, here])
        own32, prev32 = own.astype(f32), prev.astype(f32)
        own_mean = stats(tile_sum(own32))
        own_var = stats(tile_sum((own32 - own_mean) * (own32 - own_mean)))
        prev_tile = tile_sum(prev32)
        prev_mean = stats(prev_tile)
        if step > 1:
            nyquist = total(prev_tile * sign_tile((8, LANES)))
            prev = warp(
                prev,
                base_ref[pl.ds(index, 1), :],
                base_ref[pl.ds(index + cols, 1), :],
                swing_ref[pl.ds(index, 1), :],
                swing_ref[pl.ds(index + cols, 1), :],
                nyquist,
            ).astype(bf16)
            prev32 = prev.astype(f32)
        centre = prev32 - prev_mean
        drift = stats(tile_sum(centre))
        prev_var = stats(tile_sum(centre * centre)) - drift * drift
        spread = jnp.sqrt((own_var + 1e-5) * (prev_var + 1e-5))
        lags = correlate(own, prev, (own_mean * (prev_mean + drift)) * (8.0 * LANES), col_offset)
        score_ref[pl.ds(index, 1)] = (lags * (sharpness / area / spread))[None]

    def body(turn, carry):
        for k in range(GROUP):
            one(turn * GROUP + k)
        return carry

    lax.fori_loop(0, cols // GROUP, body, 0)
    shape = (cols, 16, LANES)
    line, lane = iota(shape, 1), iota(shape, 2)
    row_step = 16 - lane - row_offset
    inside = (line < WIDTH) & (row_step >= -HALF) & (row_step <= HALF)
    weights = jnp.where(inside, jnp.exp(jnp.where(inside, score_ref[...], 0.0)), 0.0)
    reduce = lambda value: jnp.sum(jnp.sum(value, axis=1), axis=1, keepdims=True)
    inverse = 1.0 / reduce(weights)
    flow_row = reduce(weights * (row_step + row_offset).astype(f32)) * inverse
    flow_col = reduce(weights * (line - HALF + col_offset).astype(f32)) * inverse
    shape = (cols, LANES)
    node, lane = iota(shape, 0) + first, iota(shape, 1)
    sent = jnp.where(lane == node, flow_row, jnp.where(lane == node + nodes, flow_col, 0.0))
    sent = jnp.sum(sent, axis=0, keepdims=True)
    masks = mask_ref[...].astype(f32)
    masks = jnp.concatenate(
        [jnp.zeros((1, MASK_LANE), f32), masks, masks, jnp.zeros((1, LANES - MASK_LANE - 2 * nodes), f32)],
        axis=1,
    )
    sent = sent + jnp.where(is_upper, masks, 0.0)
    out_ref[...] = jnp.broadcast_to(sent, out_ref.shape)


def home_kernel(rows, nodes, own_ref, *refs):
    gathered_refs = refs[: SECTIONS - 1]
    out_ref, shift_ref, base_ref, swing_ref = refs[SECTIONS - 1 :]
    count = lax.axis_size("tile")
    rotated = (lax.axis_index("tile") + count - rows // 2) % count
    group, row_index = rotated // rows, rotated % rows
    grid = None
    for step in range(1, SECTIONS):
        part = section_grid(gathered_refs[step - 1][...], step, rows)
        grid = part if grid is None else jnp.where(group == step, part, grid)
    row_shift = own_row(relax(grid, rows, nodes), row_index)
    row_shift = jnp.where(group == 0, 0.0, row_shift)
    shift_ref[0, :, :] = row_shift[:, :nodes]
    shift_ref[1, :, :] = pltpu.roll(row_shift, LANES - nodes, 1)[:, :nodes]
    base, swing = kernels_of(row_shift, 0, nodes, nodes)
    base_ref[...] = base
    swing_ref[...] = swing

    def one(index):
        here = pl.ds(pl.multiple_of(index * PATCH, PATCH), PATCH)
        own = own_ref[:, here]
        nyquist = total(tile_sum(own.astype(f32)) * sign_tile((8, LANES)))
        out_ref[:, here] = warp(
            own,
            base_ref[pl.ds(index, 1), :],
            base_ref[pl.ds(index + nodes, 1), :],
            swing_ref[pl.ds(index, 1), :],
            swing_ref[pl.ds(index + nodes, 1), :],
            nyquist,
        ).astype(bf16)

    def body(turn, carry):
        for k in range(GROUP):
            one(turn * GROUP + k)
        return carry

    lax.fori_loop(0, nodes // GROUP, body, 0)


def shards(sections, valid_mask, coarse_offsets):
    count = lax.axis_size("tile")
    rows = count // SECTIONS
    nodes = valid_mask.shape[1]
    cols = nodes // 2
    width = cols * PATCH
    place = lambda group, row: (group * rows + row + rows // 2) % count
    group = (lax.axis_index("tile") + count - rows // 2) % count // rows
    row_groups = [[place(s, i) for i in range(rows)] for s in range(SECTIONS)]
    section_groups = [[place(s, i) for s in range(SECTIONS)] for i in range(rows)]

    def swapped(lower, after=None):
        half = lax.dynamic_slice_in_dim(sections, jnp.where(group == lower, width, 0), width, 1)
        if after is not None:
            half, after = lax.optimization_barrier((half, after))
        ends = [(place(lower, i), place(lower + 1, i)) for i in range(rows)]
        return lax.ppermute(half, "tile", ends + [(d, s) for s, d in ends])

    def exchanged(sent):
        near = lax.all_to_all(sent, "tile", 0, 0, axis_index_groups=row_groups, tiled=True)
        near = jnp.broadcast_to(near[None], (SECTIONS,) + near.shape)
        return lax.all_to_all(
            near, "tile", 0, 0, axis_index_groups=section_groups, tiled=True
        ).reshape(count, LANES)

    others = [swapped(0), swapped(1)]
    others += [swapped(s, others[0]) for s in range(2, SECTIONS - 1)]

    vmem = pl.BlockSpec(memory_space=pltpu.VMEM)
    smem = pl.BlockSpec(memory_space=pltpu.SMEM)
    params = pltpu.CompilerParams(vmem_limit_bytes=16 * 2**20)
    gathered = []
    for step in range(1, SECTIONS):
        extra = gathered[-1:]
        sent = pl.pallas_call(
            functools.partial(chain_kernel, step, rows, nodes),
            out_shape=jax.ShapeDtypeStruct((rows, LANES), f32),
            in_specs=[smem] + [vmem] * (3 + len(extra)),
            out_specs=vmem,
            scratch_shapes=[
                pltpu.VMEM((cols, 16, LANES), f32),
                pltpu.VMEM((2 * cols, LANES), f32),
                pltpu.VMEM((2 * cols, LANES), f32),
            ],
            compiler_params=params,
            name=f"chain{step}",
        )(coarse_offsets, sections, others[step - 1], valid_mask, *extra)
        gathered.append(exchanged(sent))
    return pl.pallas_call(
        functools.partial(home_kernel, rows, nodes),
        out_shape=(
            jax.ShapeDtypeStruct(sections.shape, bf16),
            jax.ShapeDtypeStruct((2, 1, nodes), f32),
        ),
        in_specs=[vmem] * SECTIONS,
        out_specs=(vmem, vmem),
        scratch_shapes=[pltpu.VMEM((2 * nodes, LANES), f32)] * 2,
        compiler_params=params,
        name="home",
    )(sections, *gathered)


def solution(mesh):
    placed = (P(("parts", "tile"), None), P(("parts", "tile"), None), P("parts", None))
    return jax.shard_map(
        shards,
        mesh=mesh,
        in_specs=placed,
        out_specs=(P(("parts", "tile"), None), P(None, ("parts", "tile"), None)),
        check_vma=False,
    )
```

```python
import functools
import math

import jax
import jax.numpy as jnp
from jax import lax
from jax.experimental import pallas as pl
from jax.experimental.pallas import tpu as pltpu
from jax.sharding import PartitionSpec as P

SECTIONS = 4
PATCH = 128
HALF = 4
SWEEPS = 3
LANES = 128
WIDTH = 2 * HALF + 1
MASK_LANE = 64
GROUP = 4

sharpness = 12.0
anchor_weight = 2.0
f32 = jnp.float32
bf16 = jnp.bfloat16


def iota(shape, axis):
    return lax.broadcasted_iota(jnp.int32, shape, axis)


def split(value):
    high = value.astype(bf16)
    return high, (value - high.astype(f32)).astype(bf16)


def dot(lhs, rhs):
    return jnp.dot(lhs, rhs, preferred_element_type=f32)


def dot_t(lhs, rhs):
    return lax.dot_general(lhs, rhs, (((1,), (1,)), ((), ())), preferred_element_type=f32)


def sine(x):
    y = x * x
    acc = jnp.full_like(x, 1.0 / math.factorial(13))
    for order in (11, 9, 7, 5, 3, 1):
        acc = (-1.0 if order % 4 == 3 else 1.0) / math.factorial(order) + y * acc
    return x * acc


def cosine(x):
    y = x * x
    acc = jnp.full_like(x, 1.0 / math.factorial(12))
    for order in (10, 8, 6, 4, 2, 0):
        acc = (-1.0 if order % 4 == 2 else 1.0) / math.factorial(order) + y * acc
    return acc


def total(value):
    return jnp.sum(jnp.sum(value, axis=0, keepdims=True), axis=1, keepdims=True)


def tile_sum(value):
    parts = [value[r : r + 8] for r in range(0, value.shape[0], 8)]
    while len(parts) > 1:
        parts = [x + y for x, y in zip(parts[::2], parts[1::2])]
    return parts[0]


def sign_tile(shape):
    return (1 - 2 * ((iota(shape, 0) + iota(shape, 1)) % 2)).astype(f32)


def padded_rows(grid):
    return jnp.concatenate([grid, jnp.zeros((8 - grid.shape[0] % 8, LANES), f32)], axis=0)


def relax(grid, rows, nodes):
    grid = padded_rows(grid)
    shape = grid.shape
    row, lane = iota(shape, 0), iota(shape, 1)
    col = lane % nodes
    valid = (row < rows) & (lane < 2 * nodes)
    mask = pltpu.roll(grid, LANES - MASK_LANE, 1)
    one = lambda cond: jnp.where(cond, 1.0, 0.0)
    count = one(row > 0) + one(row < rows - 1) + one(col > 0) + one(col < nodes - 1)
    weight = anchor_weight * mask
    inverse = 1.0 / jnp.where(valid, weight + count, 1.0)
    pulled = weight * grid
    shift = jnp.where(valid, grid * mask, 0.0)
    for _ in range(SWEEPS):
        near = pltpu.roll(shift, 1, 0) + pltpu.roll(shift, shape[0] - 1, 0)
        near += jnp.where(col > 0, pltpu.roll(shift, 1, 1), 0.0)
        near += jnp.where(col < nodes - 1, pltpu.roll(shift, LANES - 1, 1), 0.0)
        shift = jnp.where(valid, (pulled + near) * inverse, 0.0)
    return shift


def own_row(shift, index):
    return jnp.sum(jnp.where(iota(shift.shape, 0) == index, shift, 0.0), axis=0, keepdims=True)


def kernels_of(row_shift, first, cols, nodes):
    shape = (2 * cols, LANES)
    sub, lane = iota(shape, 0), iota(shape, 1)
    is_row = sub < cols
    target = first + jnp.where(is_row, sub, sub - cols + nodes)
    shift = jnp.sum(jnp.where(lane == target, row_shift, 0.0), axis=1, keepdims=True)
    shift = jnp.broadcast_to(shift, shape)
    whole = jnp.floor(shift + 0.5)
    part = shift - whole
    steps = jnp.where(is_row, -lane, lane).astype(f32) + whole
    steps = steps - LANES * jnp.floor((steps + LANES // 2) * (1.0 / LANES))
    sign = lambda n: 1.0 - 2.0 * (n - 2.0 * jnp.floor(n * 0.5))
    swing = sine(part * math.pi)
    angle = (steps + part) * (math.pi / LANES)
    centre = (steps == 0.0) & (jnp.abs(part) < 1e-20)
    below = jnp.where(centre, 1.0, sine(angle))
    base = swing * sign(steps) * (1.0 / LANES) * cosine(angle) / below
    return jnp.where(centre, 1.0, base), swing * sign(whole)


def circulant(row):
    return pltpu.roll(jnp.broadcast_to(row, (PATCH, LANES)), 0, 1, stride=1, stride_axis=0)


def warp(patch, row_base, col_base, row_swing, col_swing, nyquist):
    row_high, row_low = split(circulant(row_base))
    col_high, col_low = split(circulant(col_base))
    inner = dot(
        jnp.concatenate([patch, patch], axis=1), jnp.concatenate([col_high, col_low], axis=0)
    )
    in_high, in_low = split(inner)
    out = dot(
        jnp.concatenate([row_high, row_low], axis=1), jnp.concatenate([in_high, in_high], axis=0)
    ) + dot(row_high, in_low)
    factor = row_swing * col_swing * nyquist * (1.0 / (PATCH * PATCH))
    return out - factor * sign_tile((PATCH, LANES))


def correlate(own, prev, base, column_offset):
    half, edge, third = PATCH // 2, 16, 3
    own32, prev32 = own.astype(f32), prev.astype(f32)
    left = []
    for i in range(third):
        amount = (PATCH + HALF - i - column_offset) % PATCH
        turned = pltpu.roll(own32, amount, 1).astype(bf16)
        left.append(jnp.concatenate([turned[:half], turned[half:]], axis=1))
    right = []
    for j in range(third):
        turned = (pltpu.roll(prev32, third * j, 1) if j else prev32).astype(bf16)
        low = jnp.concatenate([turned[PATCH - edge :], turned[: PATCH - edge]], axis=0)
        high = jnp.concatenate([turned[half - edge :], turned[: half - edge]], axis=0)
        right.append(jnp.concatenate([low, high], axis=1))
    product = dot_t(jnp.concatenate(left, axis=0), jnp.concatenate(right, axis=0))
    lane = iota((8, LANES), 1)
    sub = iota((16, LANES), 0)
    out = jnp.zeros((16, LANES), f32)
    for j in range(third):
        for i in range(third):
            block = product[i * half : (i + 1) * half, j * LANES : (j + 1) * LANES]
            band = None
            for k in range(4):
                later = (lane >= 8 * k + 32) & (lane < 8 * k + 64)
                kept = jnp.where(later, block[8 * k + 32 : 8 * k + 40], block[8 * k : 8 * k + 8])
                kept = pltpu.roll(kept, LANES - 8 * k, 1) if k else kept
                band = kept if band is None else band + kept
            band = band - base
            for step in (4, 2, 1):
                band = band + pltpu.roll(pltpu.roll(band, 8 - step, 0), LANES - step, 1)
            line = band[0:1]
            line = line + pltpu.roll(line, LANES - 32, 1)
            out = jnp.where(sub == i + third * j, line, out)
    return out


def stats(tile):
    return total(tile) * (1.0 / (PATCH * PATCH))


def looped(count, one):
    def body(turn, carry):
        for k in range(GROUP):
            one(turn * GROUP + k)
        return carry

    lax.fori_loop(0, count // GROUP, body, 0)


def columns(index):
    return pl.ds(pl.multiple_of(index * PATCH, PATCH), PATCH)


def warp_indexed(patch, base_ref, swing_ref, index, cols):
    nyquist = total(tile_sum(patch.astype(f32)) * sign_tile((8, LANES)))
    return warp(
        patch,
        base_ref[pl.ds(index, 1), :],
        base_ref[pl.ds(index + cols, 1), :],
        swing_ref[pl.ds(index, 1), :],
        swing_ref[pl.ds(index + cols, 1), :],
        nyquist,
    ).astype(bf16)


def chain_kernel(step, rows, nodes, offsets_ref, own_ref, other_ref, mask_ref, *refs):
    out_ref, score_ref, prev_ref, base_ref, swing_ref = refs[-5:]
    cols = nodes // 2
    count = lax.axis_size("tile")
    rotated = (lax.axis_index("tile") + count - rows // 2) % count
    group, row_index = rotated // rows, rotated % rows
    is_upper = group == step
    first = jnp.where(is_upper, cols, 0)
    row_offset, col_offset = offsets_ref[step, 0], offsets_ref[step, 1]
    area = float(PATCH * PATCH)

    if step > 1:
        near_ref, next_ref, beyond_ref = refs[:3]
        grid = next_ref[...] + jnp.where(is_upper, beyond_ref[...], near_ref[...])
        row_shift = own_row(relax(grid, rows, nodes), row_index)
        base_ref[...], swing_ref[...] = kernels_of(row_shift, first, cols, nodes)

        def warp_one(index):
            patch = jnp.where(is_upper, other_ref[:, columns(index)], own_ref[:, columns(index)])
            prev_ref[index] = warp_indexed(patch, base_ref, swing_ref, index, cols)

        looped(cols, warp_one)

    def one(index):
        other = other_ref[:, columns(index)]
        own = jnp.where(is_upper, own_ref[:, columns(index + cols)], other)
        prev = prev_ref[index] if step > 1 else jnp.where(is_upper, other, own_ref[:, columns(index)])
        own32, prev32 = own.astype(f32), prev.astype(f32)
        own_mean, prev_mean = stats(tile_sum(own32)), stats(tile_sum(prev32))
        own_var = stats(tile_sum((own32 - own_mean) * (own32 - own_mean)))
        prev_var = stats(tile_sum((prev32 - prev_mean) * (prev32 - prev_mean)))
        spread = jnp.sqrt((own_var + 1e-5) * (prev_var + 1e-5))
        lags = correlate(own, prev, (own_mean * prev_mean) * (8.0 * LANES), col_offset)
        score_ref[pl.ds(index, 1)] = (lags * (sharpness / area / spread))[None]

    looped(cols, one)
    shape = (cols, 16, LANES)
    line, lane = iota(shape, 1), iota(shape, 2)
    row_step = 16 - lane - row_offset
    inside = (line < WIDTH) & (row_step >= -HALF) & (row_step <= HALF)
    weights = jnp.where(inside, jnp.exp(jnp.where(inside, score_ref[...], 0.0)), 0.0)
    reduce = lambda value: jnp.sum(jnp.sum(value, axis=1), axis=1, keepdims=True)
    inverse = 1.0 / reduce(weights)
    flow_row = reduce(weights * (row_step + row_offset).astype(f32)) * inverse
    flow_col = reduce(weights * (line - HALF + col_offset).astype(f32)) * inverse
    shape = (cols, LANES)
    node, lane = iota(shape, 0) + first, iota(shape, 1)
    sent = jnp.where(lane == node, flow_row, jnp.where(lane == node + nodes, flow_col, 0.0))
    sent = jnp.sum(sent, axis=0, keepdims=True)
    masks = mask_ref[...].astype(f32)
    masks = jnp.concatenate(
        [jnp.zeros((1, MASK_LANE), f32), masks, masks, jnp.zeros((1, LANES - MASK_LANE - 2 * nodes), f32)],
        axis=1,
    )
    sent = sent + jnp.where(is_upper, masks, 0.0)
    out_ref[...] = jnp.where(iota(out_ref.shape, 0) == row_index, sent, 0.0)


def home_kernel(rows, nodes, own_ref, *refs):
    out_ref, shift_ref, base_ref, swing_ref = refs[-4:]
    count = lax.axis_size("tile")
    rotated = (lax.axis_index("tile") + count - rows // 2) % count
    group, row_index = rotated // rows, rotated % rows
    grid = None
    for step in range(1, SECTIONS):
        near_ref, next_ref = refs[2 * step - 2 : 2 * step]
        part = near_ref[...] + next_ref[...]
        grid = part if grid is None else jnp.where(group == step, part, grid)
    row_shift = own_row(relax(grid, rows, nodes), row_index)
    row_shift = jnp.where(group == 0, 0.0, row_shift)
    shift_ref[0, :, :] = row_shift[:, :nodes]
    shift_ref[1, :, :] = pltpu.roll(row_shift, LANES - nodes, 1)[:, :nodes]
    base_ref[...], swing_ref[...] = kernels_of(row_shift, 0, nodes, nodes)

    def one(index):
        here = columns(index)
        out_ref[:, here] = warp_indexed(own_ref[:, here], base_ref, swing_ref, index, nodes)

    looped(nodes, one)


def shards(sections, valid_mask, coarse_offsets):
    count = lax.axis_size("tile")
    rows = count // SECTIONS
    nodes = valid_mask.shape[1]
    cols = nodes // 2
    width = cols * PATCH
    place = lambda group, row: (group * rows + row + rows // 2) % count
    group = (lax.axis_index("tile") + count - rows // 2) % count // rows
    moved = lambda value, pairs: lax.ppermute(value, "tile", pairs)

    def swapped(lower, after=None):
        half = lax.dynamic_slice_in_dim(sections, jnp.where(group == lower, width, 0), width, 1)
        if after is not None:
            half, after = lax.optimization_barrier((half, after))
        ends = [(place(lower, i), place(lower + 1, i)) for i in range(rows)]
        return moved(half, ends + [(d, s) for s, d in ends])

    def exchanged(sent, step):
        around = [
            moved(
                sent,
                [
                    (place(s, i), place(s, (i + k) % rows))
                    for s in range(SECTIONS)
                    for i in range(rows)
                ],
            )
            for k in range(1, rows)
        ]
        near = functools.reduce(jnp.add, around, sent)
        onward = lambda source, ahead: [
            (place(source, i), place(source + ahead, i))
            for i in range(rows)
            if source + ahead < SECTIONS
        ]
        ahead = moved(near, onward(step - 1, 1) + onward(step, 1))
        if step + 1 == SECTIONS:
            return near, ahead
        return near, ahead, moved(near, onward(step - 1, 2))

    others = [swapped(0), swapped(1)]

    vmem = pl.BlockSpec(memory_space=pltpu.VMEM)
    smem = pl.BlockSpec(memory_space=pltpu.SMEM)
    params = pltpu.CompilerParams(vmem_limit_bytes=16 * 2**20)
    gathered = []
    for step in range(1, SECTIONS):
        extra = gathered[-1] if gathered else ()
        sent = pl.pallas_call(
            functools.partial(chain_kernel, step, rows, nodes),
            out_shape=jax.ShapeDtypeStruct((rows, LANES), f32),
            in_specs=[smem] + [vmem] * (3 + len(extra)),
            out_specs=vmem,
            scratch_shapes=[
                pltpu.VMEM((cols, 16, LANES), f32),
                pltpu.VMEM((cols, PATCH, PATCH), bf16),
                pltpu.VMEM((2 * cols, LANES), f32),
                pltpu.VMEM((2 * cols, LANES), f32),
            ],
            compiler_params=params,
            name=f"chain{step}",
        )(coarse_offsets, sections, others[step - 1], valid_mask, *extra)
        gathered.append(exchanged(sent, step))
        if step + 1 < SECTIONS - 1:
            others.append(swapped(step + 1, gathered[-1][0]))
    return pl.pallas_call(
        functools.partial(home_kernel, rows, nodes),
        out_shape=(
            jax.ShapeDtypeStruct(sections.shape, bf16),
            jax.ShapeDtypeStruct((2, 1, nodes), f32),
        ),
        in_specs=[vmem] * (2 * SECTIONS - 1),
        out_specs=(vmem, vmem),
        scratch_shapes=[pltpu.VMEM((2 * nodes, LANES), f32)] * 2,
        compiler_params=params,
        name="home",
    )(sections, *[rows_of for parts in gathered for rows_of in parts[:2]])


def solution(mesh):
    placed = (P(("parts", "tile"), None), P(("parts", "tile"), None), P("parts", None))
    return jax.shard_map(
        shards,
        mesh=mesh,
        in_specs=placed,
        out_specs=(P(("parts", "tile"), None), P(None, ("parts", "tile"), None)),
        check_vma=False,
    )
```

```python
import functools
import math

import jax
import jax.numpy as jnp
from jax import lax
from jax.experimental import pallas as pl
from jax.experimental.pallas import tpu as pltpu
from jax.sharding import PartitionSpec as P

SECTIONS = 4
PATCH = 128
HALF = 4
SWEEPS = 3
LANES = 128
WIDTH = 2 * HALF + 1
MASK_LANE = 64
GROUP = 4

sharpness = 12.0
anchor_weight = 2.0
f32 = jnp.float32
bf16 = jnp.bfloat16


def iota(shape, axis):
    return lax.broadcasted_iota(jnp.int32, shape, axis)


def split(value):
    high = value.astype(bf16)
    return high, (value - high.astype(f32)).astype(bf16)


def dot(lhs, rhs):
    return jnp.dot(lhs, rhs, preferred_element_type=f32)


def dot_t(lhs, rhs):
    return lax.dot_general(lhs, rhs, (((1,), (1,)), ((), ())), preferred_element_type=f32)


def sine(x):
    y = x * x
    acc = jnp.full_like(x, 1.0 / math.factorial(13))
    for order in (11, 9, 7, 5, 3, 1):
        acc = (-1.0 if order % 4 == 3 else 1.0) / math.factorial(order) + y * acc
    return x * acc


def cosine(x):
    y = x * x
    acc = jnp.full_like(x, 1.0 / math.factorial(12))
    for order in (10, 8, 6, 4, 2, 0):
        acc = (-1.0 if order % 4 == 2 else 1.0) / math.factorial(order) + y * acc
    return acc


def total(value):
    return jnp.sum(jnp.sum(value, axis=0, keepdims=True), axis=1, keepdims=True)


def tile_sum(value):
    parts = [value[r : r + 8] for r in range(0, value.shape[0], 8)]
    while len(parts) > 1:
        parts = [x + y for x, y in zip(parts[::2], parts[1::2])]
    return parts[0]


def sign_tile(shape):
    return (1 - 2 * ((iota(shape, 0) + iota(shape, 1)) % 2)).astype(f32)


def padded_rows(grid):
    return jnp.concatenate([grid, jnp.zeros((8 - grid.shape[0] % 8, LANES), f32)], axis=0)


def relax(grid, rows, nodes):
    grid = padded_rows(grid)
    shape = grid.shape
    row, lane = iota(shape, 0), iota(shape, 1)
    col = lane % nodes
    valid = (row < rows) & (lane < 2 * nodes)
    mask = pltpu.roll(grid, LANES - MASK_LANE, 1)
    one = lambda cond: jnp.where(cond, 1.0, 0.0)
    count = one(row > 0) + one(row < rows - 1) + one(col > 0) + one(col < nodes - 1)
    weight = anchor_weight * mask
    inverse = 1.0 / jnp.where(valid, weight + count, 1.0)
    pulled = weight * grid
    shift = jnp.where(valid, grid * mask, 0.0)
    for _ in range(SWEEPS):
        near = pltpu.roll(shift, 1, 0) + pltpu.roll(shift, shape[0] - 1, 0)
        near += jnp.where(col > 0, pltpu.roll(shift, 1, 1), 0.0)
        near += jnp.where(col < nodes - 1, pltpu.roll(shift, LANES - 1, 1), 0.0)
        shift = jnp.where(valid, (pulled + near) * inverse, 0.0)
    return shift


def own_row(shift, index):
    return jnp.sum(jnp.where(iota(shift.shape, 0) == index, shift, 0.0), axis=0, keepdims=True)


def kernels_of(row_shift, first, cols, nodes):
    shape = (2 * cols, LANES)
    sub, lane = iota(shape, 0), iota(shape, 1)
    is_row = sub < cols
    target = first + jnp.where(is_row, sub, sub - cols + nodes)
    shift = jnp.sum(jnp.where(lane == target, row_shift, 0.0), axis=1, keepdims=True)
    shift = jnp.broadcast_to(shift, shape)
    whole = jnp.floor(shift + 0.5)
    part = shift - whole
    steps = jnp.where(is_row, -lane, lane).astype(f32) + whole
    steps = steps - LANES * jnp.floor((steps + LANES // 2) * (1.0 / LANES))
    sign = lambda n: 1.0 - 2.0 * (n - 2.0 * jnp.floor(n * 0.5))
    swing = sine(part * math.pi)
    angle = (steps + part) * (math.pi / LANES)
    centre = (steps == 0.0) & (jnp.abs(part) < 1e-20)
    below = jnp.where(centre, 1.0, sine(angle))
    base = swing * sign(steps) * (1.0 / LANES) * cosine(angle) / below
    return jnp.where(centre, 1.0, base), swing * sign(whole)


def circulant(row):
    first = pltpu.roll(jnp.broadcast_to(row, (8, LANES)), 0, 1, stride=1, stride_axis=0)
    later = [pltpu.roll(first, r, 1) for r in range(8, PATCH, 8)]
    return jnp.concatenate([first] + later, axis=0)


def warp(patch, row_base, col_base, row_swing, col_swing, nyquist):
    row_high, row_low = split(circulant(row_base))
    col_high, col_low = split(circulant(col_base))
    inner = dot(
        jnp.concatenate([patch, patch], axis=1), jnp.concatenate([col_high, col_low], axis=0)
    )
    in_high, in_low = split(inner)
    out = dot(
        jnp.concatenate([row_high, row_low], axis=1), jnp.concatenate([in_high, in_high], axis=0)
    ) + dot(row_high, in_low)
    factor = row_swing * col_swing * nyquist * (1.0 / (PATCH * PATCH))
    return out - factor * sign_tile((PATCH, LANES))


def correlate(own, prev, base, column_offset, band_ref):
    half, edge, third = PATCH // 2, 16, 3
    own32, prev32 = own.astype(f32), prev.astype(f32)
    left = []
    for i in range(third):
        amount = (PATCH + HALF - i - column_offset) % PATCH
        turned = pltpu.roll(own32, amount, 1).astype(bf16)
        left.append(jnp.concatenate([turned[:half], turned[half:]], axis=1))
    right = []
    for j in range(third):
        turned = pltpu.roll(prev32, third * j, 1).astype(bf16) if j else prev
        low = jnp.concatenate([turned[PATCH - edge :], turned[: PATCH - edge]], axis=0)
        high = jnp.concatenate([turned[half - edge :], turned[: half - edge]], axis=0)
        right.append(jnp.concatenate([low, high], axis=1))
    product = dot_t(jnp.concatenate(left, axis=0), jnp.concatenate(right, axis=0))
    lane = iota((8, LANES), 1)
    for j in range(third):
        for i in range(third):
            block = product[i * half : (i + 1) * half, j * LANES : (j + 1) * LANES]
            band = None
            for k in range(4):
                later = (lane >= 8 * k + 32) & (lane < 8 * k + 64)
                kept = jnp.where(later, block[8 * k + 32 : 8 * k + 40], block[8 * k : 8 * k + 8])
                kept = pltpu.roll(kept, LANES - 8 * k, 1) if k else kept
                band = kept if band is None else band + kept
            band_ref[8 * (i + third * j) : 8 * (i + third * j) + 8, :] = band - base
    out = None
    for row in range(8):
        part = band_ref[pl.ds(row, WIDTH, stride=8), :]
        part = pltpu.roll(part, LANES - row, 1) if row else part
        out = part if out is None else out + part
    return out + pltpu.roll(out, LANES - 32, 1)


def moments(values, corner):
    values = values.astype(f32) - corner
    return tile_sum(values), tile_sum(values * values)


def looped(count, one):
    def body(turn, carry):
        for k in range(GROUP):
            one(turn * GROUP + k)
        return carry

    lax.fori_loop(0, count // GROUP, body, 0)


def columns(index):
    return pl.ds(pl.multiple_of(index * PATCH, PATCH), PATCH)


def warp_indexed(patch, base_ref, swing_ref, index, cols):
    nyquist = total(tile_sum(patch.astype(f32)) * sign_tile((8, LANES)))
    return warp(
        patch,
        base_ref[pl.ds(index, 1), :],
        base_ref[pl.ds(index + cols, 1), :],
        swing_ref[pl.ds(index, 1), :],
        swing_ref[pl.ds(index + cols, 1), :],
        nyquist,
    ).astype(bf16)


def chain_kernel(step, rows, nodes, offsets_ref, own_ref, other_ref, mask_ref, *refs):
    out_ref, score_ref, band_ref, sums_ref, corner_ref, prev_ref, base_ref, swing_ref = refs[-8:]
    cols = nodes // 2
    count = lax.axis_size("tile")
    rotated = (lax.axis_index("tile") + count - rows // 2) % count
    group, row_index = rotated // rows, rotated % rows
    is_upper = group == step
    first = jnp.where(is_upper, cols, 0)
    row_offset, col_offset = offsets_ref[step, 0], offsets_ref[step, 1]
    area = float(PATCH * PATCH)

    if step > 1:
        row_shift = own_row(relax(refs[0][...], rows, nodes), row_index)
        base_ref[...], swing_ref[...] = kernels_of(row_shift, first, cols, nodes)

        def warp_one(index):
            patch = jnp.where(is_upper, other_ref[:, columns(index)], own_ref[:, columns(index)])
            prev_ref[index] = warp_indexed(patch, base_ref, swing_ref, index, cols)

        looped(cols, warp_one)

    def one(index):
        other = other_ref[:, columns(index)]
        own = jnp.where(is_upper, own_ref[:, columns(index + cols)], other)
        prev = prev_ref[index] if step > 1 else jnp.where(is_upper, other, own_ref[:, columns(index)])
        own_corner, prev_corner = (x[0:1, 0:1].astype(f32) for x in (own, prev))
        corner_ref[0, pl.ds(index, 1), :] = jnp.broadcast_to(own_corner, (1, LANES))
        corner_ref[1, pl.ds(index, 1), :] = jnp.broadcast_to(prev_corner, (1, LANES))
        sums = moments(own, own_corner) + moments(prev, prev_corner)
        for k, value in enumerate(sums):
            sums_ref[k, pl.ds(index, 1)] = value[None]
        base = own_corner * prev_corner * (8.0 * LANES)
        score_ref[pl.ds(index, 1)] = correlate(own, prev, base, col_offset, band_ref.at[index])[None]

    looped(cols, one)
    reduce = lambda value: jnp.sum(jnp.sum(value, axis=1), axis=1, keepdims=True)
    own_sum, own_square, prev_sum, prev_square = (reduce(sums_ref[k]) * (1.0 / area) for k in range(4))
    spread = jnp.sqrt(
        (jnp.maximum(own_square - own_sum * own_sum, 0.0) + 1e-5)
        * (jnp.maximum(prev_square - prev_sum * prev_sum, 0.0) + 1e-5)
    )
    scale = sharpness / area / spread
    level = corner_ref[0] * prev_sum + corner_ref[1] * own_sum + own_sum * prev_sum
    shape = (cols, WIDTH, LANES)
    line, lane = iota(shape, 1), iota(shape, 2)
    row_step = 16 - lane - row_offset
    inside = (row_step >= -HALF) & (row_step <= HALF)
    score = (score_ref[...] - (level * area)[:, None, :]) * jnp.broadcast_to(scale, (cols, LANES))[:, None, :]
    weights = jnp.where(inside, jnp.exp(jnp.where(inside, score, 0.0)), 0.0)
    inverse = 1.0 / reduce(weights)
    flow_row = reduce(weights * (row_step + row_offset).astype(f32)) * inverse
    flow_col = reduce(weights * (line - HALF + col_offset).astype(f32)) * inverse
    shape = (cols, LANES)
    node, lane = iota(shape, 0) + first, iota(shape, 1)
    sent = jnp.where(lane == node, flow_row, jnp.where(lane == node + nodes, flow_col, 0.0))
    sent = jnp.sum(sent, axis=0, keepdims=True)
    masks = mask_ref[...].astype(f32)
    masks = jnp.concatenate(
        [jnp.zeros((1, MASK_LANE), f32), masks, masks, jnp.zeros((1, LANES - MASK_LANE - 2 * nodes), f32)],
        axis=1,
    )
    sent = sent + jnp.where(is_upper, masks, 0.0)
    sends = (iota(out_ref.shape, 0) == row_index) & (is_upper | (group == step - 1))
    out_ref[...] = jnp.where(sends, sent, 0.0)


def home_kernel(rows, nodes, own_ref, *refs):
    out_ref, shift_ref, base_ref, swing_ref = refs[-4:]
    count = lax.axis_size("tile")
    rotated = (lax.axis_index("tile") + count - rows // 2) % count
    group, row_index = rotated // rows, rotated % rows
    grid = None
    for step in range(1, SECTIONS):
        part = refs[step - 1][...]
        grid = part if grid is None else jnp.where(group == step, part, grid)
    row_shift = own_row(relax(grid, rows, nodes), row_index)
    row_shift = jnp.where(group == 0, 0.0, row_shift)
    shift_ref[0, :, :] = row_shift[:, :nodes]
    shift_ref[1, :, :] = pltpu.roll(row_shift, LANES - nodes, 1)[:, :nodes]
    base_ref[...], swing_ref[...] = kernels_of(row_shift, 0, nodes, nodes)

    def one(index):
        here = columns(index)
        out_ref[:, here] = warp_indexed(own_ref[:, here], base_ref, swing_ref, index, nodes)

    looped(nodes, one)


def shards(sections, valid_mask, coarse_offsets):
    count = lax.axis_size("tile")
    rows = count // SECTIONS
    nodes = valid_mask.shape[1]
    cols = nodes // 2
    width = cols * PATCH
    place = lambda group, row: (group * rows + row + rows // 2) % count
    group = (lax.axis_index("tile") + count - rows // 2) % count // rows
    moved = lambda value, pairs: lax.ppermute(value, "tile", pairs)

    def swapped(lower, after=None):
        half = lax.dynamic_slice_in_dim(sections, jnp.where(group == lower, width, 0), width, 1)
        if after is not None:
            half, after = lax.optimization_barrier((half, after))
        ends = [(place(lower, i), place(lower + 1, i)) for i in range(rows)]
        return moved(half, ends + [(d, s) for s, d in ends])

    others = [swapped(0), swapped(1)]

    vmem = pl.BlockSpec(memory_space=pltpu.VMEM)
    smem = pl.BlockSpec(memory_space=pltpu.SMEM)
    params = pltpu.CompilerParams(vmem_limit_bytes=16 * 2**20)
    gathered = []
    for step in range(1, SECTIONS):
        extra = gathered[-1:]
        sent = pl.pallas_call(
            functools.partial(chain_kernel, step, rows, nodes),
            out_shape=jax.ShapeDtypeStruct((rows, LANES), f32),
            in_specs=[smem] + [vmem] * (3 + len(extra)),
            out_specs=vmem,
            scratch_shapes=[
                pltpu.VMEM((cols, WIDTH, LANES), f32),
                pltpu.VMEM((cols, 8 * WIDTH, LANES), f32),
                pltpu.VMEM((4, cols, 8, LANES), f32),
                pltpu.VMEM((2, cols, LANES), f32),
                pltpu.VMEM((cols, PATCH, PATCH), bf16),
                pltpu.VMEM((2 * cols, LANES), f32),
                pltpu.VMEM((2 * cols, LANES), f32),
            ],
            compiler_params=params,
            name=f"chain{step}",
        )(coarse_offsets, sections, others[step - 1], valid_mask, *extra)
        gathered.append(lax.psum(sent, "tile"))
        if step + 1 < SECTIONS - 1:
            others.append(swapped(step + 1, sent))
    return pl.pallas_call(
        functools.partial(home_kernel, rows, nodes),
        out_shape=(
            jax.ShapeDtypeStruct(sections.shape, bf16),
            jax.ShapeDtypeStruct((2, 1, nodes), f32),
        ),
        in_specs=[vmem] * SECTIONS,
        out_specs=(vmem, vmem),
        scratch_shapes=[pltpu.VMEM((2 * nodes, LANES), f32)] * 2,
        compiler_params=params,
        name="home",
    )(sections, *gathered)


def solution(mesh):
    placed = (P(("parts", "tile"), None), P(("parts", "tile"), None), P("parts", None))
    return jax.shard_map(
        shards,
        mesh=mesh,
        in_specs=placed,
        out_specs=(P(("parts", "tile"), None), P(None, ("parts", "tile"), None)),
        check_vma=False,
    )
```

```python
import functools
import math

import jax
import jax.numpy as jnp
from jax import lax
from jax.experimental import pallas as pl
from jax.experimental.pallas import tpu as pltpu
from jax.sharding import PartitionSpec as P

SECTIONS = 4
PATCH = 128
HALF = 4
SWEEPS = 3
LANES = 128
WIDTH = 2 * HALF + 1
MASK_LANE = 64
GROUP = 4
THIRD = WIDTH // 3
SPAN = PATCH // 2 + 16

sharpness = 12.0
anchor_weight = 2.0
f32 = jnp.float32
bf16 = jnp.bfloat16


def iota(shape, axis):
    return lax.broadcasted_iota(jnp.int32, shape, axis)


def split(value):
    high = value.astype(bf16)
    return high, (value - high.astype(f32)).astype(bf16)


def dot(lhs, rhs):
    return jnp.dot(lhs, rhs, preferred_element_type=f32)


def dot_t(lhs, rhs):
    return lax.dot_general(lhs, rhs, (((1,), (1,)), ((), ())), preferred_element_type=f32)


def sine(x):
    y = x * x
    acc = jnp.full_like(x, 1.0 / math.factorial(13))
    for order in (11, 9, 7, 5, 3, 1):
        acc = (-1.0 if order % 4 == 3 else 1.0) / math.factorial(order) + y * acc
    return x * acc


def cosine(x):
    y = x * x
    acc = jnp.full_like(x, 1.0 / math.factorial(12))
    for order in (10, 8, 6, 4, 2, 0):
        acc = (-1.0 if order % 4 == 2 else 1.0) / math.factorial(order) + y * acc
    return acc


def total(value):
    return jnp.sum(jnp.sum(value, axis=0, keepdims=True), axis=1, keepdims=True)


def tile_sum(value):
    parts = [value[r : r + 8] for r in range(0, value.shape[0], 8)]
    while len(parts) > 1:
        parts = [x + y for x, y in zip(parts[::2], parts[1::2])]
    return parts[0]


def sign_tile(shape):
    return (1 - 2 * ((iota(shape, 0) + iota(shape, 1)) % 2)).astype(f32)


def section_grid(gathered, step, rows):
    count = gathered.shape[0]
    out = None
    for group in (step - 1, step):
        start = (group * rows + rows // 2) % count
        part = jnp.concatenate([gathered[start:], gathered[:start]], axis=0)[:rows]
        out = part if out is None else out + part
    return jnp.concatenate([out, jnp.zeros((8 - rows % 8, LANES), f32)], axis=0)


def relax(grid, rows, nodes):
    shape = grid.shape
    row, lane = iota(shape, 0), iota(shape, 1)
    col = lane % nodes
    valid = (row < rows) & (lane < 2 * nodes)
    mask = pltpu.roll(grid, LANES - MASK_LANE, 1)
    one = lambda cond: jnp.where(cond, 1.0, 0.0)
    count = one(row > 0) + one(row < rows - 1) + one(col > 0) + one(col < nodes - 1)
    weight = anchor_weight * mask
    inverse = 1.0 / jnp.where(valid, weight + count, 1.0)
    pulled = weight * grid
    shift = jnp.where(valid, grid * mask, 0.0)
    for _ in range(SWEEPS):
        near = pltpu.roll(shift, 1, 0) + pltpu.roll(shift, shape[0] - 1, 0)
        near += jnp.where(col > 0, pltpu.roll(shift, 1, 1), 0.0)
        near += jnp.where(col < nodes - 1, pltpu.roll(shift, LANES - 1, 1), 0.0)
        shift = jnp.where(valid, (pulled + near) * inverse, 0.0)
    return shift


def own_row(shift, index):
    return jnp.sum(jnp.where(iota(shift.shape, 0) == index, shift, 0.0), axis=0, keepdims=True)


def kernels_of(row_shift, first, cols, nodes):
    shape = (2 * cols, LANES)
    sub, lane = iota(shape, 0), iota(shape, 1)
    is_row = sub < cols
    target = first + jnp.where(is_row, sub, sub - cols + nodes)
    shift = jnp.sum(jnp.where(lane == target, row_shift, 0.0), axis=1, keepdims=True)
    shift = jnp.broadcast_to(shift, shape)
    whole = jnp.floor(shift + 0.5)
    part = shift - whole
    steps = jnp.where(is_row, -lane, lane).astype(f32) + whole
    steps = steps - LANES * jnp.floor((steps + LANES // 2) * (1.0 / LANES))
    sign = lambda n: 1.0 - 2.0 * (n - 2.0 * jnp.floor(n * 0.5))
    swing = sine(part * math.pi)
    angle = (steps + part) * (math.pi / LANES)
    centre = (steps == 0.0) & (jnp.abs(part) < 1e-20)
    below = jnp.where(centre, 1.0, sine(angle))
    base = swing * sign(steps) * (1.0 / LANES) * cosine(angle) / below
    return jnp.where(centre, 1.0, base), swing * sign(whole)


def circulant(row):
    return pltpu.roll(jnp.broadcast_to(row, (PATCH, LANES)), 0, 1, stride=1, stride_axis=0)


def warp(patch, row_base, col_base, row_swing, col_swing, nyquist):
    row_high, row_low = split(circulant(row_base))
    col_high, col_low = split(circulant(col_base))
    inner = dot(
        jnp.concatenate([patch, patch], axis=1), jnp.concatenate([col_high, col_low], axis=0)
    )
    in_high, in_low = split(inner)
    upper = jnp.concatenate([in_high, in_low], axis=1)
    lower = jnp.concatenate([in_high, jnp.zeros_like(in_low)], axis=1)
    out = dot(
        jnp.concatenate([row_high, row_low], axis=1), jnp.concatenate([upper, lower], axis=0)
    )
    out = out[:, :LANES] + out[:, LANES:]
    factor = row_swing * col_swing * nyquist * (1.0 / (PATCH * PATCH))
    return out - factor * sign_tile((PATCH, LANES))


def lag_layout(shape, axis):
    spot = (iota(shape, axis) + 16) % (2 * LANES)
    return spot // SPAN, 8 - spot % SPAN


def correlate(own, prev, level, column_offset, band_ref):
    own32, prev32 = own.astype(f32), prev.astype(f32)
    half = PATCH // 2
    left, right = [], []
    for i in range(THIRD):
        amount = (PATCH + HALF - i - column_offset) % PATCH
        turned = pltpu.roll(own32, amount, 1)
        low = jnp.concatenate([turned[PATCH - 8 :], turned[: half + 8]], axis=0)
        high = jnp.concatenate([turned[half - 8 :], turned[:8]], axis=0)
        left.append(jnp.concatenate([low, high], axis=1).astype(bf16))
    for j in range(THIRD):
        turned = pltpu.roll(prev32, THIRD * j, 1).astype(bf16) if j else prev
        right.append(jnp.concatenate([turned[:half], turned[half:]], axis=1))
        right.append(jnp.zeros((SPAN - half, 2 * LANES), bf16))
    right.append(jnp.zeros((2 * LANES - THIRD * SPAN, 2 * LANES), bf16))
    product = dot_t(jnp.concatenate(left, axis=0), jnp.concatenate(right, axis=0))
    spot = iota((8, 2 * LANES), 1) % SPAN
    base = jnp.where((spot < half) & (iota((8, 2 * LANES), 1) < THIRD * SPAN), level * (2.0 * LANES), 0.0)
    unused = lag_layout(spot.shape, 1)[1] >= 8 - iota(spot.shape, 0)
    for i in range(THIRD):
        tile = lambda r: product[i * SPAN + 8 * r : i * SPAN + 8 * r + 8]
        band = None
        for k in range(3):
            kept = tile(k)
            for m in range(1, 4 if k == 0 else 3):
                kept = jnp.where(spot >= 8 * k + 24 * m - 16, tile(k + 3 * m), kept)
            kept = kept - base
            kept = pltpu.roll(kept, 2 * LANES - 8 * k, 1) if k else kept
            band = kept if band is None else band + kept
        band = jnp.where(unused, 0.0, band)
        for side in range(2):
            band_ref[side, 8 * i : 8 * i + 8, :] = band[:, side * LANES : (side + 1) * LANES]
    out = None
    for row in range(8):
        part = jnp.concatenate(
            [band_ref[side, pl.ds(row, THIRD, stride=8), :] for side in range(2)], axis=1
        )
        part = pltpu.roll(part, 2 * LANES - row, 1) if row else part
        out = part if out is None else out + part
    back = lambda lanes: pltpu.roll(out, 2 * LANES - lanes, 1)
    _, row_lag = lag_layout(out.shape, 1)
    return out + back(24) + back(48) + jnp.where(row_lag > 0, back(72), 0.0)


def moments(values, corner):
    values = values.astype(f32) - corner
    return tile_sum(values), tile_sum(values * values)


def looped(count, one):
    def body(turn, carry):
        for k in range(GROUP):
            one(turn * GROUP + k)
        return carry

    lax.fori_loop(0, count // GROUP, body, 0)


def columns(index):
    return pl.ds(pl.multiple_of(index * PATCH, PATCH), PATCH)


def warp_indexed(patch, base_ref, swing_ref, index, cols):
    nyquist = total(tile_sum(patch.astype(f32)) * sign_tile((8, LANES)))
    return warp(
        patch,
        base_ref[pl.ds(index, 1), :],
        base_ref[pl.ds(index + cols, 1), :],
        swing_ref[pl.ds(index, 1), :],
        swing_ref[pl.ds(index + cols, 1), :],
        nyquist,
    ).astype(bf16)


def chain_kernel(step, rows, nodes, offsets_ref, own_ref, other_ref, mask_ref, *refs):
    out_ref, score_ref, band_ref, sums_ref, corner_ref, prev_ref, base_ref, swing_ref = refs[-8:]
    cols = nodes // 2
    count = lax.axis_size("tile")
    rotated = (lax.axis_index("tile") + count - rows // 2) % count
    group, row_index = rotated // rows, rotated % rows
    is_upper = group == step
    first = jnp.where(is_upper, cols, 0)
    row_offset, col_offset = offsets_ref[step, 0], offsets_ref[step, 1]
    area = float(PATCH * PATCH)

    if step > 1:
        row_shift = own_row(relax(section_grid(refs[0][...], step - 1, rows), rows, nodes), row_index)
        base_ref[...], swing_ref[...] = kernels_of(row_shift, first, cols, nodes)

        def warp_one(index):
            patch = jnp.where(is_upper, other_ref[:, columns(index)], own_ref[:, columns(index)])
            prev_ref[index] = warp_indexed(patch, base_ref, swing_ref, index, cols)

        looped(cols, warp_one)

    def one(index):
        other = other_ref[:, columns(index)]
        own = jnp.where(is_upper, own_ref[:, columns(index + cols)], other)
        prev = prev_ref[index] if step > 1 else jnp.where(is_upper, other, own_ref[:, columns(index)])
        own_corner, prev_corner = (x[0:1, 0:1].astype(f32) for x in (own, prev))
        corner_ref[0, pl.ds(index, 1), :] = jnp.broadcast_to(own_corner, (1, LANES))
        corner_ref[1, pl.ds(index, 1), :] = jnp.broadcast_to(prev_corner, (1, LANES))
        sums = moments(own, own_corner) + moments(prev, prev_corner)
        for k, value in enumerate(sums):
            sums_ref[k, pl.ds(index, 1)] = value[None]
        level = own_corner * prev_corner
        score_ref[pl.ds(index, 1)] = correlate(own, prev, level, col_offset, band_ref.at[index])[None]

    looped(cols, one)
    reduce = lambda value: jnp.sum(jnp.sum(value, axis=1), axis=1, keepdims=True)
    own_sum, own_square, prev_sum, prev_square = (reduce(sums_ref[k]) * (1.0 / area) for k in range(4))
    spread = jnp.sqrt(
        (jnp.maximum(own_square - own_sum * own_sum, 0.0) + 1e-5)
        * (jnp.maximum(prev_square - prev_sum * prev_sum, 0.0) + 1e-5)
    )
    scale = sharpness / area / spread
    level = corner_ref[0] * prev_sum + corner_ref[1] * own_sum + own_sum * prev_sum
    shape = (cols, THIRD, 2 * LANES)
    third, row_lag = lag_layout(shape, 2)
    col_lag = iota(shape, 1) + THIRD * third - HALF + col_offset
    inside = (jnp.abs(row_lag - row_offset) <= HALF) & (third < THIRD)
    level = jnp.concatenate([level, level], axis=1) * area
    scale = jnp.broadcast_to(scale, (cols, 2 * LANES))
    score = (score_ref[...] - level[:, None, :]) * scale[:, None, :]
    weights = jnp.where(inside, jnp.exp(jnp.where(inside, score, 0.0)), 0.0)
    inverse = 1.0 / reduce(weights)
    flow_row = reduce(weights * row_lag.astype(f32)) * inverse
    flow_col = reduce(weights * col_lag.astype(f32)) * inverse
    shape = (cols, LANES)
    node, lane = iota(shape, 0) + first, iota(shape, 1)
    sent = jnp.where(lane == node, flow_row, jnp.where(lane == node + nodes, flow_col, 0.0))
    sent = jnp.sum(sent, axis=0, keepdims=True)
    masks = mask_ref[...].astype(f32)
    masks = jnp.concatenate(
        [jnp.zeros((1, MASK_LANE), f32), masks, masks, jnp.zeros((1, LANES - MASK_LANE - 2 * nodes), f32)],
        axis=1,
    )
    sent = sent + jnp.where(is_upper, masks, 0.0)
    out_ref[...] = jnp.broadcast_to(sent, out_ref.shape)


def home_kernel(rows, nodes, own_ref, *refs):
    out_ref, shift_ref, base_ref, swing_ref = refs[-4:]
    count = lax.axis_size("tile")
    rotated = (lax.axis_index("tile") + count - rows // 2) % count
    group, row_index = rotated // rows, rotated % rows
    grid = None
    for step in range(1, SECTIONS):
        part = section_grid(refs[step - 1][...], step, rows)
        grid = part if grid is None else jnp.where(group == step, part, grid)
    row_shift = own_row(relax(grid, rows, nodes), row_index)
    row_shift = jnp.where(group == 0, 0.0, row_shift)
    shift_ref[0, :, :] = row_shift[:, :nodes]
    shift_ref[1, :, :] = pltpu.roll(row_shift, LANES - nodes, 1)[:, :nodes]
    base_ref[...], swing_ref[...] = kernels_of(row_shift, 0, nodes, nodes)

    def one(index):
        here = columns(index)
        out_ref[:, here] = warp_indexed(own_ref[:, here], base_ref, swing_ref, index, nodes)

    looped(nodes, one)


def shards(sections, valid_mask, coarse_offsets):
    count = lax.axis_size("tile")
    rows = count // SECTIONS
    nodes = valid_mask.shape[1]
    cols = nodes // 2
    width = cols * PATCH
    place = lambda group, row: (group * rows + row + rows // 2) % count
    group = (lax.axis_index("tile") + count - rows // 2) % count // rows
    moved = lambda value, pairs: lax.ppermute(value, "tile", pairs)

    def swapped(lower, after=None):
        half = lax.dynamic_slice_in_dim(sections, jnp.where(group == lower, width, 0), width, 1)
        if after is not None:
            half, after = lax.optimization_barrier((half, after))
        ends = [(place(lower, i), place(lower + 1, i)) for i in range(rows)]
        return moved(half, ends + [(d, s) for s, d in ends])

    others = [swapped(0), swapped(1)]

    vmem = pl.BlockSpec(memory_space=pltpu.VMEM)
    smem = pl.BlockSpec(memory_space=pltpu.SMEM)
    params = pltpu.CompilerParams(vmem_limit_bytes=16 * 2**20)
    gathered = []
    for step in range(1, SECTIONS):
        extra = gathered[-1:]
        sent = pl.pallas_call(
            functools.partial(chain_kernel, step, rows, nodes),
            out_shape=jax.ShapeDtypeStruct((count, LANES), f32),
            in_specs=[smem] + [vmem] * (3 + len(extra)),
            out_specs=vmem,
            scratch_shapes=[
                pltpu.VMEM((cols, THIRD, 2 * LANES), f32),
                pltpu.VMEM((cols, 2, 8 * THIRD, LANES), f32),
                pltpu.VMEM((4, cols, 8, LANES), f32),
                pltpu.VMEM((2, cols, LANES), f32),
                pltpu.VMEM((cols, PATCH, PATCH), bf16),
                pltpu.VMEM((2 * cols, LANES), f32),
                pltpu.VMEM((2 * cols, LANES), f32),
            ],
            compiler_params=params,
            name=f"chain{step}",
        )(coarse_offsets, sections, others[step - 1], valid_mask, *extra)
        gathered.append(lax.all_to_all(sent, "tile", 0, 0, tiled=True))
        if step + 1 < SECTIONS - 1:
            others.append(swapped(step + 1, sent))
    return pl.pallas_call(
        functools.partial(home_kernel, rows, nodes),
        out_shape=(
            jax.ShapeDtypeStruct(sections.shape, bf16),
            jax.ShapeDtypeStruct((2, 1, nodes), f32),
        ),
        in_specs=[vmem] * SECTIONS,
        out_specs=(vmem, vmem),
        scratch_shapes=[pltpu.VMEM((2 * nodes, LANES), f32)] * 2,
        compiler_params=params,
        name="home",
    )(sections, *gathered)


def solution(mesh):
    placed = (P(("parts", "tile"), None), P(("parts", "tile"), None), P("parts", None))
    return jax.shard_map(
        shards,
        mesh=mesh,
        in_specs=placed,
        out_specs=(P(("parts", "tile"), None), P(None, ("parts", "tile"), None)),
        check_vma=False,
    )
```

```python
import functools
import math

import jax
import jax.numpy as jnp
from jax import lax
from jax.experimental import pallas as pl
from jax.experimental.pallas import tpu as pltpu
from jax.sharding import PartitionSpec as P

SECTIONS = 4
PATCH = 128
HALF = 4
SWEEPS = 3
LANES = 128
WIDTH = 2 * HALF + 1
MASK_LANE = 64
GROUP = 4
THIRD = WIDTH // 3
SPAN = PATCH // 2 + 16

sharpness = 12.0
anchor_weight = 2.0
f32 = jnp.float32
bf16 = jnp.bfloat16


def iota(shape, axis):
    return lax.broadcasted_iota(jnp.int32, shape, axis)


def split(value):
    high = value.astype(bf16)
    return high, (value - high.astype(f32)).astype(bf16)


def dot(lhs, rhs):
    return jnp.dot(lhs, rhs, preferred_element_type=f32)


def dot_t(lhs, rhs):
    return lax.dot_general(lhs, rhs, (((1,), (1,)), ((), ())), preferred_element_type=f32)


def sine(x):
    y = x * x
    acc = jnp.full_like(x, 1.0 / math.factorial(13))
    for order in (11, 9, 7, 5, 3, 1):
        acc = (-1.0 if order % 4 == 3 else 1.0) / math.factorial(order) + y * acc
    return x * acc


def cosine(x):
    y = x * x
    acc = jnp.full_like(x, 1.0 / math.factorial(12))
    for order in (10, 8, 6, 4, 2, 0):
        acc = (-1.0 if order % 4 == 2 else 1.0) / math.factorial(order) + y * acc
    return acc


def total(value):
    return jnp.sum(jnp.sum(value, axis=0, keepdims=True), axis=1, keepdims=True)


def tile_sum(value):
    parts = [value[r : r + 8] for r in range(0, value.shape[0], 8)]
    while len(parts) > 1:
        parts = [x + y for x, y in zip(parts[::2], parts[1::2])]
    return parts[0]


def sign_tile(shape):
    return (1 - 2 * ((iota(shape, 0) + iota(shape, 1)) % 2)).astype(f32)


def section_grid(gathered, step, rows):
    count = gathered.shape[0]
    out = None
    for group in (step - 1, step):
        start = (group * rows + rows // 2) % count
        part = jnp.concatenate([gathered[start:], gathered[:start]], axis=0)[:rows]
        out = part if out is None else out + part
    return jnp.concatenate([out, jnp.zeros((8 - rows % 8, LANES), f32)], axis=0)


def relax(grid, rows, nodes):
    shape = grid.shape
    row, lane = iota(shape, 0), iota(shape, 1)
    col = lane % nodes
    valid = (row < rows) & (lane < 2 * nodes)
    mask = pltpu.roll(grid, LANES - MASK_LANE, 1)
    one = lambda cond: jnp.where(cond, 1.0, 0.0)
    count = one(row > 0) + one(row < rows - 1) + one(col > 0) + one(col < nodes - 1)
    weight = anchor_weight * mask
    inverse = 1.0 / jnp.where(valid, weight + count, 1.0)
    pulled = weight * grid
    shift = jnp.where(valid, grid * mask, 0.0)
    for _ in range(SWEEPS):
        near = pltpu.roll(shift, 1, 0) + pltpu.roll(shift, shape[0] - 1, 0)
        near += jnp.where(col > 0, pltpu.roll(shift, 1, 1), 0.0)
        near += jnp.where(col < nodes - 1, pltpu.roll(shift, LANES - 1, 1), 0.0)
        shift = jnp.where(valid, (pulled + near) * inverse, 0.0)
    return shift


def own_row(shift, index):
    return jnp.sum(jnp.where(iota(shift.shape, 0) == index, shift, 0.0), axis=0, keepdims=True)


def kernels_of(row_shift, first, cols, nodes):
    shape = (2 * cols, LANES)
    sub, lane = iota(shape, 0), iota(shape, 1)
    is_row = sub < cols
    target = first + jnp.where(is_row, sub, sub - cols + nodes)
    shift = jnp.sum(jnp.where(lane == target, row_shift, 0.0), axis=1, keepdims=True)
    shift = jnp.broadcast_to(shift, shape)
    whole = jnp.floor(shift + 0.5)
    part = shift - whole
    steps = jnp.where(is_row, -lane, lane).astype(f32) + whole
    steps = steps - LANES * jnp.floor((steps + LANES // 2) * (1.0 / LANES))
    sign = lambda n: 1.0 - 2.0 * (n - 2.0 * jnp.floor(n * 0.5))
    swing = sine(part * math.pi)
    angle = (steps + part) * (math.pi / LANES)
    centre = (steps == 0.0) & (jnp.abs(part) < 1e-20)
    below = jnp.where(centre, 1.0, sine(angle))
    base = swing * sign(steps) * (1.0 / LANES) * cosine(angle) / below
    return jnp.where(centre, 1.0, base), swing * sign(whole)


def circulant(row):
    return pltpu.roll(jnp.broadcast_to(row, (PATCH, LANES)), 0, 1, stride=1, stride_axis=0)


def warp(patch, row_base, col_base, row_swing, col_swing, nyquist):
    row_high, row_low = split(circulant(row_base))
    col_high, col_low = split(circulant(col_base))
    inner = dot(
        jnp.concatenate([patch, patch], axis=1), jnp.concatenate([col_high, col_low], axis=0)
    )
    in_high, in_low = split(inner)
    upper = jnp.concatenate([in_high, in_low], axis=1)
    lower = jnp.concatenate([in_high, jnp.zeros_like(in_low)], axis=1)
    out = dot(
        jnp.concatenate([row_high, row_low], axis=1), jnp.concatenate([upper, lower], axis=0)
    )
    out = out[:, :LANES] + out[:, LANES:]
    factor = row_swing * col_swing * nyquist * (1.0 / (PATCH * PATCH))
    return out - factor * sign_tile((PATCH, LANES))


def lag_layout(shape, axis):
    spot = (iota(shape, axis) + 16) % (2 * LANES)
    return spot // SPAN, 8 - spot % SPAN


def correlate(own, prev, level, column_offset, band_ref):
    own32, prev32 = own.astype(f32), prev.astype(f32)
    half = PATCH // 2
    left, right = [], []
    for i in range(THIRD):
        amount = (PATCH + HALF - i - column_offset) % PATCH
        turned = pltpu.roll(own32, amount, 1)
        low = jnp.concatenate([turned[PATCH - 8 :], turned[: half + 8]], axis=0)
        high = jnp.concatenate([turned[half - 8 :], turned[:8]], axis=0)
        left.append(jnp.concatenate([low, high], axis=1).astype(bf16))
    for j in range(THIRD):
        turned = pltpu.roll(prev32, THIRD * j, 1).astype(bf16) if j else prev
        right.append(jnp.concatenate([turned[:half], turned[half:]], axis=1))
        right.append(jnp.zeros((SPAN - half, 2 * LANES), bf16))
    right.append(jnp.zeros((2 * LANES - THIRD * SPAN, 2 * LANES), bf16))
    product = dot_t(jnp.concatenate(left, axis=0), jnp.concatenate(right, axis=0))
    spot = iota((8, 2 * LANES), 1) % SPAN
    base = jnp.where((spot < half) & (iota((8, 2 * LANES), 1) < THIRD * SPAN), level * (2.0 * LANES), 0.0)
    unused = lag_layout(spot.shape, 1)[1] >= 8 - iota(spot.shape, 0)
    for i in range(THIRD):
        tile = lambda r: product[i * SPAN + 8 * r : i * SPAN + 8 * r + 8]
        band = None
        for k in range(3):
            kept = tile(k)
            for m in range(1, 4 if k == 0 else 3):
                kept = jnp.where(spot >= 8 * k + 24 * m - 16, tile(k + 3 * m), kept)
            kept = kept - base
            kept = pltpu.roll(kept, 2 * LANES - 8 * k, 1) if k else kept
            band = kept if band is None else band + kept
        band = jnp.where(unused, 0.0, band)
        for side in range(2):
            band_ref[side, 8 * i : 8 * i + 8, :] = band[:, side * LANES : (side + 1) * LANES]
    out = None
    for row in range(8):
        part = jnp.concatenate(
            [band_ref[side, pl.ds(row, THIRD, stride=8), :] for side in range(2)], axis=1
        )
        part = pltpu.roll(part, 2 * LANES - row, 1) if row else part
        out = part if out is None else out + part
    back = lambda lanes: pltpu.roll(out, 2 * LANES - lanes, 1)
    _, row_lag = lag_layout(out.shape, 1)
    return out + back(24) + back(48) + jnp.where(row_lag > 0, back(72), 0.0)


def moments(values, corner):
    values = values.astype(f32) - corner
    return tile_sum(values), tile_sum(values * values)


def looped(count, one):
    def body(turn, carry):
        for k in range(GROUP):
            one(turn * GROUP + k, k)
        return carry

    lax.fori_loop(0, count // GROUP, body, 0)


def columns(index):
    return pl.ds(pl.multiple_of(index * PATCH, PATCH), PATCH)


def warp_indexed(patch, base_ref, swing_ref, index, cols):
    nyquist = total(tile_sum(patch.astype(f32)) * sign_tile((8, LANES)))
    return warp(
        patch,
        base_ref[pl.ds(index, 1), :],
        base_ref[pl.ds(index + cols, 1), :],
        swing_ref[pl.ds(index, 1), :],
        swing_ref[pl.ds(index + cols, 1), :],
        nyquist,
    ).astype(bf16)


def chain_kernel(step, rows, nodes, begin, cols, offsets_ref, own_ref, other_ref, mask_ref, *refs):
    out_ref, score_ref, band_ref, sums_ref, corner_ref, prev_ref, base_ref, swing_ref = refs[-8:]
    count = lax.axis_size("tile")
    rotated = (lax.axis_index("tile") + count - rows // 2) % count
    group, row_index = rotated // rows, rotated % rows
    is_upper = group == step
    first = begin + jnp.where(is_upper, nodes // 2, 0)
    row_offset, col_offset = offsets_ref[step, 0], offsets_ref[step, 1]
    area = float(PATCH * PATCH)

    if step > 1:
        row_shift = own_row(relax(section_grid(refs[0][...], step - 1, rows), rows, nodes), row_index)
        base_ref[...], swing_ref[...] = kernels_of(row_shift, first, cols, nodes)

        def warp_one(index, slot):
            patch = jnp.where(is_upper, other_ref[:, columns(index)], own_ref[:, columns(index + begin)])
            prev_ref[index] = warp_indexed(patch, base_ref, swing_ref, index, cols)

        looped(cols, warp_one)

    def one(index, slot):
        other = other_ref[:, columns(index)]
        own = jnp.where(is_upper, own_ref[:, columns(index + begin + nodes // 2)], other)
        if step > 1:
            prev = prev_ref[index]
        else:
            prev = jnp.where(is_upper, other, own_ref[:, columns(index + begin)])
        own_corner, prev_corner = (x[0:1, 0:1].astype(f32) for x in (own, prev))
        corner_ref[0, pl.ds(index, 1), :] = jnp.broadcast_to(own_corner, (1, LANES))
        corner_ref[1, pl.ds(index, 1), :] = jnp.broadcast_to(prev_corner, (1, LANES))
        sums = moments(own, own_corner) + moments(prev, prev_corner)
        for k, value in enumerate(sums):
            sums_ref[k, pl.ds(index, 1)] = value[None]
        level = own_corner * prev_corner
        score_ref[pl.ds(index, 1)] = correlate(own, prev, level, col_offset, band_ref.at[slot])[None]

    looped(cols, one)
    reduce = lambda value: jnp.sum(jnp.sum(value, axis=1), axis=1, keepdims=True)
    own_sum, own_square, prev_sum, prev_square = (reduce(sums_ref[k]) * (1.0 / area) for k in range(4))
    spread = jnp.sqrt(
        (jnp.maximum(own_square - own_sum * own_sum, 0.0) + 1e-5)
        * (jnp.maximum(prev_square - prev_sum * prev_sum, 0.0) + 1e-5)
    )
    scale = sharpness / area / spread
    level = corner_ref[0] * prev_sum + corner_ref[1] * own_sum + own_sum * prev_sum
    shape = (cols, THIRD, 2 * LANES)
    third, row_lag = lag_layout(shape, 2)
    col_lag = iota(shape, 1) + THIRD * third - HALF + col_offset
    inside = (jnp.abs(row_lag - row_offset) <= HALF) & (third < THIRD)
    level = jnp.concatenate([level, level], axis=1) * area
    scale = jnp.broadcast_to(scale, (cols, 2 * LANES))
    score = (score_ref[...] - level[:, None, :]) * scale[:, None, :]
    weights = jnp.where(inside, jnp.exp(jnp.where(inside, score, 0.0)), 0.0)
    inverse = 1.0 / reduce(weights)
    flow_row = reduce(weights * row_lag.astype(f32)) * inverse
    flow_col = reduce(weights * col_lag.astype(f32)) * inverse
    shape = (cols, LANES)
    node, lane = iota(shape, 0) + first, iota(shape, 1)
    sent = jnp.where(lane == node, flow_row, jnp.where(lane == node + nodes, flow_col, 0.0))
    sent = jnp.sum(sent, axis=0, keepdims=True)
    if begin == 0:
        masks = mask_ref[...].astype(f32)
        masks = jnp.concatenate(
            [jnp.zeros((1, MASK_LANE), f32), masks, masks, jnp.zeros((1, LANES - MASK_LANE - 2 * nodes), f32)],
            axis=1,
        )
        sent = sent + jnp.where(is_upper, masks, 0.0)
    else:
        sent = sent + refs[0][0:1, :]
    out_ref[...] = jnp.broadcast_to(sent, out_ref.shape)


def home_kernel(rows, nodes, own_ref, *refs):
    out_ref, shift_ref, base_ref, swing_ref = refs[-4:]
    count = lax.axis_size("tile")
    rotated = (lax.axis_index("tile") + count - rows // 2) % count
    group, row_index = rotated // rows, rotated % rows
    grid = None
    for step in range(1, SECTIONS):
        part = section_grid(refs[step - 1][...], step, rows)
        grid = part if grid is None else jnp.where(group == step, part, grid)
    row_shift = own_row(relax(grid, rows, nodes), row_index)
    row_shift = jnp.where(group == 0, 0.0, row_shift)
    shift_ref[0, :, :] = row_shift[:, :nodes]
    shift_ref[1, :, :] = pltpu.roll(row_shift, LANES - nodes, 1)[:, :nodes]
    base_ref[...], swing_ref[...] = kernels_of(row_shift, 0, nodes, nodes)

    def one(index, slot):
        here = columns(index)
        out_ref[:, here] = warp_indexed(own_ref[:, here], base_ref, swing_ref, index, nodes)

    looped(nodes, one)


def shards(sections, valid_mask, coarse_offsets):
    count = lax.axis_size("tile")
    rows = count // SECTIONS
    nodes = valid_mask.shape[1]
    place = lambda group, row: (group * rows + row + rows // 2) % count
    group = (lax.axis_index("tile") + count - rows // 2) % count // rows
    moved = lambda value, pairs: lax.ppermute(value, "tile", pairs)

    def swapped(source, lower, begin, cols, after=None):
        start = (begin + jnp.where(group == lower, nodes // 2, 0)) * PATCH
        half = lax.dynamic_slice_in_dim(source, start, cols * PATCH, 1)
        if after is not None:
            half, after = lax.optimization_barrier((half, after))
        ends = [(place(lower, i), place(lower + 1, i)) for i in range(rows)]
        idle = [
            (place(s, i),) * 2 for s in range(SECTIONS) if s not in (lower, lower + 1) for i in range(rows)
        ]
        return half, moved(half, ends + [(d, s) for s, d in ends] + idle)

    half = nodes // 2
    chunk = half // 2
    head, first_chunk = swapped(sections, 0, 0, chunk)
    source, head = lax.optimization_barrier((sections, head))
    others = {
        1: [(0, chunk, first_chunk), (chunk, chunk, swapped(source, 0, chunk, chunk)[1])],
        2: [(0, half, swapped(source, 1, 0, half)[1])],
    }

    vmem = pl.BlockSpec(memory_space=pltpu.VMEM)
    smem = pl.BlockSpec(memory_space=pltpu.SMEM)
    params = pltpu.CompilerParams(vmem_limit_bytes=16 * 2**20)
    gathered = []
    for step in range(1, SECTIONS):
        extra = gathered[-1:]
        for begin, cols, other in others[step]:
            sent = pl.pallas_call(
                functools.partial(chain_kernel, step, rows, nodes, begin, cols),
                out_shape=jax.ShapeDtypeStruct((count, LANES), f32),
                in_specs=[smem] + [vmem] * (3 + len(extra)),
                out_specs=vmem,
                scratch_shapes=[
                    pltpu.VMEM((cols, THIRD, 2 * LANES), f32),
                    pltpu.VMEM((GROUP, 2, 8 * THIRD, LANES), f32),
                    pltpu.VMEM((4, cols, 8, LANES), f32),
                    pltpu.VMEM((2, cols, LANES), f32),
                    pltpu.VMEM((cols, PATCH, PATCH), bf16),
                    pltpu.VMEM((2 * cols, LANES), f32),
                    pltpu.VMEM((2 * cols, LANES), f32),
                ],
                compiler_params=params,
                name=f"chain{step}_{begin}",
            )(coarse_offsets, sections, other, valid_mask, *extra)
            extra = [sent]
        gathered.append(lax.all_to_all(sent, "tile", 0, 0, tiled=True))
        if step + 1 < SECTIONS - 1:
            others[step + 2] = [(0, half, swapped(source, step + 1, 0, half, sent)[1])]
    return pl.pallas_call(
        functools.partial(home_kernel, rows, nodes),
        out_shape=(
            jax.ShapeDtypeStruct(sections.shape, bf16),
            jax.ShapeDtypeStruct((2, 1, nodes), f32),
        ),
        in_specs=[vmem] * SECTIONS,
        out_specs=(vmem, vmem),
        scratch_shapes=[pltpu.VMEM((2 * nodes, LANES), f32)] * 2,
        compiler_params=params,
        name="home",
    )(sections, *gathered)


def solution(mesh):
    placed = (P(("parts", "tile"), None), P(("parts", "tile"), None), P("parts", None))
    return jax.shard_map(
        shards,
        mesh=mesh,
        in_specs=placed,
        out_specs=(P(("parts", "tile"), None), P(None, ("parts", "tile"), None)),
        check_vma=False,
    )
```

```python
import functools
import math

import jax
import jax.numpy as jnp
from jax import lax
from jax.experimental import pallas as pl
from jax.experimental.pallas import tpu as pltpu
from jax.sharding import PartitionSpec as P

SECTIONS = 4
PATCH = 128
HALF = 4
SWEEPS = 3
LANES = 128
WIDTH = 2 * HALF + 1
MASK_LANE = 64
GROUP = 8
THIRD = WIDTH // 3
SPAN = PATCH // 2 + 16

sharpness = 12.0
anchor_weight = 2.0
f32 = jnp.float32
bf16 = jnp.bfloat16


def iota(shape, axis):
    return lax.broadcasted_iota(jnp.int32, shape, axis)


def split(value):
    high = value.astype(bf16)
    return high, (value - high.astype(f32)).astype(bf16)


def dot(lhs, rhs):
    return jnp.dot(lhs, rhs, preferred_element_type=f32)


def dot_t(lhs, rhs):
    return lax.dot_general(lhs, rhs, (((1,), (1,)), ((), ())), preferred_element_type=f32)


def sine(x):
    y = x * x
    acc = jnp.full_like(x, 1.0 / math.factorial(13))
    for order in (11, 9, 7, 5, 3, 1):
        acc = (-1.0 if order % 4 == 3 else 1.0) / math.factorial(order) + y * acc
    return x * acc


def cosine(x):
    y = x * x
    acc = jnp.full_like(x, 1.0 / math.factorial(12))
    for order in (10, 8, 6, 4, 2, 0):
        acc = (-1.0 if order % 4 == 2 else 1.0) / math.factorial(order) + y * acc
    return acc


def total(value):
    return jnp.sum(jnp.sum(value, axis=0, keepdims=True), axis=1, keepdims=True)


def tile_sum(value):
    parts = [value[r : r + 8] for r in range(0, value.shape[0], 8)]
    while len(parts) > 1:
        parts = [x + y for x, y in zip(parts[::2], parts[1::2])]
    return parts[0]


def sign_tile(shape):
    return (1 - 2 * ((iota(shape, 0) + iota(shape, 1)) % 2)).astype(f32)


def section_grid(gathered, step, rows):
    count = gathered.shape[0]
    out = None
    for group in (step - 1, step):
        start = (group * rows + rows // 2) % count
        part = jnp.concatenate([gathered[start:], gathered[:start]], axis=0)[:rows]
        out = part if out is None else out + part
    return jnp.concatenate([out, jnp.zeros((8 - rows % 8, LANES), f32)], axis=0)


def relax(grid, rows, nodes):
    shape = grid.shape
    row, lane = iota(shape, 0), iota(shape, 1)
    col = lane % nodes
    valid = (row < rows) & (lane < 2 * nodes)
    mask = pltpu.roll(grid, LANES - MASK_LANE, 1)
    one = lambda cond: jnp.where(cond, 1.0, 0.0)
    count = one(row > 0) + one(row < rows - 1) + one(col > 0) + one(col < nodes - 1)
    weight = anchor_weight * mask
    inverse = 1.0 / jnp.where(valid, weight + count, 1.0)
    pulled = weight * grid
    shift = jnp.where(valid, grid * mask, 0.0)
    for _ in range(SWEEPS):
        near = pltpu.roll(shift, 1, 0) + pltpu.roll(shift, shape[0] - 1, 0)
        near += jnp.where(col > 0, pltpu.roll(shift, 1, 1), 0.0)
        near += jnp.where(col < nodes - 1, pltpu.roll(shift, LANES - 1, 1), 0.0)
        shift = jnp.where(valid, (pulled + near) * inverse, 0.0)
    return shift


def own_row(shift, index):
    return jnp.sum(jnp.where(iota(shift.shape, 0) == index, shift, 0.0), axis=0, keepdims=True)


def kernels_of(row_shift, first, cols, nodes):
    shape = (2 * cols, LANES)
    sub, lane = iota(shape, 0), iota(shape, 1)
    is_row = sub < cols
    target = first + jnp.where(is_row, sub, sub - cols + nodes)
    shift = jnp.sum(jnp.where(lane == target, row_shift, 0.0), axis=1, keepdims=True)
    shift = jnp.broadcast_to(shift, shape)
    whole = jnp.floor(shift + 0.5)
    part = shift - whole
    steps = jnp.where(is_row, -lane, lane).astype(f32) + whole
    steps = steps - LANES * jnp.floor((steps + LANES // 2) * (1.0 / LANES))
    sign = lambda n: 1.0 - 2.0 * (n - 2.0 * jnp.floor(n * 0.5))
    swing = sine(part * math.pi)
    angle = (steps + part) * (math.pi / LANES)
    centre = (steps == 0.0) & (jnp.abs(part) < 1e-20)
    below = jnp.where(centre, 1.0, sine(angle))
    base = swing * sign(steps) * (1.0 / LANES) * cosine(angle) / below
    return jnp.where(centre, 1.0, base), swing * sign(whole)


def circulant(row):
    return pltpu.roll(jnp.broadcast_to(row, (PATCH, LANES)), 0, 1, stride=1, stride_axis=0)


def warp(patch, row_base, col_base, row_swing, col_swing, nyquist):
    row_high, row_low = split(circulant(row_base))
    col_high, col_low = split(circulant(col_base))
    inner = dot(
        jnp.concatenate([patch, patch], axis=1), jnp.concatenate([col_high, col_low], axis=0)
    )
    in_high, in_low = split(inner)
    upper = jnp.concatenate([in_high, in_low], axis=1)
    lower = jnp.concatenate([in_high, jnp.zeros_like(in_low)], axis=1)
    out = dot(
        jnp.concatenate([row_high, row_low], axis=1), jnp.concatenate([upper, lower], axis=0)
    )
    out = out[:, :LANES] + out[:, LANES:]
    factor = row_swing * col_swing * nyquist * (1.0 / (PATCH * PATCH))
    return out - factor * sign_tile((PATCH, LANES))


def lag_layout(shape, axis):
    spot = (iota(shape, axis) + 16) % (2 * LANES)
    return spot // SPAN, 8 - spot % SPAN


def correlate(own, prev, level, column_offset, band_ref):
    own32, prev32 = own.astype(f32), prev.astype(f32)
    half = PATCH // 2
    left, right = [], []
    for i in range(THIRD):
        amount = (PATCH + HALF - i - column_offset) % PATCH
        turned = pltpu.roll(own32, amount, 1)
        low = jnp.concatenate([turned[PATCH - 8 :], turned[: half + 8]], axis=0)
        high = jnp.concatenate([turned[half - 8 :], turned[:8]], axis=0)
        left.append(jnp.concatenate([low, high], axis=1).astype(bf16))
    for j in range(THIRD):
        turned = pltpu.roll(prev32, THIRD * j, 1).astype(bf16) if j else prev
        right.append(jnp.concatenate([turned[:half], turned[half:]], axis=1))
        right.append(jnp.zeros((SPAN - half, 2 * LANES), bf16))
    right.append(jnp.zeros((2 * LANES - THIRD * SPAN, 2 * LANES), bf16))
    product = dot_t(jnp.concatenate(left, axis=0), jnp.concatenate(right, axis=0))
    spot = iota((8, 2 * LANES), 1) % SPAN
    base = jnp.where((spot < half) & (iota((8, 2 * LANES), 1) < THIRD * SPAN), level * (2.0 * LANES), 0.0)
    unused = lag_layout(spot.shape, 1)[1] >= 8 - iota(spot.shape, 0)
    for i in range(THIRD):
        tile = lambda r: product[i * SPAN + 8 * r : i * SPAN + 8 * r + 8]
        band = None
        for k in range(3):
            kept = tile(k)
            for m in range(1, 4 if k == 0 else 3):
                kept = jnp.where(spot >= 8 * k + 24 * m - 16, tile(k + 3 * m), kept)
            kept = kept - base
            kept = pltpu.roll(kept, 2 * LANES - 8 * k, 1) if k else kept
            band = kept if band is None else band + kept
        band = jnp.where(unused, 0.0, band)
        for side in range(2):
            band_ref[side, 8 * i : 8 * i + 8, :] = band[:, side * LANES : (side + 1) * LANES]
    out = None
    for row in range(8):
        part = jnp.concatenate(
            [band_ref[side, pl.ds(row, THIRD, stride=8), :] for side in range(2)], axis=1
        )
        part = pltpu.roll(part, 2 * LANES - row, 1) if row else part
        out = part if out is None else out + part
    back = lambda lanes: pltpu.roll(out, 2 * LANES - lanes, 1)
    _, row_lag = lag_layout(out.shape, 1)
    return out + back(24) + back(48) + jnp.where(row_lag > 0, back(72), 0.0)


def moments(values, corner):
    values = values.astype(f32) - corner
    return tile_sum(values), tile_sum(values * values)


def looped(count, one):
    width = min(GROUP, count)

    def body(turn, carry):
        for k in range(width):
            one(turn * width + k, k)
        return carry

    if count == width:
        body(0, 0)
    else:
        lax.fori_loop(0, count // width, body, 0)


def columns(index):
    start = index * PATCH
    return pl.ds(start if isinstance(start, int) else pl.multiple_of(start, PATCH), PATCH)


def warp_indexed(patch, base_ref, swing_ref, index, cols):
    nyquist = total(tile_sum(patch.astype(f32)) * sign_tile((8, LANES)))
    return warp(
        patch,
        base_ref[pl.ds(index, 1), :],
        base_ref[pl.ds(index + cols, 1), :],
        swing_ref[pl.ds(index, 1), :],
        swing_ref[pl.ds(index + cols, 1), :],
        nyquist,
    ).astype(bf16)


def chain_kernel(step, rows, nodes, begin, cols, offsets_ref, own_ref, other_ref, mask_ref, *refs):
    out_ref, score_ref, band_ref, sums_ref, corner_ref, prev_ref, base_ref, swing_ref = refs[-8:]
    count = lax.axis_size("tile")
    rotated = (lax.axis_index("tile") + count - rows // 2) % count
    group, row_index = rotated // rows, rotated % rows
    is_upper = group == step
    first = begin + jnp.where(is_upper, nodes // 2, 0)

    @pl.when(is_upper | (group == step - 1))
    def _():
        row_offset, col_offset = offsets_ref[step, 0], offsets_ref[step, 1]
        area = float(PATCH * PATCH)

        if step > 1:
            row_shift = own_row(relax(section_grid(refs[0][...], step - 1, rows), rows, nodes), row_index)
            base_ref[...], swing_ref[...] = kernels_of(row_shift, first, cols, nodes)

            def warp_one(index, slot):
                patch = jnp.where(is_upper, other_ref[:, columns(index)], own_ref[:, columns(index + begin)])
                prev_ref[index] = warp_indexed(patch, base_ref, swing_ref, index, cols)

            looped(cols, warp_one)

        def one(index, slot):
            other = other_ref[:, columns(index)]
            own = jnp.where(is_upper, own_ref[:, columns(index + begin + nodes // 2)], other)
            if step > 1:
                prev = prev_ref[index]
            else:
                prev = jnp.where(is_upper, other, own_ref[:, columns(index + begin)])
            own_corner, prev_corner = (x[0:1, 0:1].astype(f32) for x in (own, prev))
            corner_ref[0, pl.ds(index, 1), :] = jnp.broadcast_to(own_corner, (1, LANES))
            corner_ref[1, pl.ds(index, 1), :] = jnp.broadcast_to(prev_corner, (1, LANES))
            sums = moments(own, own_corner) + moments(prev, prev_corner)
            for k, value in enumerate(sums):
                sums_ref[k, pl.ds(index, 1)] = value[None]
            level = own_corner * prev_corner
            score_ref[pl.ds(index, 1)] = correlate(own, prev, level, col_offset, band_ref.at[slot])[None]

        looped(cols, one)
        reduce = lambda value: jnp.sum(jnp.sum(value, axis=1), axis=1, keepdims=True)
        own_sum, own_square, prev_sum, prev_square = (reduce(sums_ref[k]) * (1.0 / area) for k in range(4))
        spread = jnp.sqrt(
            (jnp.maximum(own_square - own_sum * own_sum, 0.0) + 1e-5)
            * (jnp.maximum(prev_square - prev_sum * prev_sum, 0.0) + 1e-5)
        )
        scale = sharpness / area / spread
        level = corner_ref[0] * prev_sum + corner_ref[1] * own_sum + own_sum * prev_sum
        shape = (cols, THIRD, 2 * LANES)
        third, row_lag = lag_layout(shape, 2)
        col_lag = iota(shape, 1) + THIRD * third - HALF + col_offset
        inside = (jnp.abs(row_lag - row_offset) <= HALF) & (third < THIRD)
        level = jnp.concatenate([level, level], axis=1) * area
        scale = jnp.broadcast_to(scale, (cols, 2 * LANES))
        score = (score_ref[...] - level[:, None, :]) * scale[:, None, :]
        weights = jnp.where(inside, jnp.exp(jnp.where(inside, score, 0.0)), 0.0)
        inverse = 1.0 / reduce(weights)
        flow_row = reduce(weights * row_lag.astype(f32)) * inverse
        flow_col = reduce(weights * col_lag.astype(f32)) * inverse
        shape = (cols, LANES)
        node, lane = iota(shape, 0) + first, iota(shape, 1)
        sent = jnp.where(lane == node, flow_row, jnp.where(lane == node + nodes, flow_col, 0.0))
        sent = jnp.sum(sent, axis=0, keepdims=True)
        if begin == 0:
            masks = mask_ref[...].astype(f32)
            masks = jnp.concatenate(
                [jnp.zeros((1, MASK_LANE), f32), masks, masks, jnp.zeros((1, LANES - MASK_LANE - 2 * nodes), f32)],
                axis=1,
            )
            sent = sent + jnp.where(is_upper, masks, 0.0)
        else:
            sent = sent + refs[0][0:1, :]
        out_ref[...] = jnp.broadcast_to(sent, out_ref.shape)


def home_kernel(rows, nodes, own_ref, *refs):
    out_ref, shift_ref, base_ref, swing_ref = refs[-4:]
    count = lax.axis_size("tile")
    rotated = (lax.axis_index("tile") + count - rows // 2) % count
    group, row_index = rotated // rows, rotated % rows
    grid = None
    for step in range(1, SECTIONS):
        part = section_grid(refs[step - 1][...], step, rows)
        grid = part if grid is None else jnp.where(group == step, part, grid)
    row_shift = own_row(relax(grid, rows, nodes), row_index)
    row_shift = jnp.where(group == 0, 0.0, row_shift)
    shift_ref[0, :, :] = row_shift[:, :nodes]
    shift_ref[1, :, :] = pltpu.roll(row_shift, LANES - nodes, 1)[:, :nodes]
    base_ref[...], swing_ref[...] = kernels_of(row_shift, 0, nodes, nodes)

    def one(index, slot):
        here = columns(index)
        out_ref[:, here] = warp_indexed(own_ref[:, here], base_ref, swing_ref, index, nodes)

    looped(nodes, one)


def shards(sections, valid_mask, coarse_offsets):
    count = lax.axis_size("tile")
    rows = count // SECTIONS
    nodes = valid_mask.shape[1]
    place = lambda group, row: (group * rows + row + rows // 2) % count
    group = (lax.axis_index("tile") + count - rows // 2) % count // rows
    moved = lambda value, pairs: lax.ppermute(value, "tile", pairs)

    def swapped(source, lower, begin, cols, after=None):
        start = (begin + jnp.where(group == lower, nodes // 2, 0)) * PATCH
        half = lax.dynamic_slice_in_dim(source, start, cols * PATCH, 1)
        if after is not None:
            half, after = lax.optimization_barrier((half, after))
        ends = [(place(lower, i), place(lower + 1, i)) for i in range(rows)]
        return half, moved(half, ends + [(d, s) for s, d in ends])

    half = nodes // 2
    chunk = half // 2
    heads, chunks = zip(*(swapped(sections, 0, k * chunk, chunk) for k in range(2)))
    source, heads = lax.optimization_barrier((sections, heads))
    others = {1: [(k * chunk, chunk, chunks[k]) for k in range(2)]}

    vmem = pl.BlockSpec(memory_space=pltpu.VMEM)
    smem = pl.BlockSpec(memory_space=pltpu.SMEM)
    params = pltpu.CompilerParams(vmem_limit_bytes=16 * 2**20)
    gathered = []
    for step in range(1, SECTIONS):
        extra = gathered[-1:]
        for begin, cols, other in others[step]:
            sent = pl.pallas_call(
                functools.partial(chain_kernel, step, rows, nodes, begin, cols),
                out_shape=jax.ShapeDtypeStruct((count, LANES), f32),
                in_specs=[smem] + [vmem] * (3 + len(extra)),
                out_specs=vmem,
                scratch_shapes=[
                    pltpu.VMEM((cols, THIRD, 2 * LANES), f32),
                    pltpu.VMEM((GROUP, 2, 8 * THIRD, LANES), f32),
                    pltpu.VMEM((4, cols, 8, LANES), f32),
                    pltpu.VMEM((2, cols, LANES), f32),
                    pltpu.VMEM((cols, PATCH, PATCH), bf16),
                    pltpu.VMEM((2 * cols, LANES), f32),
                    pltpu.VMEM((2 * cols, LANES), f32),
                ],
                compiler_params=params,
                name=f"chain{step}_{begin}",
            )(coarse_offsets, sections, other, valid_mask, *extra)
            extra = [sent]
            waiting = max(others) + 1
            if waiting < SECTIONS:
                others[waiting] = [(0, half, swapped(source, waiting - 1, 0, half, sent)[1])]
        gathered.append(lax.all_to_all(sent, "tile", 0, 0, tiled=True))
    return pl.pallas_call(
        functools.partial(home_kernel, rows, nodes),
        out_shape=(
            jax.ShapeDtypeStruct(sections.shape, bf16),
            jax.ShapeDtypeStruct((2, 1, nodes), f32),
        ),
        in_specs=[vmem] * SECTIONS,
        out_specs=(vmem, vmem),
        scratch_shapes=[pltpu.VMEM((2 * nodes, LANES), f32)] * 2,
        compiler_params=params,
        name="home",
    )(sections, *gathered)


def solution(mesh):
    placed = (P(("parts", "tile"), None), P(("parts", "tile"), None), P("parts", None))
    return jax.shard_map(
        shards,
        mesh=mesh,
        in_specs=placed,
        out_specs=(P(("parts", "tile"), None), P(None, ("parts", "tile"), None)),
        check_vma=False,
    )
```

```python
import functools
import math

import jax
import jax.numpy as jnp
from jax import lax
from jax.experimental import pallas as pl
from jax.experimental.pallas import tpu as pltpu
from jax.sharding import PartitionSpec as P

SECTIONS = 4
PATCH = 128
HALF = 4
SWEEPS = 3
LANES = 128
WIDTH = 2 * HALF + 1
MASK_LANE = 64
GROUP = 8
THIRD = WIDTH // 3
SPAN = PATCH // 2 + 16

sharpness = 12.0
anchor_weight = 2.0
f32 = jnp.float32
bf16 = jnp.bfloat16


def iota(shape, axis):
    return lax.broadcasted_iota(jnp.int32, shape, axis)


def split(value):
    high = value.astype(bf16)
    return high, (value - high.astype(f32)).astype(bf16)


def dot(lhs, rhs):
    return jnp.dot(lhs, rhs, preferred_element_type=f32)


def dot_t(lhs, rhs):
    return lax.dot_general(lhs, rhs, (((1,), (1,)), ((), ())), preferred_element_type=f32)


def sine(x):
    y = x * x
    acc = jnp.full_like(x, 1.0 / math.factorial(13))
    for order in (11, 9, 7, 5, 3, 1):
        acc = (-1.0 if order % 4 == 3 else 1.0) / math.factorial(order) + y * acc
    return x * acc


def cosine(x):
    y = x * x
    acc = jnp.full_like(x, 1.0 / math.factorial(12))
    for order in (10, 8, 6, 4, 2, 0):
        acc = (-1.0 if order % 4 == 2 else 1.0) / math.factorial(order) + y * acc
    return acc


def total(value):
    return jnp.sum(jnp.sum(value, axis=0, keepdims=True), axis=1, keepdims=True)


def tile_sum(value):
    parts = [value[r : r + 8] for r in range(0, value.shape[0], 8)]
    while len(parts) > 1:
        parts = [x + y for x, y in zip(parts[::2], parts[1::2])]
    return parts[0]


def sign_tile(shape):
    return (1 - 2 * ((iota(shape, 0) + iota(shape, 1)) % 2)).astype(f32)


def section_grid(gathered, step, rows):
    count = gathered.shape[0]
    out = None
    for group in (step - 1, step):
        start = (group * rows + rows // 2) % count
        part = jnp.concatenate([gathered[start:], gathered[:start]], axis=0)[:rows]
        out = part if out is None else out + part
    return jnp.concatenate([out, jnp.zeros((8 - rows % 8, LANES), f32)], axis=0)


def relax(grid, rows, nodes):
    shape = grid.shape
    row, lane = iota(shape, 0), iota(shape, 1)
    col = lane % nodes
    valid = (row < rows) & (lane < 2 * nodes)
    mask = pltpu.roll(grid, LANES - MASK_LANE, 1)
    one = lambda cond: jnp.where(cond, 1.0, 0.0)
    count = one(row > 0) + one(row < rows - 1) + one(col > 0) + one(col < nodes - 1)
    weight = anchor_weight * mask
    inverse = 1.0 / jnp.where(valid, weight + count, 1.0)
    pulled = weight * grid
    shift = jnp.where(valid, grid * mask, 0.0)
    for _ in range(SWEEPS):
        near = pltpu.roll(shift, 1, 0) + pltpu.roll(shift, shape[0] - 1, 0)
        near += jnp.where(col > 0, pltpu.roll(shift, 1, 1), 0.0)
        near += jnp.where(col < nodes - 1, pltpu.roll(shift, LANES - 1, 1), 0.0)
        shift = jnp.where(valid, (pulled + near) * inverse, 0.0)
    return shift


def own_row(shift, index):
    return jnp.sum(jnp.where(iota(shift.shape, 0) == index, shift, 0.0), axis=0, keepdims=True)


def kernels_of(row_shift, first, cols, nodes):
    shape = (2 * cols, LANES)
    sub, lane = iota(shape, 0), iota(shape, 1)
    is_row = sub < cols
    target = first + jnp.where(is_row, sub, sub - cols + nodes)
    shift = jnp.sum(jnp.where(lane == target, row_shift, 0.0), axis=1, keepdims=True)
    shift = jnp.broadcast_to(shift, shape)
    whole = jnp.floor(shift + 0.5)
    part = shift - whole
    steps = jnp.where(is_row, -lane, lane).astype(f32) + whole
    steps = steps - LANES * jnp.floor((steps + LANES // 2) * (1.0 / LANES))
    sign = lambda n: 1.0 - 2.0 * (n - 2.0 * jnp.floor(n * 0.5))
    swing = sine(part * math.pi)
    angle = (steps + part) * (math.pi / LANES)
    centre = (steps == 0.0) & (jnp.abs(part) < 1e-20)
    below = jnp.where(centre, 1.0, sine(angle))
    base = swing * sign(steps) * (1.0 / LANES) * cosine(angle) / below
    return jnp.where(centre, 1.0, base), swing * sign(whole)


def circulant(row):
    return pltpu.roll(jnp.broadcast_to(row, (PATCH, LANES)), 0, 1, stride=1, stride_axis=0)


def warp(patch, row_base, col_base, row_swing, col_swing, nyquist):
    row_high, row_low = split(circulant(row_base))
    col_high, col_low = split(circulant(col_base))
    inner = dot(
        jnp.concatenate([patch, patch], axis=1), jnp.concatenate([col_high, col_low], axis=0)
    )
    in_high, in_low = split(inner)
    upper = jnp.concatenate([in_high, in_low], axis=1)
    lower = jnp.concatenate([in_high, jnp.zeros_like(in_low)], axis=1)
    out = dot(
        jnp.concatenate([row_high, row_low], axis=1), jnp.concatenate([upper, lower], axis=0)
    )
    out = out[:, :LANES] + out[:, LANES:]
    factor = row_swing * col_swing * nyquist * (1.0 / (PATCH * PATCH))
    return out - factor * sign_tile((PATCH, LANES))


def lag_layout(shape, axis):
    spot = (iota(shape, axis) + 16) % (2 * LANES)
    return spot // SPAN, 8 - spot % SPAN


def correlate(own, prev, level, column_offset, band_ref):
    own32, prev32 = own.astype(f32), prev.astype(f32)
    half = PATCH // 2
    left, right = [], []
    for i in range(THIRD):
        amount = (PATCH + HALF - i - column_offset) % PATCH
        turned = pltpu.roll(own32, amount, 1)
        low = jnp.concatenate([turned[PATCH - 8 :], turned[: half + 8]], axis=0)
        high = jnp.concatenate([turned[half - 8 :], turned[:8]], axis=0)
        left.append(jnp.concatenate([low, high], axis=1).astype(bf16))
    for j in range(THIRD):
        turned = pltpu.roll(prev32, THIRD * j, 1).astype(bf16) if j else prev
        right.append(jnp.concatenate([turned[:half], turned[half:]], axis=1))
        right.append(jnp.zeros((SPAN - half, 2 * LANES), bf16))
    right.append(jnp.zeros((2 * LANES - THIRD * SPAN, 2 * LANES), bf16))
    product = dot_t(jnp.concatenate(left, axis=0), jnp.concatenate(right, axis=0))
    spot = iota((8, 2 * LANES), 1) % SPAN
    base = jnp.where((spot < half) & (iota((8, 2 * LANES), 1) < THIRD * SPAN), level * (2.0 * LANES), 0.0)
    unused = lag_layout(spot.shape, 1)[1] >= 8 - iota(spot.shape, 0)
    for i in range(THIRD):
        tile = lambda r: product[i * SPAN + 8 * r : i * SPAN + 8 * r + 8]
        band = None
        for k in range(3):
            kept = tile(k)
            for m in range(1, 4 if k == 0 else 3):
                kept = jnp.where(spot >= 8 * k + 24 * m - 16, tile(k + 3 * m), kept)
            kept = kept - base
            kept = pltpu.roll(kept, 2 * LANES - 8 * k, 1) if k else kept
            band = kept if band is None else band + kept
        band = jnp.where(unused, 0.0, band)
        for side in range(2):
            band_ref[side, 8 * i : 8 * i + 8, :] = band[:, side * LANES : (side + 1) * LANES]
    out = None
    for row in range(8):
        part = jnp.concatenate(
            [band_ref[side, pl.ds(row, THIRD, stride=8), :] for side in range(2)], axis=1
        )
        part = pltpu.roll(part, 2 * LANES - row, 1) if row else part
        out = part if out is None else out + part
    back = lambda lanes: pltpu.roll(out, 2 * LANES - lanes, 1)
    _, row_lag = lag_layout(out.shape, 1)
    return out + back(24) + back(48) + jnp.where(row_lag > 0, back(72), 0.0)


def moments(values, corner):
    values = values.astype(f32) - corner
    return tile_sum(values), tile_sum(values * values)


def looped(count, one):
    width = min(GROUP, count)

    def body(turn, carry):
        for k in range(width):
            one(turn * width + k, k)
        return carry

    if count == width:
        body(0, 0)
    else:
        lax.fori_loop(0, count // width, body, 0)


def columns(index):
    start = index * PATCH
    return pl.ds(start if isinstance(start, int) else pl.multiple_of(start, PATCH), PATCH)


def warp_indexed(patch, base_ref, swing_ref, index, cols):
    nyquist = total(tile_sum(patch.astype(f32)) * sign_tile((8, LANES)))
    return warp(
        patch,
        base_ref[pl.ds(index, 1), :],
        base_ref[pl.ds(index + cols, 1), :],
        swing_ref[pl.ds(index, 1), :],
        swing_ref[pl.ds(index + cols, 1), :],
        nyquist,
    ).astype(bf16)


def chain_kernel(step, rows, nodes, offsets_ref, own_ref, other_ref, mask_ref, *refs):
    out_ref, score_ref, band_ref, sums_ref, corner_ref, prev_ref, base_ref, swing_ref = refs[-8:]
    cols = nodes // 2
    count = lax.axis_size("tile")
    rotated = (lax.axis_index("tile") + count - rows // 2) % count
    group, row_index = rotated // rows, rotated % rows
    is_upper = group == step
    first = jnp.where(is_upper, cols, 0)

    @pl.when(is_upper | (group == step - 1) | (step == 1))
    def _():
        row_offset, col_offset = offsets_ref[step, 0], offsets_ref[step, 1]
        area = float(PATCH * PATCH)

        if step > 1:
            row_shift = own_row(relax(section_grid(refs[0][...], step - 1, rows), rows, nodes), row_index)
            base_ref[...], swing_ref[...] = kernels_of(row_shift, first, cols, nodes)

            def warp_one(index, slot):
                patch = jnp.where(is_upper, other_ref[:, columns(index)], own_ref[:, columns(index)])
                prev_ref[index] = warp_indexed(patch, base_ref, swing_ref, index, cols)

            looped(cols, warp_one)

        def one(index, slot):
            other = other_ref[:, columns(index)]
            own = jnp.where(is_upper, own_ref[:, columns(index + cols)], other)
            if step > 1:
                prev = prev_ref[index]
            else:
                prev = jnp.where(is_upper, other, own_ref[:, columns(index)])
            own_corner, prev_corner = (x[0:1, 0:1].astype(f32) for x in (own, prev))
            corner_ref[0, pl.ds(index, 1), :] = jnp.broadcast_to(own_corner, (1, LANES))
            corner_ref[1, pl.ds(index, 1), :] = jnp.broadcast_to(prev_corner, (1, LANES))
            sums = moments(own, own_corner) + moments(prev, prev_corner)
            for k, value in enumerate(sums):
                sums_ref[k, pl.ds(index, 1)] = value[None]
            level = own_corner * prev_corner
            score_ref[pl.ds(index, 1)] = correlate(own, prev, level, col_offset, band_ref.at[slot])[None]

        looped(cols, one)
        reduce = lambda value: jnp.sum(jnp.sum(value, axis=1), axis=1, keepdims=True)
        own_sum, own_square, prev_sum, prev_square = (reduce(sums_ref[k]) * (1.0 / area) for k in range(4))
        spread = jnp.sqrt(
            (jnp.maximum(own_square - own_sum * own_sum, 0.0) + 1e-5)
            * (jnp.maximum(prev_square - prev_sum * prev_sum, 0.0) + 1e-5)
        )
        scale = sharpness / area / spread
        level = corner_ref[0] * prev_sum + corner_ref[1] * own_sum + own_sum * prev_sum
        shape = (cols, THIRD, 2 * LANES)
        third, row_lag = lag_layout(shape, 2)
        col_lag = iota(shape, 1) + THIRD * third - HALF + col_offset
        inside = (jnp.abs(row_lag - row_offset) <= HALF) & (third < THIRD)
        level = jnp.concatenate([level, level], axis=1) * area
        scale = jnp.broadcast_to(scale, (cols, 2 * LANES))
        score = (score_ref[...] - level[:, None, :]) * scale[:, None, :]
        weights = jnp.where(inside, jnp.exp(jnp.where(inside, score, 0.0)), 0.0)
        inverse = 1.0 / reduce(weights)
        flow_row = reduce(weights * row_lag.astype(f32)) * inverse
        flow_col = reduce(weights * col_lag.astype(f32)) * inverse
        shape = (cols, LANES)
        node, lane = iota(shape, 0) + first, iota(shape, 1)
        sent = jnp.where(lane == node, flow_row, jnp.where(lane == node + nodes, flow_col, 0.0))
        sent = jnp.sum(sent, axis=0, keepdims=True)
        masks = mask_ref[...].astype(f32)
        gap = jnp.zeros((1, MASK_LANE - 2 * nodes), f32)
        masks = jnp.concatenate([gap, jnp.zeros((1, 2 * nodes), f32), masks, masks, gap], axis=1)
        sent = sent + jnp.where(is_upper, masks, 0.0)
        out_ref[...] = jnp.broadcast_to(sent, out_ref.shape)


def home_kernel(rows, nodes, own_ref, *refs):
    out_ref, shift_ref, base_ref, swing_ref = refs[-4:]
    count = lax.axis_size("tile")
    rotated = (lax.axis_index("tile") + count - rows // 2) % count
    group, row_index = rotated // rows, rotated % rows
    grid = None
    for step in range(1, SECTIONS):
        part = section_grid(refs[step - 1][...], step, rows)
        grid = part if grid is None else jnp.where(group == step, part, grid)
    row_shift = own_row(relax(grid, rows, nodes), row_index)
    row_shift = jnp.where(group == 0, 0.0, row_shift)
    shift_ref[0, :, :] = row_shift[:, :nodes]
    shift_ref[1, :, :] = pltpu.roll(row_shift, LANES - nodes, 1)[:, :nodes]
    base_ref[...], swing_ref[...] = kernels_of(row_shift, 0, nodes, nodes)

    def one(index, slot):
        here = columns(index)
        out_ref[:, here] = warp_indexed(own_ref[:, here], base_ref, swing_ref, index, nodes)

    looped(nodes, one)


def shards(sections, valid_mask, coarse_offsets):
    count = lax.axis_size("tile")
    rows = count // SECTIONS
    nodes = valid_mask.shape[1]
    place = lambda group, row: (group * rows + row + rows // 2) % count
    group = (lax.axis_index("tile") + count - rows // 2) % count // rows
    moved = lambda value, pairs: lax.ppermute(value, "tile", pairs)

    def swapped(lower, after=None):
        start = jnp.where(group == lower, half * PATCH, 0)
        sent = lax.dynamic_slice_in_dim(sections, start, half * PATCH, 1)
        if after is not None:
            sent, after = lax.optimization_barrier((sent, after))
        ends = [(place(lower, i), place(lower + 1, i)) for i in range(rows)]
        return moved(sent, ends + [(d, s) for s, d in ends])

    half = nodes // 2
    others = [swapped(0), swapped(1)]

    vmem = pl.BlockSpec(memory_space=pltpu.VMEM)
    smem = pl.BlockSpec(memory_space=pltpu.SMEM)
    params = pltpu.CompilerParams(vmem_limit_bytes=16 * 2**20)
    gathered = []
    for step in range(1, SECTIONS):
        extra = gathered[-1:]
        sent = pl.pallas_call(
            functools.partial(chain_kernel, step, rows, nodes),
            out_shape=jax.ShapeDtypeStruct((count, LANES), f32),
            in_specs=[smem] + [vmem] * (3 + len(extra)),
            out_specs=vmem,
            scratch_shapes=[
                pltpu.VMEM((half, THIRD, 2 * LANES), f32),
                pltpu.VMEM((GROUP, 2, 8 * THIRD, LANES), f32),
                pltpu.VMEM((4, half, 8, LANES), f32),
                pltpu.VMEM((2, half, LANES), f32),
                pltpu.VMEM((half, PATCH, PATCH), bf16),
                pltpu.VMEM((2 * half, LANES), f32),
                pltpu.VMEM((2 * half, LANES), f32),
            ],
            compiler_params=params,
            name=f"chain{step}",
        )(coarse_offsets, sections, others[step - 1], valid_mask, *extra)
        gathered.append(lax.all_to_all(sent, "tile", 0, 0, tiled=True))
        if step + 1 < SECTIONS - 1:
            others.append(swapped(step + 1, sent))
    return pl.pallas_call(
        functools.partial(home_kernel, rows, nodes),
        out_shape=(
            jax.ShapeDtypeStruct(sections.shape, bf16),
            jax.ShapeDtypeStruct((2, 1, nodes), f32),
        ),
        in_specs=[vmem] * SECTIONS,
        out_specs=(vmem, vmem),
        scratch_shapes=[pltpu.VMEM((2 * nodes, LANES), f32)] * 2,
        compiler_params=params,
        name="home",
    )(sections, *gathered)


def solution(mesh):
    placed = (P(("parts", "tile"), None), P(("parts", "tile"), None), P("parts", None))
    return jax.shard_map(
        shards,
        mesh=mesh,
        in_specs=placed,
        out_specs=(P(("parts", "tile"), None), P(None, ("parts", "tile"), None)),
        check_vma=False,
    )
```

```python
import functools
import math

import jax
import jax.numpy as jnp
from jax import lax
from jax.experimental import pallas as pl
from jax.experimental.pallas import tpu as pltpu
from jax.sharding import PartitionSpec as P

SECTIONS = 4
PATCH = 128
HALF = 4
SWEEPS = 3
LANES = 128
WIDTH = 2 * HALF + 1
MASK_LANE = 64
GROUP = 16
THIRD = WIDTH // 3
SPAN = PATCH // 2 + 16

sharpness = 12.0
anchor_weight = 2.0
f32 = jnp.float32
bf16 = jnp.bfloat16


def iota(shape, axis):
    return lax.broadcasted_iota(jnp.int32, shape, axis)


def split(value):
    high = value.astype(bf16)
    return high, (value - high.astype(f32)).astype(bf16)


def dot(lhs, rhs):
    return jnp.dot(lhs, rhs, preferred_element_type=f32)


def dot_t(lhs, rhs):
    return lax.dot_general(lhs, rhs, (((1,), (1,)), ((), ())), preferred_element_type=f32)


def sine(x):
    y = x * x
    acc = jnp.full_like(x, 1.0 / math.factorial(13))
    for order in (11, 9, 7, 5, 3, 1):
        acc = (-1.0 if order % 4 == 3 else 1.0) / math.factorial(order) + y * acc
    return x * acc


def cosine(x):
    y = x * x
    acc = jnp.full_like(x, 1.0 / math.factorial(12))
    for order in (10, 8, 6, 4, 2, 0):
        acc = (-1.0 if order % 4 == 2 else 1.0) / math.factorial(order) + y * acc
    return acc


def total(value):
    return jnp.sum(jnp.sum(value, axis=0, keepdims=True), axis=1, keepdims=True)


def tile_sum(value):
    parts = [value[r : r + 8] for r in range(0, value.shape[0], 8)]
    while len(parts) > 1:
        parts = [x + y for x, y in zip(parts[::2], parts[1::2])]
    return parts[0]


def sign_tile(shape):
    return (1 - 2 * ((iota(shape, 0) + iota(shape, 1)) % 2)).astype(f32)


def section_grid(gathered, step, rows):
    count = gathered.shape[0]
    out = None
    for group in (step - 1, step):
        start = (group * rows + rows // 2) % count
        part = jnp.concatenate([gathered[start:], gathered[:start]], axis=0)[:rows]
        out = part if out is None else out + part
    return jnp.concatenate([out, jnp.zeros((8 - rows % 8, LANES), f32)], axis=0)


def relax(grid, rows, nodes):
    shape = grid.shape
    row, lane = iota(shape, 0), iota(shape, 1)
    col = lane % nodes
    valid = (row < rows) & (lane < 2 * nodes)
    mask = pltpu.roll(grid, LANES - MASK_LANE, 1)
    one = lambda cond: jnp.where(cond, 1.0, 0.0)
    count = one(row > 0) + one(row < rows - 1) + one(col > 0) + one(col < nodes - 1)
    weight = anchor_weight * mask
    inverse = 1.0 / jnp.where(valid, weight + count, 1.0)
    pulled = weight * grid
    shift = jnp.where(valid, grid * mask, 0.0)
    for _ in range(SWEEPS):
        near = pltpu.roll(shift, 1, 0) + pltpu.roll(shift, shape[0] - 1, 0)
        near += jnp.where(col > 0, pltpu.roll(shift, 1, 1), 0.0)
        near += jnp.where(col < nodes - 1, pltpu.roll(shift, LANES - 1, 1), 0.0)
        shift = jnp.where(valid, (pulled + near) * inverse, 0.0)
    return shift


def own_row(shift, index):
    return jnp.sum(jnp.where(iota(shift.shape, 0) == index, shift, 0.0), axis=0, keepdims=True)


def kernels_of(row_shift, first, cols, nodes):
    shape = (2 * cols, LANES)
    sub, lane = iota(shape, 0), iota(shape, 1)
    is_row = sub < cols
    target = first + jnp.where(is_row, sub, sub - cols + nodes)
    shift = jnp.sum(jnp.where(lane == target, row_shift, 0.0), axis=1, keepdims=True)
    shift = jnp.broadcast_to(shift, shape)
    whole = jnp.floor(shift + 0.5)
    part = shift - whole
    steps = jnp.where(is_row, -lane, lane).astype(f32) + whole
    steps = steps - LANES * jnp.floor((steps + LANES // 2) * (1.0 / LANES))
    sign = lambda n: 1.0 - 2.0 * (n - 2.0 * jnp.floor(n * 0.5))
    swing = sine(part * math.pi)
    angle = (steps + part) * (math.pi / LANES)
    centre = (steps == 0.0) & (jnp.abs(part) < 1e-20)
    below = jnp.where(centre, 1.0, sine(angle))
    base = swing * sign(steps) * (1.0 / LANES) * cosine(angle) / below
    return jnp.where(centre, 1.0, base), swing * sign(whole)


def circulant(row):
    return pltpu.roll(jnp.broadcast_to(row, (PATCH, LANES)), 0, 1, stride=1, stride_axis=0)


def warp(patch, row_base, col_base, row_swing, col_swing, nyquist):
    row_high, row_low = split(circulant(row_base))
    col_high, col_low = split(circulant(col_base))
    inner = dot(
        jnp.concatenate([patch, patch], axis=1), jnp.concatenate([col_high, col_low], axis=0)
    )
    in_high, in_low = split(inner)
    upper = jnp.concatenate([in_high, in_low], axis=1)
    lower = jnp.concatenate([in_high, jnp.zeros_like(in_low)], axis=1)
    out = dot(
        jnp.concatenate([row_high, row_low], axis=1), jnp.concatenate([upper, lower], axis=0)
    )
    out = out[:, :LANES] + out[:, LANES:]
    factor = row_swing * col_swing * nyquist * (1.0 / (PATCH * PATCH))
    return out - factor * sign_tile((PATCH, LANES))


def lag_layout(shape, axis):
    spot = (iota(shape, axis) + 16) % (2 * LANES)
    return spot // SPAN, 8 - spot % SPAN


def correlate(own, prev, level, column_offset, band_ref):
    own32, prev32 = own.astype(f32), prev.astype(f32)
    half = PATCH // 2
    left, right = [], []
    for i in range(THIRD):
        amount = (PATCH + HALF - i - column_offset) % PATCH
        turned = pltpu.roll(own32, amount, 1)
        low = jnp.concatenate([turned[PATCH - 8 :], turned[: half + 8]], axis=0)
        high = jnp.concatenate([turned[half - 8 :], turned[:8]], axis=0)
        left.append(jnp.concatenate([low, high], axis=1).astype(bf16))
    for j in range(THIRD):
        turned = pltpu.roll(prev32, THIRD * j, 1).astype(bf16) if j else prev
        right.append(jnp.concatenate([turned[:half], turned[half:]], axis=1))
        right.append(jnp.zeros((SPAN - half, 2 * LANES), bf16))
    right.append(jnp.zeros((2 * LANES - THIRD * SPAN, 2 * LANES), bf16))
    product = dot_t(jnp.concatenate(left, axis=0), jnp.concatenate(right, axis=0))
    spot = iota((8, 2 * LANES), 1) % SPAN
    base = jnp.where((spot < half) & (iota((8, 2 * LANES), 1) < THIRD * SPAN), level * (2.0 * LANES), 0.0)
    unused = lag_layout(spot.shape, 1)[1] >= 8 - iota(spot.shape, 0)
    for i in range(THIRD):
        tile = lambda r: product[i * SPAN + 8 * r : i * SPAN + 8 * r + 8]
        band = None
        for k in range(3):
            kept = tile(k)
            for m in range(1, 4 if k == 0 else 3):
                kept = jnp.where(spot >= 8 * k + 24 * m - 16, tile(k + 3 * m), kept)
            kept = kept - base
            kept = pltpu.roll(kept, 2 * LANES - 8 * k, 1) if k else kept
            band = kept if band is None else band + kept
        band = jnp.where(unused, 0.0, band)
        for side in range(2):
            band_ref[side, 8 * i : 8 * i + 8, :] = band[:, side * LANES : (side + 1) * LANES]
    out = None
    for row in range(8):
        part = jnp.concatenate(
            [band_ref[side, pl.ds(row, THIRD, stride=8), :] for side in range(2)], axis=1
        )
        part = pltpu.roll(part, 2 * LANES - row, 1) if row else part
        out = part if out is None else out + part
    back = lambda lanes: pltpu.roll(out, 2 * LANES - lanes, 1)
    _, row_lag = lag_layout(out.shape, 1)
    return out + back(24) + back(48) + jnp.where(row_lag > 0, back(72), 0.0)


def moments(values, corner):
    values = values.astype(f32) - corner
    return tile_sum(values), tile_sum(values * values)


def looped(count, one):
    width = min(GROUP, count)

    def body(turn, carry):
        for k in range(width):
            one(turn * width + k, k)
        return carry

    if count == width:
        body(0, 0)
    else:
        lax.fori_loop(0, count // width, body, 0)


def columns(index):
    start = index * PATCH
    return pl.ds(start if isinstance(start, int) else pl.multiple_of(start, PATCH), PATCH)


def warp_indexed(patch, base_ref, swing_ref, index, cols):
    nyquist = total(tile_sum(patch.astype(f32)) * sign_tile((8, LANES)))
    return warp(
        patch,
        base_ref[pl.ds(index, 1), :],
        base_ref[pl.ds(index + cols, 1), :],
        swing_ref[pl.ds(index, 1), :],
        swing_ref[pl.ds(index + cols, 1), :],
        nyquist,
    ).astype(bf16)


def chain_kernel(step, rows, nodes, offsets_ref, own_ref, other_ref, mask_ref, *refs):
    out_ref, score_ref, band_ref, sums_ref, corner_ref, prev_ref, base_ref, swing_ref = refs[-8:]
    cols = nodes // 2
    count = lax.axis_size("tile")
    rotated = (lax.axis_index("tile") + count - rows // 2) % count
    group, row_index = rotated // rows, rotated % rows
    is_upper = group == step
    first = jnp.where(is_upper, cols, 0)

    @pl.when(is_upper | (group == step - 1) | (step == 1))
    def _():
        row_offset, col_offset = offsets_ref[step, 0], offsets_ref[step, 1]
        area = float(PATCH * PATCH)

        if step > 1:
            row_shift = own_row(relax(section_grid(refs[0][...], step - 1, rows), rows, nodes), row_index)
            base_ref[...], swing_ref[...] = kernels_of(row_shift, first, cols, nodes)

        def stage(index, slot):
            patch = jnp.where(is_upper, other_ref[:, columns(index)], own_ref[:, columns(index)])
            if step > 1:
                patch = warp_indexed(patch, base_ref, swing_ref, index, cols)
            prev_ref[index] = patch

        looped(cols, stage)

        def one(index, slot):
            own = jnp.where(is_upper, own_ref[:, columns(index + cols)], other_ref[:, columns(index)])
            prev = prev_ref[index]
            own_corner, prev_corner = (x[0:1, 0:1].astype(f32) for x in (own, prev))
            corner_ref[0, pl.ds(index, 1), :] = jnp.broadcast_to(own_corner, (1, LANES))
            corner_ref[1, pl.ds(index, 1), :] = jnp.broadcast_to(prev_corner, (1, LANES))
            sums = moments(own, own_corner) + moments(prev, prev_corner)
            for k, value in enumerate(sums):
                sums_ref[k, pl.ds(index, 1)] = value[None]
            level = own_corner * prev_corner
            score_ref[pl.ds(index, 1)] = correlate(own, prev, level, col_offset, band_ref.at[slot])[None]

        looped(cols, one)
        reduce = lambda value: jnp.sum(jnp.sum(value, axis=1), axis=1, keepdims=True)
        own_sum, own_square, prev_sum, prev_square = (reduce(sums_ref[k]) * (1.0 / area) for k in range(4))
        spread = jnp.sqrt(
            (jnp.maximum(own_square - own_sum * own_sum, 0.0) + 1e-5)
            * (jnp.maximum(prev_square - prev_sum * prev_sum, 0.0) + 1e-5)
        )
        scale = sharpness / area / spread
        level = corner_ref[0] * prev_sum + corner_ref[1] * own_sum + own_sum * prev_sum
        shape = (cols, THIRD, 2 * LANES)
        third, row_lag = lag_layout(shape, 2)
        col_lag = iota(shape, 1) + THIRD * third - HALF + col_offset
        inside = (jnp.abs(row_lag - row_offset) <= HALF) & (third < THIRD)
        level = jnp.concatenate([level, level], axis=1) * area
        scale = jnp.broadcast_to(scale, (cols, 2 * LANES))
        score = (score_ref[...] - level[:, None, :]) * scale[:, None, :]
        weights = jnp.where(inside, jnp.exp(jnp.where(inside, score, 0.0)), 0.0)
        inverse = 1.0 / reduce(weights)
        flow_row = reduce(weights * row_lag.astype(f32)) * inverse
        flow_col = reduce(weights * col_lag.astype(f32)) * inverse
        shape = (cols, LANES)
        node, lane = iota(shape, 0) + first, iota(shape, 1)
        sent = jnp.where(lane == node, flow_row, jnp.where(lane == node + nodes, flow_col, 0.0))
        sent = jnp.sum(sent, axis=0, keepdims=True)
        masks = mask_ref[...].astype(f32)
        gap = jnp.zeros((1, MASK_LANE - 2 * nodes), f32)
        masks = jnp.concatenate([gap, jnp.zeros((1, 2 * nodes), f32), masks, masks, gap], axis=1)
        sent = sent + jnp.where(is_upper, masks, 0.0)
        out_ref[...] = jnp.broadcast_to(sent, out_ref.shape)


def home_kernel(rows, nodes, own_ref, *refs):
    out_ref, shift_ref, base_ref, swing_ref = refs[-4:]
    count = lax.axis_size("tile")
    rotated = (lax.axis_index("tile") + count - rows // 2) % count
    group, row_index = rotated // rows, rotated % rows
    grid = None
    for step in range(1, SECTIONS):
        part = section_grid(refs[step - 1][...], step, rows)
        grid = part if grid is None else jnp.where(group == step, part, grid)
    row_shift = own_row(relax(grid, rows, nodes), row_index)
    row_shift = jnp.where(group == 0, 0.0, row_shift)
    shift_ref[0, :, :] = row_shift[:, :nodes]
    shift_ref[1, :, :] = pltpu.roll(row_shift, LANES - nodes, 1)[:, :nodes]
    base_ref[...], swing_ref[...] = kernels_of(row_shift, 0, nodes, nodes)

    def one(index, slot):
        here = columns(index)
        out_ref[:, here] = warp_indexed(own_ref[:, here], base_ref, swing_ref, index, nodes)

    looped(nodes, one)


def shards(sections, valid_mask, coarse_offsets):
    count = lax.axis_size("tile")
    rows = count // SECTIONS
    nodes = valid_mask.shape[1]
    place = lambda group, row: (group * rows + row + rows // 2) % count
    group = (lax.axis_index("tile") + count - rows // 2) % count // rows
    moved = lambda value, pairs: lax.ppermute(value, "tile", pairs)

    def swapped(lower, after=None):
        start = jnp.where(group == lower, half * PATCH, 0)
        sent = lax.dynamic_slice_in_dim(sections, start, half * PATCH, 1)
        if after is not None:
            sent, after = lax.optimization_barrier((sent, after))
        ends = [(place(lower, i), place(lower + 1, i)) for i in range(rows)]
        return moved(sent, ends + [(d, s) for s, d in ends])

    half = nodes // 2
    others = [swapped(0), swapped(1)]

    vmem = pl.BlockSpec(memory_space=pltpu.VMEM)
    smem = pl.BlockSpec(memory_space=pltpu.SMEM)
    params = pltpu.CompilerParams(vmem_limit_bytes=16 * 2**20)
    gathered = []
    for step in range(1, SECTIONS):
        extra = gathered[-1:]
        sent = pl.pallas_call(
            functools.partial(chain_kernel, step, rows, nodes),
            out_shape=jax.ShapeDtypeStruct((count, LANES), f32),
            in_specs=[smem] + [vmem] * (3 + len(extra)),
            out_specs=vmem,
            scratch_shapes=[
                pltpu.VMEM((half, THIRD, 2 * LANES), f32),
                pltpu.VMEM((half, 2, 8 * THIRD, LANES), f32),
                pltpu.VMEM((4, half, 8, LANES), f32),
                pltpu.VMEM((2, half, LANES), f32),
                pltpu.VMEM((half, PATCH, PATCH), bf16),
                pltpu.VMEM((2 * half, LANES), f32),
                pltpu.VMEM((2 * half, LANES), f32),
            ],
            compiler_params=params,
            name=f"chain{step}",
        )(coarse_offsets, sections, others[step - 1], valid_mask, *extra)
        gathered.append(lax.all_to_all(sent, "tile", 0, 0, tiled=True))
        if step + 1 < SECTIONS - 1:
            others.append(swapped(step + 1, sent))
    return pl.pallas_call(
        functools.partial(home_kernel, rows, nodes),
        out_shape=(
            jax.ShapeDtypeStruct(sections.shape, bf16),
            jax.ShapeDtypeStruct((2, 1, nodes), f32),
        ),
        in_specs=[vmem] * SECTIONS,
        out_specs=(vmem, vmem),
        scratch_shapes=[pltpu.VMEM((2 * nodes, LANES), f32)] * 2,
        compiler_params=params,
        name="home",
    )(sections, *gathered)


def solution(mesh):
    placed = (P(("parts", "tile"), None), P(("parts", "tile"), None), P("parts", None))
    return jax.shard_map(
        shards,
        mesh=mesh,
        in_specs=placed,
        out_specs=(P(("parts", "tile"), None), P(None, ("parts", "tile"), None)),
        check_vma=False,
    )
```

```python
import functools
import math

import jax
import jax.numpy as jnp
from jax import lax
from jax.experimental import pallas as pl
from jax.experimental.pallas import tpu as pltpu
from jax.sharding import PartitionSpec as P

SECTIONS = 4
PATCH = 128
HALF = 4
SWEEPS = 3
LANES = 128
WIDTH = 2 * HALF + 1
MASK_LANE = 64
GROUP = 16
THIRD = WIDTH // 3
SPAN = PATCH // 2 + 16

sharpness = 12.0
anchor_weight = 2.0
f32 = jnp.float32
bf16 = jnp.bfloat16


def iota(shape, axis):
    return lax.broadcasted_iota(jnp.int32, shape, axis)


def split(value):
    high = value.astype(bf16)
    return high, (value - high.astype(f32)).astype(bf16)


def dot(lhs, rhs):
    return jnp.dot(lhs, rhs, preferred_element_type=f32)


def dot_t(lhs, rhs):
    return lax.dot_general(lhs, rhs, (((1,), (1,)), ((), ())), preferred_element_type=f32)


def sine(x):
    y = x * x
    acc = jnp.full_like(x, 1.0 / math.factorial(13))
    for order in (11, 9, 7, 5, 3, 1):
        acc = (-1.0 if order % 4 == 3 else 1.0) / math.factorial(order) + y * acc
    return x * acc


def cosine(x):
    y = x * x
    acc = jnp.full_like(x, 1.0 / math.factorial(12))
    for order in (10, 8, 6, 4, 2, 0):
        acc = (-1.0 if order % 4 == 2 else 1.0) / math.factorial(order) + y * acc
    return acc


def total(value):
    return jnp.sum(jnp.sum(value, axis=0, keepdims=True), axis=1, keepdims=True)


def tile_sum(value):
    parts = [value[r : r + 8] for r in range(0, value.shape[0], 8)]
    while len(parts) > 1:
        parts = [x + y for x, y in zip(parts[::2], parts[1::2])]
    return parts[0]


def sign_tile(shape):
    return (1 - 2 * ((iota(shape, 0) + iota(shape, 1)) % 2)).astype(f32)


def section_grid(gathered, step, rows):
    count = gathered.shape[0]
    out = None
    for group in (step - 1, step):
        start = (group * rows + rows // 2) % count
        part = jnp.concatenate([gathered[start:], gathered[:start]], axis=0)[:rows]
        out = part if out is None else out + part
    return jnp.concatenate([out, jnp.zeros((8 - rows % 8, LANES), f32)], axis=0)


def relax(grid, rows, nodes):
    shape = grid.shape
    row, lane = iota(shape, 0), iota(shape, 1)
    col = lane % nodes
    valid = (row < rows) & (lane < 2 * nodes)
    mask = pltpu.roll(grid, LANES - MASK_LANE, 1)
    one = lambda cond: jnp.where(cond, 1.0, 0.0)
    count = one(row > 0) + one(row < rows - 1) + one(col > 0) + one(col < nodes - 1)
    weight = anchor_weight * mask
    inverse = 1.0 / jnp.where(valid, weight + count, 1.0)
    pulled = weight * grid
    shift = jnp.where(valid, grid * mask, 0.0)
    for _ in range(SWEEPS):
        near = pltpu.roll(shift, 1, 0) + pltpu.roll(shift, shape[0] - 1, 0)
        near += jnp.where(col > 0, pltpu.roll(shift, 1, 1), 0.0)
        near += jnp.where(col < nodes - 1, pltpu.roll(shift, LANES - 1, 1), 0.0)
        shift = jnp.where(valid, (pulled + near) * inverse, 0.0)
    return shift


def own_row(shift, index):
    return jnp.sum(jnp.where(iota(shift.shape, 0) == index, shift, 0.0), axis=0, keepdims=True)


def kernels_of(row_shift, first, cols, nodes):
    shape = (2 * cols, LANES)
    sub, lane = iota(shape, 0), iota(shape, 1)
    is_row = sub < cols
    target = first + jnp.where(is_row, sub, sub - cols + nodes)
    shift = jnp.sum(jnp.where(lane == target, row_shift, 0.0), axis=1, keepdims=True)
    shift = jnp.broadcast_to(shift, shape)
    whole = jnp.floor(shift + 0.5)
    part = shift - whole
    steps = jnp.where(is_row, -lane, lane).astype(f32) + whole
    steps = steps - LANES * jnp.floor((steps + LANES // 2) * (1.0 / LANES))
    sign = lambda n: 1.0 - 2.0 * (n - 2.0 * jnp.floor(n * 0.5))
    swing = sine(part * math.pi)
    angle = (steps + part) * (math.pi / LANES)
    centre = (steps == 0.0) & (jnp.abs(part) < 1e-20)
    below = jnp.where(centre, 1.0, sine(angle))
    base = swing * sign(steps) * (1.0 / LANES) * cosine(angle) / below
    return jnp.where(centre, 1.0, base), swing * sign(whole)


def circulant(row):
    return pltpu.roll(jnp.broadcast_to(row, (PATCH, LANES)), 0, 1, stride=1, stride_axis=0)


def warp(patch, row_base, col_base, row_swing, col_swing, nyquist):
    row_high, row_low = split(circulant(row_base))
    col_high, col_low = split(circulant(col_base))
    inner = dot(
        jnp.concatenate([patch, patch], axis=1), jnp.concatenate([col_high, col_low], axis=0)
    )
    in_high, in_low = split(inner)
    upper = jnp.concatenate([in_high, in_low], axis=1)
    lower = jnp.concatenate([in_high, jnp.zeros_like(in_low)], axis=1)
    out = dot(
        jnp.concatenate([row_high, row_low], axis=1), jnp.concatenate([upper, lower], axis=0)
    )
    out = out[:, :LANES] + out[:, LANES:]
    factor = row_swing * col_swing * nyquist * (1.0 / (PATCH * PATCH))
    return out - factor * sign_tile((PATCH, LANES))


def lag_layout(shape, axis):
    spot = (iota(shape, axis) + 16) % (2 * LANES)
    return spot // SPAN, 8 - spot % SPAN


def correlate(own, prev, level, column_offset, band_ref):
    own32, prev32 = own.astype(f32), prev.astype(f32)
    half = PATCH // 2
    left, right = [], []
    for i in range(THIRD):
        amount = (PATCH + HALF - i - column_offset) % PATCH
        turned = pltpu.roll(own32, amount, 1)
        low = jnp.concatenate([turned[PATCH - 8 :], turned[: half + 8]], axis=0)
        high = jnp.concatenate([turned[half - 8 :], turned[:8]], axis=0)
        left.append(jnp.concatenate([low, high], axis=1).astype(bf16))
    for j in range(THIRD):
        turned = pltpu.roll(prev32, THIRD * j, 1).astype(bf16) if j else prev
        right.append(jnp.concatenate([turned[:half], turned[half:]], axis=1))
        right.append(jnp.zeros((SPAN - half, 2 * LANES), bf16))
    right.append(jnp.zeros((2 * LANES - THIRD * SPAN, 2 * LANES), bf16))
    product = dot_t(jnp.concatenate(left, axis=0), jnp.concatenate(right, axis=0))
    spot = iota((8, 2 * LANES), 1) % SPAN
    base = jnp.where((spot < half) & (iota((8, 2 * LANES), 1) < THIRD * SPAN), level * (2.0 * LANES), 0.0)
    unused = lag_layout(spot.shape, 1)[1] >= 8 - iota(spot.shape, 0)
    for i in range(THIRD):
        tile = lambda r: product[i * SPAN + 8 * r : i * SPAN + 8 * r + 8]
        band = None
        for k in range(3):
            kept = tile(k)
            for m in range(1, 4 if k == 0 else 3):
                kept = jnp.where(spot >= 8 * k + 24 * m - 16, tile(k + 3 * m), kept)
            kept = kept - base
            kept = pltpu.roll(kept, 2 * LANES - 8 * k, 1) if k else kept
            band = kept if band is None else band + kept
        band = jnp.where(unused, 0.0, band)
        for side in range(2):
            band_ref[side, 8 * i : 8 * i + 8, :] = band[:, side * LANES : (side + 1) * LANES]
    out = None
    for row in range(8):
        part = jnp.concatenate(
            [band_ref[side, pl.ds(row, THIRD, stride=8), :] for side in range(2)], axis=1
        )
        part = pltpu.roll(part, 2 * LANES - row, 1) if row else part
        out = part if out is None else out + part
    back = lambda lanes: pltpu.roll(out, 2 * LANES - lanes, 1)
    _, row_lag = lag_layout(out.shape, 1)
    return out + back(24) + back(48) + jnp.where(row_lag > 0, back(72), 0.0)


def moments(values, corner):
    values = values.astype(f32) - corner
    return tile_sum(values), tile_sum(values * values)


def looped(count, one):
    width = min(GROUP, count)

    def body(turn, carry):
        for k in range(width):
            one(turn * width + k, k)
        return carry

    if count == width:
        body(0, 0)
    else:
        lax.fori_loop(0, count // width, body, 0)


def columns(index):
    start = index * PATCH
    return pl.ds(start if isinstance(start, int) else pl.multiple_of(start, PATCH), PATCH)


def warp_indexed(patch, base_ref, swing_ref, index, cols):
    nyquist = total(tile_sum(patch.astype(f32)) * sign_tile((8, LANES)))
    return warp(
        patch,
        base_ref[pl.ds(index, 1), :],
        base_ref[pl.ds(index + cols, 1), :],
        swing_ref[pl.ds(index, 1), :],
        swing_ref[pl.ds(index + cols, 1), :],
        nyquist,
    ).astype(bf16)


def chain_kernel(step, rows, nodes, offsets_ref, own_ref, other_ref, mask_ref, *refs):
    out_ref, score_ref, band_ref, sums_ref, corner_ref, prev_ref, base_ref, swing_ref = refs[-8:]
    cols = nodes // 2
    count = lax.axis_size("tile")
    rotated = (lax.axis_index("tile") + count - rows // 2) % count
    group, row_index = rotated // rows, rotated % rows
    is_upper = group == step
    first = jnp.where(is_upper, cols, 0)

    @pl.when(is_upper | (group == step - 1) | (step == 1))
    def _():
        row_offset, col_offset = offsets_ref[step, 0], offsets_ref[step, 1]
        area = float(PATCH * PATCH)

        if step > 1:
            row_shift = own_row(relax(section_grid(refs[0][...], step - 1, rows), rows, nodes), row_index)
            base_ref[...], swing_ref[...] = kernels_of(row_shift, first, cols, nodes)

        def stage(index, slot):
            patch = jnp.where(is_upper, other_ref[:, columns(index)], own_ref[:, columns(index)])
            if step > 1:
                patch = warp_indexed(patch, base_ref, swing_ref, index, cols)
            prev_ref[index] = patch

        looped(cols, stage)

        def one(index, slot):
            own = jnp.where(is_upper, own_ref[:, columns(index + cols)], other_ref[:, columns(index)])
            prev = prev_ref[index]
            own_corner, prev_corner = (x[0:1, 0:1].astype(f32) for x in (own, prev))
            corner_ref[0, pl.ds(index, 1), :] = jnp.broadcast_to(own_corner, (1, LANES))
            corner_ref[1, pl.ds(index, 1), :] = jnp.broadcast_to(prev_corner, (1, LANES))
            sums = moments(own, own_corner) + moments(prev, prev_corner)
            for k, value in enumerate(sums):
                sums_ref[k, pl.ds(index, 1)] = value[None]
            level = own_corner * prev_corner
            score_ref[pl.ds(index, 1)] = correlate(own, prev, level, col_offset, band_ref.at[slot])[None]

        looped(cols, one)
        reduce = lambda value: jnp.sum(jnp.sum(value, axis=1), axis=1, keepdims=True)
        own_sum, own_square, prev_sum, prev_square = (reduce(sums_ref[k]) * (1.0 / area) for k in range(4))
        spread = jnp.sqrt(
            (jnp.maximum(own_square - own_sum * own_sum, 0.0) + 1e-5)
            * (jnp.maximum(prev_square - prev_sum * prev_sum, 0.0) + 1e-5)
        )
        scale = sharpness / area / spread
        level = corner_ref[0] * prev_sum + corner_ref[1] * own_sum + own_sum * prev_sum
        shape = (cols, THIRD, 2 * LANES)
        third, row_lag = lag_layout(shape, 2)
        col_lag = iota(shape, 1) + THIRD * third - HALF + col_offset
        inside = (jnp.abs(row_lag - row_offset) <= HALF) & (third < THIRD)
        level = jnp.concatenate([level, level], axis=1) * area
        scale = jnp.broadcast_to(scale, (cols, 2 * LANES))
        score = (score_ref[...] - level[:, None, :]) * scale[:, None, :]
        weights = jnp.where(inside, jnp.exp(jnp.where(inside, score, 0.0)), 0.0)
        inverse = 1.0 / reduce(weights)
        flow_row = reduce(weights * row_lag.astype(f32)) * inverse
        flow_col = reduce(weights * col_lag.astype(f32)) * inverse
        shape = (cols, LANES)
        node, lane = iota(shape, 0) + first, iota(shape, 1)
        sent = jnp.where(lane == node, flow_row, jnp.where(lane == node + nodes, flow_col, 0.0))
        sent = jnp.sum(sent, axis=0, keepdims=True)
        masks = mask_ref[...].astype(f32)
        gap = jnp.zeros((1, MASK_LANE - 2 * nodes), f32)
        masks = jnp.concatenate([gap, jnp.zeros((1, 2 * nodes), f32), masks, masks, gap], axis=1)
        sent = sent + jnp.where(is_upper, masks, 0.0)
        out_ref[...] = jnp.broadcast_to(sent, out_ref.shape)


def home_kernel(rows, nodes, own_ref, *refs):
    out_ref, shift_ref, base_ref, swing_ref = refs[-4:]
    count = lax.axis_size("tile")
    rotated = (lax.axis_index("tile") + count - rows // 2) % count
    group, row_index = rotated // rows, rotated % rows
    grid = None
    for step in range(1, SECTIONS):
        part = section_grid(refs[step - 1][...], step, rows)
        grid = part if grid is None else jnp.where(group == step, part, grid)
    row_shift = own_row(relax(grid, rows, nodes), row_index)
    row_shift = jnp.where(group == 0, 0.0, row_shift)
    shift_ref[0, :, :] = row_shift[:, :nodes]
    shift_ref[1, :, :] = pltpu.roll(row_shift, LANES - nodes, 1)[:, :nodes]
    base_ref[...], swing_ref[...] = kernels_of(row_shift, 0, nodes, nodes)

    def one(index, slot):
        here = columns(index)
        out_ref[:, here] = warp_indexed(own_ref[:, here], base_ref, swing_ref, index, nodes)

    looped(nodes, one)


def shards(sections, valid_mask, coarse_offsets):
    count = lax.axis_size("tile")
    rows = count // SECTIONS
    nodes = valid_mask.shape[1]
    place = lambda group, row: (group * rows + row + rows // 2) % count
    group = (lax.axis_index("tile") + count - rows // 2) % count // rows
    moved = lambda value, pairs: lax.ppermute(value, "tile", pairs)

    def half_of(source, lower):
        start = jnp.where(group == lower, half * PATCH, 0)
        return lax.dynamic_slice_in_dim(source, start, half * PATCH, 1)

    def swapped(sent, lower):
        ends = [(place(lower, i), place(lower + 1, i)) for i in range(rows)]
        return moved(sent, ends + [(d, s) for s, d in ends])

    half = nodes // 2
    first_half = half_of(sections, 0)
    source, first_half = lax.optimization_barrier((sections, first_half))
    others = [swapped(first_half, 0), swapped(half_of(source, 1), 1)]

    vmem = pl.BlockSpec(memory_space=pltpu.VMEM)
    params = pltpu.CompilerParams(vmem_limit_bytes=16 * 2**20)
    gathered = []
    for step in range(1, SECTIONS):
        extra = gathered[-1:]
        sent = pl.pallas_call(
            functools.partial(chain_kernel, step, rows, nodes),
            out_shape=jax.ShapeDtypeStruct((count, LANES), f32),
            in_specs=[vmem] * (4 + len(extra)),
            out_specs=vmem,
            scratch_shapes=[
                pltpu.VMEM((half, THIRD, 2 * LANES), f32),
                pltpu.VMEM((half, 2, 8 * THIRD, LANES), f32),
                pltpu.VMEM((4, half, 8, LANES), f32),
                pltpu.VMEM((2, half, LANES), f32),
                pltpu.VMEM((half, PATCH, PATCH), bf16),
                pltpu.VMEM((2 * half, LANES), f32),
                pltpu.VMEM((2 * half, LANES), f32),
            ],
            compiler_params=params,
            name=f"chain{step}",
        )(coarse_offsets, sections, others[step - 1], valid_mask, *extra)
        gathered.append(lax.all_to_all(sent, "tile", 0, 0, tiled=True))
        if step + 1 < SECTIONS - 1:
            later, sent = lax.optimization_barrier((half_of(source, step + 1), sent))
            others.append(swapped(later, step + 1))
    return pl.pallas_call(
        functools.partial(home_kernel, rows, nodes),
        out_shape=(
            jax.ShapeDtypeStruct(sections.shape, bf16),
            jax.ShapeDtypeStruct((2, 1, nodes), f32),
        ),
        in_specs=[vmem] * SECTIONS,
        out_specs=(vmem, vmem),
        scratch_shapes=[pltpu.VMEM((2 * nodes, LANES), f32)] * 2,
        compiler_params=params,
        name="home",
    )(sections, *gathered)


def solution(mesh):
    placed = (P(("parts", "tile"), None), P(("parts", "tile"), None), P("parts", None))
    return jax.shard_map(
        shards,
        mesh=mesh,
        in_specs=placed,
        out_specs=(P(("parts", "tile"), None), P(None, ("parts", "tile"), None)),
        check_vma=False,
    )
```

```python
import functools
import math

import jax
import jax.numpy as jnp
from jax import lax
from jax.experimental import pallas as pl
from jax.experimental.pallas import tpu as pltpu
from jax.sharding import PartitionSpec as P

SECTIONS = 4
PATCH = 128
HALF = 4
SWEEPS = 3
LANES = 128
WIDTH = 2 * HALF + 1
MASK_LANE = 64
GROUP = 16
THIRD = WIDTH // 3
SPAN = PATCH // 2 + 16

sharpness = 12.0
anchor_weight = 2.0
f32 = jnp.float32
bf16 = jnp.bfloat16


def iota(shape, axis):
    return lax.broadcasted_iota(jnp.int32, shape, axis)


def split(value):
    high = value.astype(bf16)
    return high, (value - high.astype(f32)).astype(bf16)


def dot(lhs, rhs):
    return jnp.dot(lhs, rhs, preferred_element_type=f32)


def dot_t(lhs, rhs):
    return lax.dot_general(lhs, rhs, (((1,), (1,)), ((), ())), preferred_element_type=f32)


def sine(x):
    y = x * x
    acc = jnp.full_like(x, 1.0 / math.factorial(13))
    for order in (11, 9, 7, 5, 3, 1):
        acc = (-1.0 if order % 4 == 3 else 1.0) / math.factorial(order) + y * acc
    return x * acc


def cosine(x):
    y = x * x
    acc = jnp.full_like(x, 1.0 / math.factorial(12))
    for order in (10, 8, 6, 4, 2, 0):
        acc = (-1.0 if order % 4 == 2 else 1.0) / math.factorial(order) + y * acc
    return acc


def total(value):
    return jnp.sum(jnp.sum(value, axis=0, keepdims=True), axis=1, keepdims=True)


def tile_sum(value):
    parts = [value[r : r + 8] for r in range(0, value.shape[0], 8)]
    while len(parts) > 1:
        parts = [x + y for x, y in zip(parts[::2], parts[1::2])]
    return parts[0]


def sign_tile(shape):
    return (1 - 2 * ((iota(shape, 0) + iota(shape, 1)) % 2)).astype(f32)


def section_grid(gathered, step, rows):
    count = gathered.shape[0]
    out = None
    for group in (step - 1, step):
        start = (group * rows + rows // 2) % count
        part = jnp.concatenate([gathered[start:], gathered[:start]], axis=0)[:rows]
        out = part if out is None else out + part
    return jnp.concatenate([out, jnp.zeros((8 - rows % 8, LANES), f32)], axis=0)


def relax(grid, rows, nodes):
    shape = grid.shape
    row, lane = iota(shape, 0), iota(shape, 1)
    col = lane % nodes
    valid = (row < rows) & (lane < 2 * nodes)
    mask = pltpu.roll(grid, LANES - MASK_LANE, 1)
    one = lambda cond: jnp.where(cond, 1.0, 0.0)
    count = one(row > 0) + one(row < rows - 1) + one(col > 0) + one(col < nodes - 1)
    weight = anchor_weight * mask
    inverse = 1.0 / jnp.where(valid, weight + count, 1.0)
    pulled = weight * grid
    shift = jnp.where(valid, grid * mask, 0.0)
    for _ in range(SWEEPS):
        near = pltpu.roll(shift, 1, 0) + pltpu.roll(shift, shape[0] - 1, 0)
        near += jnp.where(col > 0, pltpu.roll(shift, 1, 1), 0.0)
        near += jnp.where(col < nodes - 1, pltpu.roll(shift, LANES - 1, 1), 0.0)
        shift = jnp.where(valid, (pulled + near) * inverse, 0.0)
    return shift


def own_row(shift, index):
    return jnp.sum(jnp.where(iota(shift.shape, 0) == index, shift, 0.0), axis=0, keepdims=True)


def kernels_of(row_shift, first, cols, nodes):
    shape = (2 * cols, LANES)
    sub, lane = iota(shape, 0), iota(shape, 1)
    is_row = sub < cols
    target = first + jnp.where(is_row, sub, sub - cols + nodes)
    shift = jnp.sum(jnp.where(lane == target, row_shift, 0.0), axis=1, keepdims=True)
    shift = jnp.broadcast_to(shift, shape)
    whole = jnp.floor(shift + 0.5)
    part = shift - whole
    steps = jnp.where(is_row, -lane, lane).astype(f32) + whole
    steps = steps - LANES * jnp.floor((steps + LANES // 2) * (1.0 / LANES))
    sign = lambda n: 1.0 - 2.0 * (n - 2.0 * jnp.floor(n * 0.5))
    swing = sine(part * math.pi)
    angle = (steps + part) * (math.pi / LANES)
    centre = (steps == 0.0) & (jnp.abs(part) < 1e-20)
    below = jnp.where(centre, 1.0, sine(angle))
    base = swing * sign(steps) * (1.0 / LANES) * cosine(angle) / below
    return jnp.where(centre, 1.0, base), swing * sign(whole)


def circulant(row):
    return pltpu.roll(jnp.broadcast_to(row, (PATCH, LANES)), 0, 1, stride=1, stride_axis=0)


def warp(patch, row_base, col_base, row_swing, col_swing, nyquist):
    row_high, row_low = split(circulant(row_base))
    col_high, col_low = split(circulant(col_base))
    inner = dot(
        jnp.concatenate([patch, patch], axis=1), jnp.concatenate([col_high, col_low], axis=0)
    )
    in_high, in_low = split(inner)
    upper = jnp.concatenate([in_high, in_low], axis=1)
    lower = jnp.concatenate([in_high, jnp.zeros_like(in_low)], axis=1)
    out = dot(
        jnp.concatenate([row_high, row_low], axis=1), jnp.concatenate([upper, lower], axis=0)
    )
    out = out[:, :LANES] + out[:, LANES:]
    factor = row_swing * col_swing * nyquist * (1.0 / (PATCH * PATCH))
    return out - factor * sign_tile((PATCH, LANES))


def lag_layout(shape, axis):
    spot = (iota(shape, axis) + 16) % (2 * LANES)
    return spot // SPAN, 8 - spot % SPAN


def correlate(own, prev, level, column_offset, put):
    own32, prev32 = own.astype(f32), prev.astype(f32)
    half = PATCH // 2
    left, right = [], []
    for i in range(THIRD):
        amount = (PATCH + HALF - i - column_offset) % PATCH
        turned = pltpu.roll(own32, amount, 1)
        low = jnp.concatenate([turned[PATCH - 8 :], turned[: half + 8]], axis=0)
        high = jnp.concatenate([turned[half - 8 :], turned[:8]], axis=0)
        left.append(jnp.concatenate([low, high], axis=1).astype(bf16))
    for j in range(THIRD):
        turned = pltpu.roll(prev32, THIRD * j, 1).astype(bf16) if j else prev
        right.append(jnp.concatenate([turned[:half], turned[half:]], axis=1))
        right.append(jnp.zeros((SPAN - half, 2 * LANES), bf16))
    right.append(jnp.zeros((2 * LANES - THIRD * SPAN, 2 * LANES), bf16))
    product = dot_t(jnp.concatenate(left, axis=0), jnp.concatenate(right, axis=0))
    spot = iota((8, 2 * LANES), 1) % SPAN
    base = jnp.where((spot < half) & (iota((8, 2 * LANES), 1) < THIRD * SPAN), level * (2.0 * LANES), 0.0)
    unused = lag_layout(spot.shape, 1)[1] >= 8 - iota(spot.shape, 0)
    for i in range(THIRD):
        tile = lambda r: product[i * SPAN + 8 * r : i * SPAN + 8 * r + 8]
        band = None
        for k in range(3):
            kept = tile(k)
            for m in range(1, 4 if k == 0 else 3):
                kept = jnp.where(spot >= 8 * k + 24 * m - 16, tile(k + 3 * m), kept)
            kept = kept - base
            kept = pltpu.roll(kept, 2 * LANES - 8 * k, 1) if k else kept
            band = kept if band is None else band + kept
        band = jnp.where(unused, 0.0, band)
        put(i, band)


def band_sum(band_ref, first, cols):
    out = None
    for row in range(8):
        rows = pl.ds(first + row, cols, stride=8)
        part = jnp.concatenate([band_ref[side, rows, :] for side in range(2)], axis=1)
        part = pltpu.roll(part, 2 * LANES - row, 1) if row else part
        out = part if out is None else out + part
    back = lambda lanes: pltpu.roll(out, 2 * LANES - lanes, 1)
    _, row_lag = lag_layout(out.shape, 1)
    return out + back(24) + back(48) + jnp.where(row_lag > 0, back(72), 0.0)


def moments(values, corner):
    values = values.astype(f32) - corner
    return tile_sum(values), tile_sum(values * values)


def looped(count, one):
    width = min(GROUP, count)

    def body(turn, carry):
        for k in range(width):
            one(turn * width + k, k)
        return carry

    if count == width:
        body(0, 0)
    else:
        lax.fori_loop(0, count // width, body, 0)


def rows_of(index):
    return pl.ds(index * 8 if isinstance(index, int) else pl.multiple_of(index * 8, 8), 8)


def columns(index):
    start = index * PATCH
    return pl.ds(start if isinstance(start, int) else pl.multiple_of(start, PATCH), PATCH)


def warp_indexed(patch, base_ref, swing_ref, index, cols):
    nyquist = total(tile_sum(patch.astype(f32)) * sign_tile((8, LANES)))
    return warp(
        patch,
        base_ref[pl.ds(index, 1), :],
        base_ref[pl.ds(index + cols, 1), :],
        swing_ref[pl.ds(index, 1), :],
        swing_ref[pl.ds(index + cols, 1), :],
        nyquist,
    ).astype(bf16)


def chain_kernel(step, rows, nodes, offsets_ref, own_ref, other_ref, mask_ref, *refs):
    out_ref, band_ref, sums_ref, corner_ref, prev_ref, base_ref, swing_ref = refs[-7:]
    cols = nodes // 2
    count = lax.axis_size("tile")
    rotated = (lax.axis_index("tile") + count - rows // 2) % count
    group, row_index = rotated // rows, rotated % rows
    is_upper = group == step
    first = jnp.where(is_upper, cols, 0)

    @pl.when(is_upper | (group == step - 1) | (step == 1))
    def _():
        row_offset, col_offset = offsets_ref[step, 0], offsets_ref[step, 1]
        area = float(PATCH * PATCH)

        if step > 1:
            row_shift = own_row(relax(section_grid(refs[0][...], step - 1, rows), rows, nodes), row_index)
            base_ref[...], swing_ref[...] = kernels_of(row_shift, first, cols, nodes)

        def stage(index, slot):
            patch = jnp.where(is_upper, other_ref[:, columns(index)], own_ref[:, columns(index)])
            if step > 1:
                patch = warp_indexed(patch, base_ref, swing_ref, index, cols)
            prev_ref[index] = patch

        looped(cols, stage)

        def one(index, slot):
            own = jnp.where(is_upper, own_ref[:, columns(index + cols)], other_ref[:, columns(index)])
            prev = prev_ref[index]
            own_corner, prev_corner = (x[0:1, 0:1].astype(f32) for x in (own, prev))
            corner_ref[0, pl.ds(index, 1), :] = jnp.broadcast_to(own_corner, (1, LANES))
            corner_ref[1, pl.ds(index, 1), :] = jnp.broadcast_to(prev_corner, (1, LANES))
            sums = moments(own, own_corner) + moments(prev, prev_corner)
            for k, value in enumerate(sums):
                sums_ref[k, rows_of(index), :] = value
            level = own_corner * prev_corner

            def put(third, band):
                for side in range(2):
                    band_ref[side, rows_of(third * cols + index), :] = band[:, side * LANES : (side + 1) * LANES]

            correlate(own, prev, level, col_offset, put)

        looped(cols, one)
        reduce = lambda value: jnp.sum(value, axis=1, keepdims=True)
        mean = lambda k: reduce(
            functools.reduce(jnp.add, [sums_ref[k, pl.ds(row, cols, stride=8), :] for row in range(8)])
        ) * (1.0 / area)
        own_sum, own_square, prev_sum, prev_square = (mean(k) for k in range(4))
        spread = jnp.sqrt(
            (jnp.maximum(own_square - own_sum * own_sum, 0.0) + 1e-5)
            * (jnp.maximum(prev_square - prev_sum * prev_sum, 0.0) + 1e-5)
        )
        scale = sharpness / area / spread
        level = corner_ref[0] * prev_sum + corner_ref[1] * own_sum + own_sum * prev_sum
        level = jnp.concatenate([level, level], axis=1) * area
        third, row_lag = lag_layout((cols, 2 * LANES), 1)
        inside = (jnp.abs(row_lag - row_offset) <= HALF) & (third < THIRD)
        weight = row_moment = col_moment = 0.0
        for i in range(THIRD):
            score = (band_sum(band_ref, 8 * cols * i, cols) - level) * scale
            weights = jnp.where(inside, jnp.exp(jnp.where(inside, score, 0.0)), 0.0)
            col_lag = i + THIRD * third - HALF + col_offset
            weight = weight + weights
            row_moment = row_moment + weights * row_lag.astype(f32)
            col_moment = col_moment + weights * col_lag.astype(f32)
        inverse = 1.0 / reduce(weight)
        flow_row = reduce(row_moment) * inverse
        flow_col = reduce(col_moment) * inverse
        shape = (cols, LANES)
        node, lane = iota(shape, 0) + first, iota(shape, 1)
        sent = jnp.where(lane == node, flow_row, jnp.where(lane == node + nodes, flow_col, 0.0))
        sent = jnp.sum(sent, axis=0, keepdims=True)
        masks = mask_ref[...].astype(f32)
        gap = jnp.zeros((1, MASK_LANE - 2 * nodes), f32)
        masks = jnp.concatenate([gap, jnp.zeros((1, 2 * nodes), f32), masks, masks, gap], axis=1)
        sent = sent + jnp.where(is_upper, masks, 0.0)
        out_ref[...] = jnp.broadcast_to(sent, out_ref.shape)


def home_kernel(rows, nodes, own_ref, *refs):
    out_ref, shift_ref, base_ref, swing_ref = refs[-4:]
    count = lax.axis_size("tile")
    rotated = (lax.axis_index("tile") + count - rows // 2) % count
    group, row_index = rotated // rows, rotated % rows
    grid = None
    for step in range(1, SECTIONS):
        part = section_grid(refs[step - 1][...], step, rows)
        grid = part if grid is None else jnp.where(group == step, part, grid)
    row_shift = own_row(relax(grid, rows, nodes), row_index)
    row_shift = jnp.where(group == 0, 0.0, row_shift)
    shift_ref[0, :, :] = row_shift[:, :nodes]
    shift_ref[1, :, :] = pltpu.roll(row_shift, LANES - nodes, 1)[:, :nodes]
    base_ref[...], swing_ref[...] = kernels_of(row_shift, 0, nodes, nodes)

    def one(index, slot):
        here = columns(index)
        out_ref[:, here] = warp_indexed(own_ref[:, here], base_ref, swing_ref, index, nodes)

    looped(nodes, one)


def shards(sections, valid_mask, coarse_offsets):
    count = lax.axis_size("tile")
    rows = count // SECTIONS
    nodes = valid_mask.shape[1]
    place = lambda group, row: (group * rows + row + rows // 2) % count
    group = (lax.axis_index("tile") + count - rows // 2) % count // rows
    moved = lambda value, pairs: lax.ppermute(value, "tile", pairs)

    def half_of(source, lower):
        start = jnp.where(group == lower, half * PATCH, 0)
        return lax.dynamic_slice_in_dim(source, start, half * PATCH, 1)

    def swapped(sent, lower):
        ends = [(place(lower, i), place(lower + 1, i)) for i in range(rows)]
        return moved(sent, ends + [(d, s) for s, d in ends])

    half = nodes // 2
    first_half = half_of(sections, 0)
    source, first_half = lax.optimization_barrier((sections, first_half))
    others = [swapped(first_half, 0), swapped(half_of(source, 1), 1)]

    vmem = pl.BlockSpec(memory_space=pltpu.VMEM)
    params = pltpu.CompilerParams(vmem_limit_bytes=16 * 2**20)
    gathered = []
    for step in range(1, SECTIONS):
        extra = gathered[-1:]
        sent = pl.pallas_call(
            functools.partial(chain_kernel, step, rows, nodes),
            out_shape=jax.ShapeDtypeStruct((count, LANES), f32),
            in_specs=[vmem] * (4 + len(extra)),
            out_specs=vmem,
            scratch_shapes=[
                pltpu.VMEM((2, THIRD * half * 8, LANES), f32),
                pltpu.VMEM((4, half * 8, LANES), f32),
                pltpu.VMEM((2, half, LANES), f32),
                pltpu.VMEM((half, PATCH, PATCH), bf16),
                pltpu.VMEM((2 * half, LANES), f32),
                pltpu.VMEM((2 * half, LANES), f32),
            ],
            compiler_params=params,
            name=f"chain{step}",
        )(coarse_offsets, sections, others[step - 1], valid_mask, *extra)
        gathered.append(lax.all_to_all(sent, "tile", 0, 0, tiled=True))
        if step + 1 < SECTIONS - 1:
            later, sent = lax.optimization_barrier((half_of(source, step + 1), sent))
            others.append(swapped(later, step + 1))
    return pl.pallas_call(
        functools.partial(home_kernel, rows, nodes),
        out_shape=(
            jax.ShapeDtypeStruct(sections.shape, bf16),
            jax.ShapeDtypeStruct((2, 1, nodes), f32),
        ),
        in_specs=[vmem] * SECTIONS,
        out_specs=(vmem, vmem),
        scratch_shapes=[pltpu.VMEM((2 * nodes, LANES), f32)] * 2,
        compiler_params=params,
        name="home",
    )(sections, *gathered)


def solution(mesh):
    placed = (P(("parts", "tile"), None), P(("parts", "tile"), None), P("parts", None))
    return jax.shard_map(
        shards,
        mesh=mesh,
        in_specs=placed,
        out_specs=(P(("parts", "tile"), None), P(None, ("parts", "tile"), None)),
        check_vma=False,
    )
```

```python
import functools
import math

import jax
import jax.numpy as jnp
from jax import lax
from jax.experimental import pallas as pl
from jax.experimental.pallas import tpu as pltpu
from jax.sharding import PartitionSpec as P

SECTIONS = 4
PATCH = 128
HALF = 4
SWEEPS = 3
LANES = 128
WIDTH = 2 * HALF + 1
MASK_LANE = 64
GROUP = 16
THIRD = WIDTH // 3
SPAN = PATCH // 2 + 16

sharpness = 12.0
anchor_weight = 2.0
f32 = jnp.float32
bf16 = jnp.bfloat16


def iota(shape, axis):
    return lax.broadcasted_iota(jnp.int32, shape, axis)


def split(value):
    high = value.astype(bf16)
    return high, (value - high.astype(f32)).astype(bf16)


def dot(lhs, rhs):
    return jnp.dot(lhs, rhs, preferred_element_type=f32)


def dot_t(lhs, rhs):
    return lax.dot_general(lhs, rhs, (((1,), (1,)), ((), ())), preferred_element_type=f32)


def sine(x):
    y = x * x
    acc = jnp.full_like(x, 1.0 / math.factorial(13))
    for order in (11, 9, 7, 5, 3, 1):
        acc = (-1.0 if order % 4 == 3 else 1.0) / math.factorial(order) + y * acc
    return x * acc


def cosine(x):
    y = x * x
    acc = jnp.full_like(x, 1.0 / math.factorial(12))
    for order in (10, 8, 6, 4, 2, 0):
        acc = (-1.0 if order % 4 == 2 else 1.0) / math.factorial(order) + y * acc
    return acc


def total(value):
    return jnp.sum(jnp.sum(value, axis=0, keepdims=True), axis=1, keepdims=True)


def tile_sum(value):
    parts = [value[r : r + 8] for r in range(0, value.shape[0], 8)]
    while len(parts) > 1:
        parts = [x + y for x, y in zip(parts[::2], parts[1::2])]
    return parts[0]


def sign_tile(shape):
    return (1 - 2 * ((iota(shape, 0) + iota(shape, 1)) % 2)).astype(f32)


def section_grid(gathered, step, rows):
    count = gathered.shape[0]
    out = None
    for group in (step - 1, step):
        start = (group * rows + rows // 2) % count
        part = jnp.concatenate([gathered[start:], gathered[:start]], axis=0)[:rows]
        out = part if out is None else out + part
    return jnp.concatenate([out, jnp.zeros((8 - rows % 8, LANES), f32)], axis=0)


def relax(grid, rows, nodes):
    shape = grid.shape
    row, lane = iota(shape, 0), iota(shape, 1)
    col = lane % nodes
    valid = (row < rows) & (lane < 2 * nodes)
    mask = pltpu.roll(grid, LANES - MASK_LANE, 1)
    one = lambda cond: jnp.where(cond, 1.0, 0.0)
    count = one(row > 0) + one(row < rows - 1) + one(col > 0) + one(col < nodes - 1)
    weight = anchor_weight * mask
    inverse = 1.0 / jnp.where(valid, weight + count, 1.0)
    pulled = weight * grid
    shift = jnp.where(valid, grid * mask, 0.0)
    for _ in range(SWEEPS):
        near = pltpu.roll(shift, 1, 0) + pltpu.roll(shift, shape[0] - 1, 0)
        near += jnp.where(col > 0, pltpu.roll(shift, 1, 1), 0.0)
        near += jnp.where(col < nodes - 1, pltpu.roll(shift, LANES - 1, 1), 0.0)
        shift = jnp.where(valid, (pulled + near) * inverse, 0.0)
    return shift


def own_row(shift, index):
    return jnp.sum(jnp.where(iota(shift.shape, 0) == index, shift, 0.0), axis=0, keepdims=True)


def kernels_of(row_shift, first, cols, nodes):
    shape = (2 * cols, LANES)
    sub, lane = iota(shape, 0), iota(shape, 1)
    is_row = sub < cols
    target = first + jnp.where(is_row, sub, sub - cols + nodes)
    shift = jnp.sum(jnp.where(lane == target, row_shift, 0.0), axis=1, keepdims=True)
    shift = jnp.broadcast_to(shift, shape)
    whole = jnp.floor(shift + 0.5)
    part = shift - whole
    steps = jnp.where(is_row, -lane, lane).astype(f32) + whole
    steps = steps - LANES * jnp.floor((steps + LANES // 2) * (1.0 / LANES))
    sign = lambda n: 1.0 - 2.0 * (n - 2.0 * jnp.floor(n * 0.5))
    swing = sine(part * math.pi)
    angle = (steps + part) * (math.pi / LANES)
    centre = (steps == 0.0) & (jnp.abs(part) < 1e-20)
    below = jnp.where(centre, 1.0, sine(angle))
    base = swing * sign(steps) * (1.0 / LANES) * cosine(angle) / below
    return jnp.where(centre, 1.0, base), swing * sign(whole)


def circulant(row):
    return pltpu.roll(jnp.broadcast_to(row, (PATCH, LANES)), 0, 1, stride=1, stride_axis=0)


def warp(patch, row_base, col_base, row_swing, col_swing, nyquist):
    row_high, row_low = split(circulant(row_base))
    col_high, col_low = split(circulant(col_base))
    inner = dot(
        jnp.concatenate([patch, patch], axis=1), jnp.concatenate([col_high, col_low], axis=0)
    )
    in_high, in_low = split(inner)
    upper = jnp.concatenate([in_high, in_low], axis=1)
    lower = jnp.concatenate([in_high, jnp.zeros_like(in_low)], axis=1)
    out = dot(
        jnp.concatenate([row_high, row_low], axis=1), jnp.concatenate([upper, lower], axis=0)
    )
    out = out[:, :LANES] + out[:, LANES:]
    factor = row_swing * col_swing * nyquist * (1.0 / (PATCH * PATCH))
    return out - factor * sign_tile((PATCH, LANES))


def lag_layout(shape, axis):
    spot = (iota(shape, axis) + 16) % (2 * LANES)
    return spot // SPAN, 8 - spot % SPAN


def correlate(own, prev, level, column_offset, put):
    own32, prev32 = own.astype(f32), prev.astype(f32)
    half = PATCH // 2
    left, right = [], []
    for i in range(THIRD):
        amount = (PATCH + HALF - i - column_offset) % PATCH
        turned = pltpu.roll(own32, amount, 1)
        low = jnp.concatenate([turned[PATCH - 8 :], turned[: half + 8]], axis=0)
        high = jnp.concatenate([turned[half - 8 :], turned[:8]], axis=0)
        left.append(jnp.concatenate([low, high], axis=1).astype(bf16))
    for j in range(THIRD):
        turned = pltpu.roll(prev32, THIRD * j, 1).astype(bf16) if j else prev
        right.append(jnp.concatenate([turned[:half], turned[half:]], axis=1))
        right.append(jnp.zeros((SPAN - half, 2 * LANES), bf16))
    right.append(jnp.zeros((2 * LANES - THIRD * SPAN, 2 * LANES), bf16))
    product = dot_t(jnp.concatenate(left, axis=0), jnp.concatenate(right, axis=0))
    spot = iota((8, 2 * LANES), 1) % SPAN
    base = jnp.where((spot < half) & (iota((8, 2 * LANES), 1) < THIRD * SPAN), level * (2.0 * LANES), 0.0)
    unused = lag_layout(spot.shape, 1)[1] >= 8 - iota(spot.shape, 0)
    for i in range(THIRD):
        tile = lambda r: product[i * SPAN + 8 * r : i * SPAN + 8 * r + 8]
        band = None
        for k in range(3):
            kept = tile(k)
            for m in range(1, 4 if k == 0 else 3):
                kept = jnp.where(spot >= 8 * k + 24 * m - 16, tile(k + 3 * m), kept)
            kept = kept - base
            kept = pltpu.roll(kept, 2 * LANES - 8 * k, 1) if k else kept
            band = kept if band is None else band + kept
        band = jnp.where(unused, 0.0, band)
        put(i, band)


def band_sum(band_ref, first, cols):
    out = None
    for row in range(8):
        rows = pl.ds(first + row, cols, stride=8)
        part = jnp.concatenate([band_ref[side, rows, :] for side in range(2)], axis=1)
        part = pltpu.roll(part, 2 * LANES - row, 1) if row else part
        out = part if out is None else out + part
    back = lambda lanes: pltpu.roll(out, 2 * LANES - lanes, 1)
    _, row_lag = lag_layout(out.shape, 1)
    return out + back(24) + back(48) + jnp.where(row_lag > 0, back(72), 0.0)


def moments(values, corner):
    values = values.astype(f32) - corner
    return tile_sum(values), tile_sum(values * values)


def looped(count, one):
    width = min(GROUP, count)

    def body(turn, carry):
        for k in range(width):
            one(turn * width + k, k)
        return carry

    if count == width:
        body(0, 0)
    else:
        lax.fori_loop(0, count // width, body, 0)


def rows_of(index):
    return pl.ds(index * 8 if isinstance(index, int) else pl.multiple_of(index * 8, 8), 8)


def columns(index):
    start = index * PATCH
    return pl.ds(start if isinstance(start, int) else pl.multiple_of(start, PATCH), PATCH)


def warp_indexed(patch, base_ref, swing_ref, index, cols):
    nyquist = total(tile_sum(patch.astype(f32)) * sign_tile((8, LANES)))
    return warp(
        patch,
        base_ref[pl.ds(index, 1), :],
        base_ref[pl.ds(index + cols, 1), :],
        swing_ref[pl.ds(index, 1), :],
        swing_ref[pl.ds(index + cols, 1), :],
        nyquist,
    ).astype(bf16)


def chain_kernel(step, rows, nodes, offsets_ref, own_ref, other_ref, mask_ref, *refs):
    out_ref, band_ref, sums_ref, corner_ref, prev_ref, base_ref, swing_ref = refs[-7:]
    cols = nodes // 2
    count = lax.axis_size("tile")
    rotated = (lax.axis_index("tile") + count - rows // 2) % count
    group, row_index = rotated // rows, rotated % rows
    is_upper = group == step
    first = jnp.where(is_upper, cols, 0)

    @pl.when(is_upper | (group == step - 1) | (step == 1))
    def _():
        row_offset, col_offset = offsets_ref[step, 0], offsets_ref[step, 1]
        area = float(PATCH * PATCH)

        if step > 1:
            row_shift = own_row(relax(section_grid(refs[0][...], step - 1, rows), rows, nodes), row_index)
            base_ref[...], swing_ref[...] = kernels_of(row_shift, first, cols, nodes)

        def stage(index, slot):
            patch = jnp.where(is_upper, other_ref[:, columns(index)], own_ref[:, columns(index)])
            if step > 1:
                patch = warp_indexed(patch, base_ref, swing_ref, index, cols)
            prev_ref[index] = patch

        looped(cols, stage)

        def one(index, slot):
            own = jnp.where(is_upper, own_ref[:, columns(index + cols)], other_ref[:, columns(index)])
            prev = prev_ref[index]
            own_corner, prev_corner = (x[0:1, 0:1].astype(f32) for x in (own, prev))
            corner_ref[0, pl.ds(index, 1), :] = jnp.broadcast_to(own_corner, (1, LANES))
            corner_ref[1, pl.ds(index, 1), :] = jnp.broadcast_to(prev_corner, (1, LANES))
            sums = moments(own, own_corner) + moments(prev, prev_corner)
            for k, value in enumerate(sums):
                sums_ref[k, rows_of(index), :] = value
            level = own_corner * prev_corner

            def put(third, band):
                for side in range(2):
                    band_ref[side, rows_of(third * cols + index), :] = band[:, side * LANES : (side + 1) * LANES]

            correlate(own, prev, level, col_offset, put)

        looped(cols, one)
        reduce = lambda value: jnp.sum(value, axis=1, keepdims=True)
        mean = lambda k: reduce(
            functools.reduce(jnp.add, [sums_ref[k, pl.ds(row, cols, stride=8), :] for row in range(8)])
        ) * (1.0 / area)
        own_sum, own_square, prev_sum, prev_square = (mean(k) for k in range(4))
        spread = jnp.sqrt(
            (jnp.maximum(own_square - own_sum * own_sum, 0.0) + 1e-5)
            * (jnp.maximum(prev_square - prev_sum * prev_sum, 0.0) + 1e-5)
        )
        scale = sharpness / area / spread
        level = corner_ref[0] * prev_sum + corner_ref[1] * own_sum + own_sum * prev_sum
        level = jnp.concatenate([level, level], axis=1) * area
        third, row_lag = lag_layout((cols, 2 * LANES), 1)
        inside = (jnp.abs(row_lag - row_offset) <= HALF) & (third < THIRD)
        weight = row_moment = col_moment = 0.0
        for i in range(THIRD):
            score = (band_sum(band_ref, 8 * cols * i, cols) - level) * scale
            weights = jnp.where(inside, jnp.exp(jnp.where(inside, score, 0.0)), 0.0)
            col_lag = i + THIRD * third - HALF + col_offset
            weight = weight + weights
            row_moment = row_moment + weights * row_lag.astype(f32)
            col_moment = col_moment + weights * col_lag.astype(f32)
        inverse = 1.0 / reduce(weight)
        flow_row = reduce(row_moment) * inverse
        flow_col = reduce(col_moment) * inverse
        shape = (cols, LANES)
        node, lane = iota(shape, 0) + first, iota(shape, 1)
        sent = jnp.where(lane == node, flow_row, jnp.where(lane == node + nodes, flow_col, 0.0))
        sent = jnp.sum(sent, axis=0, keepdims=True)
        masks = mask_ref[...].astype(f32)
        gap = jnp.zeros((1, MASK_LANE - 2 * nodes), f32)
        masks = jnp.concatenate([gap, jnp.zeros((1, 2 * nodes), f32), masks, masks, gap], axis=1)
        sent = sent + jnp.where(is_upper, masks, 0.0)
        out_ref[...] = jnp.broadcast_to(sent, out_ref.shape)


def home_kernel(rows, nodes, own_ref, *refs):
    out_ref, shift_ref, base_ref, swing_ref = refs[-4:]
    count = lax.axis_size("tile")
    rotated = (lax.axis_index("tile") + count - rows // 2) % count
    group, row_index = rotated // rows, rotated % rows
    grid = None
    for step in range(1, SECTIONS):
        part = section_grid(refs[step - 1][...], step, rows)
        grid = part if grid is None else jnp.where(group == step, part, grid)
    row_shift = own_row(relax(grid, rows, nodes), row_index)
    row_shift = jnp.where(group == 0, 0.0, row_shift)
    shift_ref[0, :, :] = row_shift[:, :nodes]
    shift_ref[1, :, :] = pltpu.roll(row_shift, LANES - nodes, 1)[:, :nodes]
    base_ref[...], swing_ref[...] = kernels_of(row_shift, 0, nodes, nodes)

    def one(index, slot):
        here = columns(index)
        out_ref[:, here] = warp_indexed(own_ref[:, here], base_ref, swing_ref, index, nodes)

    looped(nodes, one)


def half_kernel(rows, own_ref, out_ref, semaphore):
    count = lax.axis_size("tile")
    rotated = (lax.axis_index("tile") + count - rows // 2) % count
    width = out_ref.shape[1]
    start = pl.multiple_of(jnp.where(rotated // rows == 0, width, 0), PATCH)
    copy = pltpu.make_async_copy(own_ref.at[:, pl.ds(start, width)], out_ref, semaphore)
    copy.start()
    copy.wait()


def shards(sections, valid_mask, coarse_offsets):
    count = lax.axis_size("tile")
    rows = count // SECTIONS
    nodes = valid_mask.shape[1]
    place = lambda group, row: (group * rows + row + rows // 2) % count
    group = (lax.axis_index("tile") + count - rows // 2) % count // rows
    moved = lambda value, pairs: lax.ppermute(value, "tile", pairs)

    def half_of(source, lower):
        start = jnp.where(group == lower, half * PATCH, 0)
        return lax.dynamic_slice_in_dim(source, start, half * PATCH, 1)

    def swapped(sent, lower):
        ends = [(place(lower, i), place(lower + 1, i)) for i in range(rows)]
        return moved(sent, ends + [(d, s) for s, d in ends])

    vmem = pl.BlockSpec(memory_space=pltpu.VMEM)
    params = pltpu.CompilerParams(vmem_limit_bytes=16 * 2**20)
    half = nodes // 2
    first_half = pl.pallas_call(
        functools.partial(half_kernel, rows),
        out_shape=jax.ShapeDtypeStruct((PATCH, half * PATCH), bf16),
        in_specs=[pl.BlockSpec(memory_space=pltpu.HBM)],
        out_specs=pl.BlockSpec(memory_space=pltpu.HBM),
        scratch_shapes=[pltpu.SemaphoreType.DMA],
        compiler_params=pltpu.CompilerParams(vmem_limit_bytes=60 * 2**20),
        name="half",
    )(sections)
    source, first_half = lax.optimization_barrier((sections, first_half))
    others = [swapped(first_half, 0), swapped(half_of(source, 1), 1)]

    gathered = []
    for step in range(1, SECTIONS):
        extra = gathered[-1:]
        sent = pl.pallas_call(
            functools.partial(chain_kernel, step, rows, nodes),
            out_shape=jax.ShapeDtypeStruct((count, LANES), f32),
            in_specs=[vmem] * (4 + len(extra)),
            out_specs=vmem,
            scratch_shapes=[
                pltpu.VMEM((2, THIRD * half * 8, LANES), f32),
                pltpu.VMEM((4, half * 8, LANES), f32),
                pltpu.VMEM((2, half, LANES), f32),
                pltpu.VMEM((half, PATCH, PATCH), bf16),
                pltpu.VMEM((2 * half, LANES), f32),
                pltpu.VMEM((2 * half, LANES), f32),
            ],
            compiler_params=params,
            name=f"chain{step}",
        )(coarse_offsets, sections, others[step - 1], valid_mask, *extra)
        gathered.append(lax.all_to_all(sent, "tile", 0, 0, tiled=True))
        if step + 1 < SECTIONS - 1:
            later, sent = lax.optimization_barrier((half_of(source, step + 1), sent))
            others.append(swapped(later, step + 1))
    return pl.pallas_call(
        functools.partial(home_kernel, rows, nodes),
        out_shape=(
            jax.ShapeDtypeStruct(sections.shape, bf16),
            jax.ShapeDtypeStruct((2, 1, nodes), f32),
        ),
        in_specs=[vmem] * SECTIONS,
        out_specs=(vmem, vmem),
        scratch_shapes=[pltpu.VMEM((2 * nodes, LANES), f32)] * 2,
        compiler_params=params,
        name="home",
    )(sections, *gathered)


def solution(mesh):
    placed = (P(("parts", "tile"), None), P(("parts", "tile"), None), P("parts", None))
    return jax.shard_map(
        shards,
        mesh=mesh,
        in_specs=placed,
        out_specs=(P(("parts", "tile"), None), P(None, ("parts", "tile"), None)),
        check_vma=False,
    )
```

```python
import functools
import math

import jax
import jax.numpy as jnp
from jax import lax
from jax.experimental import pallas as pl
from jax.experimental.pallas import tpu as pltpu
from jax.sharding import PartitionSpec as P

SECTIONS = 4
PATCH = 128
HALF = 4
SWEEPS = 3
LANES = 128
WIDTH = 2 * HALF + 1
MASK_LANE = 64
GROUP = 16
THIRD = WIDTH // 3
SPAN = PATCH // 2 + 16

sharpness = 12.0
anchor_weight = 2.0
f32 = jnp.float32
bf16 = jnp.bfloat16


def iota(shape, axis):
    return lax.broadcasted_iota(jnp.int32, shape, axis)


def split(value):
    high = value.astype(bf16)
    return high, (value - high.astype(f32)).astype(bf16)


def dot(lhs, rhs):
    return jnp.dot(lhs, rhs, preferred_element_type=f32)


def dot_t(lhs, rhs):
    return lax.dot_general(lhs, rhs, (((1,), (1,)), ((), ())), preferred_element_type=f32)


def sine(x):
    y = x * x
    acc = jnp.full_like(x, 1.0 / math.factorial(13))
    for order in (11, 9, 7, 5, 3, 1):
        acc = (-1.0 if order % 4 == 3 else 1.0) / math.factorial(order) + y * acc
    return x * acc


def cosine(x):
    y = x * x
    acc = jnp.full_like(x, 1.0 / math.factorial(12))
    for order in (10, 8, 6, 4, 2, 0):
        acc = (-1.0 if order % 4 == 2 else 1.0) / math.factorial(order) + y * acc
    return acc


def total(value):
    return jnp.sum(jnp.sum(value, axis=0, keepdims=True), axis=1, keepdims=True)


def tile_sum(value):
    parts = [value[r : r + 8] for r in range(0, value.shape[0], 8)]
    while len(parts) > 1:
        parts = [x + y for x, y in zip(parts[::2], parts[1::2])]
    return parts[0]


def sign_tile(shape):
    return (1 - 2 * ((iota(shape, 0) + iota(shape, 1)) % 2)).astype(f32)


def section_grid(gathered, step, rows):
    count = gathered.shape[0]
    out = None
    for group in (step - 1, step):
        start = (group * rows + rows // 2) % count
        part = jnp.concatenate([gathered[start:], gathered[:start]], axis=0)[:rows]
        out = part if out is None else out + part
    return jnp.concatenate([out, jnp.zeros((8 - rows % 8, LANES), f32)], axis=0)


def relax(grid, rows, nodes):
    shape = grid.shape
    row, lane = iota(shape, 0), iota(shape, 1)
    col = lane % nodes
    valid = (row < rows) & (lane < 2 * nodes)
    mask = pltpu.roll(grid, LANES - MASK_LANE, 1)
    one = lambda cond: jnp.where(cond, 1.0, 0.0)
    count = one(row > 0) + one(row < rows - 1) + one(col > 0) + one(col < nodes - 1)
    weight = anchor_weight * mask
    inverse = 1.0 / jnp.where(valid, weight + count, 1.0)
    pulled = weight * grid
    shift = jnp.where(valid, grid * mask, 0.0)
    for _ in range(SWEEPS):
        near = pltpu.roll(shift, 1, 0) + pltpu.roll(shift, shape[0] - 1, 0)
        near += jnp.where(col > 0, pltpu.roll(shift, 1, 1), 0.0)
        near += jnp.where(col < nodes - 1, pltpu.roll(shift, LANES - 1, 1), 0.0)
        shift = jnp.where(valid, (pulled + near) * inverse, 0.0)
    return shift


def own_row(shift, index):
    return jnp.sum(jnp.where(iota(shift.shape, 0) == index, shift, 0.0), axis=0, keepdims=True)


def kernels_of(row_shift, first, cols, nodes):
    shape = (2 * cols, LANES)
    sub, lane = iota(shape, 0), iota(shape, 1)
    is_row = sub < cols
    target = first + jnp.where(is_row, sub, sub - cols + nodes)
    shift = jnp.sum(jnp.where(lane == target, row_shift, 0.0), axis=1, keepdims=True)
    shift = jnp.broadcast_to(shift, shape)
    whole = jnp.floor(shift + 0.5)
    part = shift - whole
    steps = jnp.where(is_row, -lane, lane).astype(f32) + whole
    steps = steps - LANES * jnp.floor((steps + LANES // 2) * (1.0 / LANES))
    sign = lambda n: 1.0 - 2.0 * (n - 2.0 * jnp.floor(n * 0.5))
    swing = sine(part * math.pi)
    angle = (steps + part) * (math.pi / LANES)
    centre = (steps == 0.0) & (jnp.abs(part) < 1e-20)
    below = jnp.where(centre, 1.0, sine(angle))
    base = swing * sign(steps) * (1.0 / LANES) * cosine(angle) / below
    return jnp.where(centre, 1.0, base), swing * sign(whole)


def circulant(row):
    return pltpu.roll(jnp.broadcast_to(row, (PATCH, LANES)), 0, 1, stride=1, stride_axis=0)


def warp(patch, row_base, col_base, row_swing, col_swing, nyquist):
    row_high, row_low = split(circulant(row_base))
    col_high, col_low = split(circulant(col_base))
    inner = dot(
        jnp.concatenate([patch, patch], axis=1), jnp.concatenate([col_high, col_low], axis=0)
    )
    in_high, in_low = split(inner)
    upper = jnp.concatenate([in_high, in_low], axis=1)
    lower = jnp.concatenate([in_high, jnp.zeros_like(in_low)], axis=1)
    out = dot(
        jnp.concatenate([row_high, row_low], axis=1), jnp.concatenate([upper, lower], axis=0)
    )
    out = out[:, :LANES] + out[:, LANES:]
    factor = row_swing * col_swing * nyquist * (1.0 / (PATCH * PATCH))
    return out - factor * sign_tile((PATCH, LANES))


def lag_layout(shape, axis):
    spot = (iota(shape, axis) + 16) % (2 * LANES)
    return spot // SPAN, 8 - spot % SPAN


def correlate(own, prev, level, column_offset, put):
    own32, prev32 = own.astype(f32), prev.astype(f32)
    half = PATCH // 2
    left, right = [], []
    for i in range(THIRD):
        amount = (PATCH + HALF - i - column_offset) % PATCH
        turned = pltpu.roll(own32, amount, 1)
        low = jnp.concatenate([turned[PATCH - 8 :], turned[: half + 8]], axis=0)
        high = jnp.concatenate([turned[half - 8 :], turned[:8]], axis=0)
        left.append(jnp.concatenate([low, high], axis=1).astype(bf16))
    for j in range(THIRD):
        turned = pltpu.roll(prev32, THIRD * j, 1).astype(bf16) if j else prev
        right.append(jnp.concatenate([turned[:half], turned[half:]], axis=1))
        right.append(jnp.zeros((SPAN - half, 2 * LANES), bf16))
    right.append(jnp.zeros((2 * LANES - THIRD * SPAN, 2 * LANES), bf16))
    product = dot_t(jnp.concatenate(left, axis=0), jnp.concatenate(right, axis=0))
    spot = iota((8, 2 * LANES), 1) % SPAN
    base = jnp.where((spot < half) & (iota((8, 2 * LANES), 1) < THIRD * SPAN), level * (2.0 * LANES), 0.0)
    unused = lag_layout(spot.shape, 1)[1] >= 8 - iota(spot.shape, 0)
    for i in range(THIRD):
        tile = lambda r: product[i * SPAN + 8 * r : i * SPAN + 8 * r + 8]
        band = None
        for k in range(3):
            kept = tile(k)
            for m in range(1, 4 if k == 0 else 3):
                kept = jnp.where(spot >= 8 * k + 24 * m - 16, tile(k + 3 * m), kept)
            kept = kept - base
            kept = pltpu.roll(kept, 2 * LANES - 8 * k, 1) if k else kept
            band = kept if band is None else band + kept
        band = jnp.where(unused, 0.0, band)
        put(i, band)


def band_sum(band_ref, first, cols):
    out = None
    for row in range(8):
        rows = pl.ds(first + row, cols, stride=8)
        part = jnp.concatenate([band_ref[side, rows, :] for side in range(2)], axis=1)
        part = pltpu.roll(part, 2 * LANES - row, 1) if row else part
        out = part if out is None else out + part
    back = lambda lanes: pltpu.roll(out, 2 * LANES - lanes, 1)
    _, row_lag = lag_layout(out.shape, 1)
    return out + back(24) + back(48) + jnp.where(row_lag > 0, back(72), 0.0)


def moments(values, corner):
    values = values.astype(f32) - corner
    return tile_sum(values), tile_sum(values * values)


def looped(count, one):
    width = min(GROUP, count)

    def body(turn, carry):
        for k in range(width):
            one(turn * width + k, k)
        return carry

    if count == width:
        body(0, 0)
    else:
        lax.fori_loop(0, count // width, body, 0)


def rows_of(index):
    return pl.ds(index * 8 if isinstance(index, int) else pl.multiple_of(index * 8, 8), 8)


def columns(index):
    start = index * PATCH
    return pl.ds(start if isinstance(start, int) else pl.multiple_of(start, PATCH), PATCH)


def warp_indexed(patch, base_ref, swing_ref, index, cols):
    nyquist = total(tile_sum(patch.astype(f32)) * sign_tile((8, LANES)))
    return warp(
        patch,
        base_ref[pl.ds(index, 1), :],
        base_ref[pl.ds(index + cols, 1), :],
        swing_ref[pl.ds(index, 1), :],
        swing_ref[pl.ds(index + cols, 1), :],
        nyquist,
    ).astype(bf16)


def chain_kernel(step, rows, nodes, offsets_ref, own_ref, other_ref, mask_ref, *refs):
    out_ref, band_ref, sums_ref, corner_ref, prev_ref, base_ref, swing_ref = refs[-7:]
    cols = nodes // 2
    count = lax.axis_size("tile")
    rotated = (lax.axis_index("tile") + count - rows // 2) % count
    group, row_index = rotated // rows, rotated % rows
    is_upper = group == step
    first = jnp.where(is_upper, cols, 0)

    @pl.when(is_upper | (group == step - 1) | (step == 1))
    def _():
        row_offset, col_offset = offsets_ref[step, 0], offsets_ref[step, 1]
        area = float(PATCH * PATCH)

        if step > 1:
            row_shift = own_row(relax(section_grid(refs[0][...], step - 1, rows), rows, nodes), row_index)
            base_ref[...], swing_ref[...] = kernels_of(row_shift, first, cols, nodes)

        def stage(index, slot):
            patch = jnp.where(is_upper, other_ref[:, columns(index)], own_ref[:, columns(index)])
            if step > 1:
                patch = warp_indexed(patch, base_ref, swing_ref, index, cols)
            prev_ref[index] = patch

        looped(cols, stage)

        def one(index, slot):
            own = jnp.where(is_upper, own_ref[:, columns(index + cols)], other_ref[:, columns(index)])
            prev = prev_ref[index]
            own_corner, prev_corner = (x[0:1, 0:1].astype(f32) for x in (own, prev))
            corner_ref[0, pl.ds(index, 1), :] = jnp.broadcast_to(own_corner, (1, LANES))
            corner_ref[1, pl.ds(index, 1), :] = jnp.broadcast_to(prev_corner, (1, LANES))
            sums = moments(own, own_corner) + moments(prev, prev_corner)
            for k, value in enumerate(sums):
                sums_ref[k, rows_of(index), :] = value
            level = own_corner * prev_corner

            def put(third, band):
                for side in range(2):
                    band_ref[side, rows_of(third * cols + index), :] = band[:, side * LANES : (side + 1) * LANES]

            correlate(own, prev, level, col_offset, put)

        looped(cols, one)
        reduce = lambda value: jnp.sum(value, axis=1, keepdims=True)
        mean = lambda k: reduce(
            functools.reduce(jnp.add, [sums_ref[k, pl.ds(row, cols, stride=8), :] for row in range(8)])
        ) * (1.0 / area)
        own_sum, own_square, prev_sum, prev_square = (mean(k) for k in range(4))
        spread = jnp.sqrt(
            (jnp.maximum(own_square - own_sum * own_sum, 0.0) + 1e-5)
            * (jnp.maximum(prev_square - prev_sum * prev_sum, 0.0) + 1e-5)
        )
        scale = sharpness / area / spread
        level = corner_ref[0] * prev_sum + corner_ref[1] * own_sum + own_sum * prev_sum
        level = jnp.concatenate([level, level], axis=1) * area
        third, row_lag = lag_layout((cols, 2 * LANES), 1)
        inside = (jnp.abs(row_lag - row_offset) <= HALF) & (third < THIRD)
        weight = row_moment = col_moment = 0.0
        for i in range(THIRD):
            score = (band_sum(band_ref, 8 * cols * i, cols) - level) * scale
            weights = jnp.where(inside, jnp.exp(jnp.where(inside, score, 0.0)), 0.0)
            col_lag = i + THIRD * third - HALF + col_offset
            weight = weight + weights
            row_moment = row_moment + weights * row_lag.astype(f32)
            col_moment = col_moment + weights * col_lag.astype(f32)
        inverse = 1.0 / reduce(weight)
        flow_row = reduce(row_moment) * inverse
        flow_col = reduce(col_moment) * inverse
        shape = (cols, LANES)
        node, lane = iota(shape, 0) + first, iota(shape, 1)
        sent = jnp.where(lane == node, flow_row, jnp.where(lane == node + nodes, flow_col, 0.0))
        sent = jnp.sum(sent, axis=0, keepdims=True)
        masks = mask_ref[...].astype(f32)
        gap = jnp.zeros((1, MASK_LANE - 2 * nodes), f32)
        masks = jnp.concatenate([gap, jnp.zeros((1, 2 * nodes), f32), masks, masks, gap], axis=1)
        sent = sent + jnp.where(is_upper, masks, 0.0)
        out_ref[...] = jnp.broadcast_to(sent, out_ref.shape)


def home_kernel(rows, nodes, own_ref, *refs):
    out_ref, shift_ref, base_ref, swing_ref = refs[-4:]
    count = lax.axis_size("tile")
    rotated = (lax.axis_index("tile") + count - rows // 2) % count
    group, row_index = rotated // rows, rotated % rows
    grid = None
    for step in range(1, SECTIONS):
        part = section_grid(refs[step - 1][...], step, rows)
        grid = part if grid is None else jnp.where(group == step, part, grid)
    row_shift = own_row(relax(grid, rows, nodes), row_index)
    row_shift = jnp.where(group == 0, 0.0, row_shift)
    shift_ref[0, :, :] = row_shift[:, :nodes]
    shift_ref[1, :, :] = pltpu.roll(row_shift, LANES - nodes, 1)[:, :nodes]
    base_ref[...], swing_ref[...] = kernels_of(row_shift, 0, nodes, nodes)

    def one(index, slot):
        here = columns(index)
        out_ref[:, here] = warp_indexed(own_ref[:, here], base_ref, swing_ref, index, nodes)

    looped(nodes, one)


def shards(sections, valid_mask, coarse_offsets):
    count = lax.axis_size("tile")
    rows = count // SECTIONS
    nodes = valid_mask.shape[1]
    place = lambda group, row: (group * rows + row + rows // 2) % count
    group = (lax.axis_index("tile") + count - rows // 2) % count // rows
    moved = lambda value, pairs: lax.ppermute(value, "tile", pairs)

    def half_of(source, lower):
        start = jnp.where(group == lower, half * PATCH, 0)
        return lax.dynamic_slice_in_dim(source, start, half * PATCH, 1)

    def swapped(sent, lower):
        ends = [(place(lower, i), place(lower + 1, i)) for i in range(rows)]
        return moved(sent, ends + [(d, s) for s, d in ends])

    half = nodes // 2
    first_half = half_of(sections, 0)
    source, first_half = lax.optimization_barrier((sections, first_half))
    others = [swapped(first_half, 0)]
    others += [swapped(half_of(source, lower), lower) for lower in range(1, SECTIONS - 1)]

    vmem = pl.BlockSpec(memory_space=pltpu.VMEM)
    params = pltpu.CompilerParams(vmem_limit_bytes=16 * 2**20)
    gathered = []
    for step in range(1, SECTIONS):
        extra = gathered[-1:]
        sent = pl.pallas_call(
            functools.partial(chain_kernel, step, rows, nodes),
            out_shape=jax.ShapeDtypeStruct((count, LANES), f32),
            in_specs=[vmem] * (4 + len(extra)),
            out_specs=vmem,
            scratch_shapes=[
                pltpu.VMEM((2, THIRD * half * 8, LANES), f32),
                pltpu.VMEM((4, half * 8, LANES), f32),
                pltpu.VMEM((2, half, LANES), f32),
                pltpu.VMEM((half, PATCH, PATCH), bf16),
                pltpu.VMEM((2 * half, LANES), f32),
                pltpu.VMEM((2 * half, LANES), f32),
            ],
            compiler_params=params,
            name=f"chain{step}",
        )(coarse_offsets, sections, others[step - 1], valid_mask, *extra)
        gathered.append(lax.all_to_all(sent, "tile", 0, 0, tiled=True))
    return pl.pallas_call(
        functools.partial(home_kernel, rows, nodes),
        out_shape=(
            jax.ShapeDtypeStruct(sections.shape, bf16),
            jax.ShapeDtypeStruct((2, 1, nodes), f32),
        ),
        in_specs=[vmem] * SECTIONS,
        out_specs=(vmem, vmem),
        scratch_shapes=[pltpu.VMEM((2 * nodes, LANES), f32)] * 2,
        compiler_params=params,
        name="home",
    )(sections, *gathered)


def solution(mesh):
    placed = (P(("parts", "tile"), None), P(("parts", "tile"), None), P("parts", None))
    return jax.shard_map(
        shards,
        mesh=mesh,
        in_specs=placed,
        out_specs=(P(("parts", "tile"), None), P(None, ("parts", "tile"), None)),
        check_vma=False,
    )
```

```python
import functools
import math

import jax
import jax.numpy as jnp
from jax import lax
from jax.experimental import pallas as pl
from jax.experimental.pallas import tpu as pltpu
from jax.sharding import PartitionSpec as P

SECTIONS = 4
PATCH = 128
HALF = 4
SWEEPS = 3
LANES = 128
WIDTH = 2 * HALF + 1
MASK_LANE = 64
GROUP = 16
THIRD = WIDTH // 3
SPAN = PATCH // 2 + 16

sharpness = 12.0
anchor_weight = 2.0
f32 = jnp.float32
bf16 = jnp.bfloat16


def iota(shape, axis):
    return lax.broadcasted_iota(jnp.int32, shape, axis)


def split(value):
    high = value.astype(bf16)
    return high, (value - high.astype(f32)).astype(bf16)


def dot(lhs, rhs):
    return jnp.dot(lhs, rhs, preferred_element_type=f32)


def dot_t(lhs, rhs):
    return lax.dot_general(lhs, rhs, (((1,), (1,)), ((), ())), preferred_element_type=f32)


def sine(x):
    y = x * x
    acc = jnp.full_like(x, 1.0 / math.factorial(13))
    for order in (11, 9, 7, 5, 3, 1):
        acc = (-1.0 if order % 4 == 3 else 1.0) / math.factorial(order) + y * acc
    return x * acc


def cosine(x):
    y = x * x
    acc = jnp.full_like(x, 1.0 / math.factorial(12))
    for order in (10, 8, 6, 4, 2, 0):
        acc = (-1.0 if order % 4 == 2 else 1.0) / math.factorial(order) + y * acc
    return acc


def total(value):
    return jnp.sum(jnp.sum(value, axis=0, keepdims=True), axis=1, keepdims=True)


def tile_sum(value):
    parts = [value[r : r + 8] for r in range(0, value.shape[0], 8)]
    while len(parts) > 1:
        parts = [x + y for x, y in zip(parts[::2], parts[1::2])]
    return parts[0]


def sign_tile(shape):
    return (1 - 2 * ((iota(shape, 0) + iota(shape, 1)) % 2)).astype(f32)


def section_grid(gathered, step, rows):
    count = gathered.shape[0]
    out = None
    for group in (step - 1, step):
        start = (group * rows + rows // 2) % count
        part = jnp.concatenate([gathered[start:], gathered[:start]], axis=0)[:rows]
        out = part if out is None else out + part
    return jnp.concatenate([out, jnp.zeros((8 - rows % 8, LANES), f32)], axis=0)


def relax(grid, rows, nodes):
    shape = grid.shape
    row, lane = iota(shape, 0), iota(shape, 1)
    col = lane % nodes
    valid = (row < rows) & (lane < 2 * nodes)
    mask = pltpu.roll(grid, LANES - MASK_LANE, 1)
    one = lambda cond: jnp.where(cond, 1.0, 0.0)
    count = one(row > 0) + one(row < rows - 1) + one(col > 0) + one(col < nodes - 1)
    weight = anchor_weight * mask
    inverse = 1.0 / jnp.where(valid, weight + count, 1.0)
    pulled = weight * grid
    shift = jnp.where(valid, grid * mask, 0.0)
    for _ in range(SWEEPS):
        near = pltpu.roll(shift, 1, 0) + pltpu.roll(shift, shape[0] - 1, 0)
        near += jnp.where(col > 0, pltpu.roll(shift, 1, 1), 0.0)
        near += jnp.where(col < nodes - 1, pltpu.roll(shift, LANES - 1, 1), 0.0)
        shift = jnp.where(valid, (pulled + near) * inverse, 0.0)
    return shift


def own_row(shift, index):
    return jnp.sum(jnp.where(iota(shift.shape, 0) == index, shift, 0.0), axis=0, keepdims=True)


def kernels_of(row_shift, first, cols, nodes):
    shape = (2 * cols, LANES)
    sub, lane = iota(shape, 0), iota(shape, 1)
    is_row = sub < cols
    target = first + jnp.where(is_row, sub, sub - cols + nodes)
    shift = jnp.sum(jnp.where(lane == target, row_shift, 0.0), axis=1, keepdims=True)
    shift = jnp.broadcast_to(shift, shape)
    whole = jnp.floor(shift + 0.5)
    part = shift - whole
    steps = jnp.where(is_row, -lane, lane).astype(f32) + whole
    steps = steps - LANES * jnp.floor((steps + LANES // 2) * (1.0 / LANES))
    sign = lambda n: 1.0 - 2.0 * (n - 2.0 * jnp.floor(n * 0.5))
    swing = sine(part * math.pi)
    angle = (steps + part) * (math.pi / LANES)
    centre = (steps == 0.0) & (jnp.abs(part) < 1e-20)
    below = jnp.where(centre, 1.0, sine(angle))
    base = swing * sign(steps) * (1.0 / LANES) * cosine(angle) / below
    return jnp.where(centre, 1.0, base), swing * sign(whole)


def circulant(row):
    return pltpu.roll(jnp.broadcast_to(row, (PATCH, LANES)), 0, 1, stride=1, stride_axis=0)


def warp(patch, row_base, col_base, row_swing, col_swing, nyquist):
    row_high, row_low = split(circulant(row_base))
    col_high, col_low = split(circulant(col_base))
    inner = dot(
        jnp.concatenate([patch, patch], axis=1), jnp.concatenate([col_high, col_low], axis=0)
    )
    in_high, in_low = split(inner)
    upper = jnp.concatenate([in_high, in_low], axis=1)
    lower = jnp.concatenate([in_high, jnp.zeros_like(in_low)], axis=1)
    out = dot(
        jnp.concatenate([row_high, row_low], axis=1), jnp.concatenate([upper, lower], axis=0)
    )
    out = out[:, :LANES] + out[:, LANES:]
    factor = row_swing * col_swing * nyquist * (1.0 / (PATCH * PATCH))
    return out - factor * sign_tile((PATCH, LANES))


def lag_layout(shape, axis):
    spot = (iota(shape, axis) + 16) % (2 * LANES)
    return spot // SPAN, 8 - spot % SPAN


def correlate(own, prev, level, column_offset, put):
    own32, prev32 = own.astype(f32), prev.astype(f32)
    half = PATCH // 2
    left, right = [], []
    for i in range(THIRD):
        amount = (PATCH + HALF - i - column_offset) % PATCH
        turned = pltpu.roll(own32, amount, 1)
        low = jnp.concatenate([turned[PATCH - 8 :], turned[: half + 8]], axis=0)
        high = jnp.concatenate([turned[half - 8 :], turned[:8]], axis=0)
        left.append(jnp.concatenate([low, high], axis=1).astype(bf16))
    for j in range(THIRD):
        turned = pltpu.roll(prev32, THIRD * j, 1).astype(bf16) if j else prev
        right.append(jnp.concatenate([turned[:half], turned[half:]], axis=1))
        right.append(jnp.zeros((SPAN - half, 2 * LANES), bf16))
    right.append(jnp.zeros((2 * LANES - THIRD * SPAN, 2 * LANES), bf16))
    product = dot_t(jnp.concatenate(left, axis=0), jnp.concatenate(right, axis=0))
    spot = iota((8, 2 * LANES), 1) % SPAN
    base = jnp.where((spot < half) & (iota((8, 2 * LANES), 1) < THIRD * SPAN), level * (2.0 * LANES), 0.0)
    unused = lag_layout(spot.shape, 1)[1] >= 8 - iota(spot.shape, 0)
    for i in range(THIRD):
        tile = lambda r: product[i * SPAN + 8 * r : i * SPAN + 8 * r + 8]
        band = None
        for k in range(3):
            kept = tile(k)
            for m in range(1, 4 if k == 0 else 3):
                kept = jnp.where(spot >= 8 * k + 24 * m - 16, tile(k + 3 * m), kept)
            kept = kept - base
            kept = pltpu.roll(kept, 2 * LANES - 8 * k, 1) if k else kept
            band = kept if band is None else band + kept
        band = jnp.where(unused, 0.0, band)
        put(i, band)


def band_sum(band_ref, first, cols):
    out = None
    for row in range(8):
        rows = pl.ds(first + row, cols, stride=8)
        part = jnp.concatenate([band_ref[side, rows, :] for side in range(2)], axis=1)
        part = pltpu.roll(part, 2 * LANES - row, 1) if row else part
        out = part if out is None else out + part
    back = lambda lanes: pltpu.roll(out, 2 * LANES - lanes, 1)
    _, row_lag = lag_layout(out.shape, 1)
    return out + back(24) + back(48) + jnp.where(row_lag > 0, back(72), 0.0)


def moments(values, corner):
    values = values.astype(f32) - corner
    return tile_sum(values), tile_sum(values * values)


def looped(count, one):
    width = min(GROUP, count)

    def body(turn, carry):
        for k in range(width):
            one(turn * width + k, k)
        return carry

    if count == width:
        body(0, 0)
    else:
        lax.fori_loop(0, count // width, body, 0)


def rows_of(index):
    return pl.ds(index * 8 if isinstance(index, int) else pl.multiple_of(index * 8, 8), 8)


def columns(index):
    start = index * PATCH
    return pl.ds(start if isinstance(start, int) else pl.multiple_of(start, PATCH), PATCH)


def warp_indexed(patch, base_ref, swing_ref, index, cols):
    nyquist = total(tile_sum(patch.astype(f32)) * sign_tile((8, LANES)))
    return warp(
        patch,
        base_ref[pl.ds(index, 1), :],
        base_ref[pl.ds(index + cols, 1), :],
        swing_ref[pl.ds(index, 1), :],
        swing_ref[pl.ds(index + cols, 1), :],
        nyquist,
    ).astype(bf16)


def chain_kernel(step, rows, nodes, offsets_ref, own_ref, other_ref, mask_ref, *refs):
    out_ref, band_ref, sums_ref, corner_ref, prev_ref, base_ref, swing_ref = refs[-7:]
    cols = nodes // 2
    count = lax.axis_size("tile")
    rotated = (lax.axis_index("tile") + count - rows // 2) % count
    group, row_index = rotated // rows, rotated % rows
    is_upper = group == step
    first = jnp.where(is_upper, cols, 0)

    @pl.when(is_upper | (group == step - 1) | (step == 1))
    def _():
        row_offset, col_offset = offsets_ref[step, 0], offsets_ref[step, 1]
        area = float(PATCH * PATCH)

        if step > 1:
            row_shift = own_row(relax(section_grid(refs[0][...], step - 1, rows), rows, nodes), row_index)
            base_ref[...], swing_ref[...] = kernels_of(row_shift, first, cols, nodes)

        def stage(index, slot):
            patch = jnp.where(is_upper, other_ref[:, columns(index)], own_ref[:, columns(index)])
            if step > 1:
                patch = warp_indexed(patch, base_ref, swing_ref, index, cols)
            prev_ref[index] = patch

        looped(cols, stage)

        def one(index, slot):
            own = jnp.where(is_upper, own_ref[:, columns(index + cols)], other_ref[:, columns(index)])
            prev = prev_ref[index]
            own_corner, prev_corner = (x[0:1, 0:1].astype(f32) for x in (own, prev))
            corner_ref[0, pl.ds(index, 1), :] = jnp.broadcast_to(own_corner, (1, LANES))
            corner_ref[1, pl.ds(index, 1), :] = jnp.broadcast_to(prev_corner, (1, LANES))
            sums = moments(own, own_corner) + moments(prev, prev_corner)
            for k, value in enumerate(sums):
                sums_ref[k, rows_of(index), :] = value
            level = own_corner * prev_corner

            def put(third, band):
                for side in range(2):
                    band_ref[side, rows_of(third * cols + index), :] = band[:, side * LANES : (side + 1) * LANES]

            correlate(own, prev, level, col_offset, put)

        looped(cols, one)
        reduce = lambda value: jnp.sum(value, axis=1, keepdims=True)
        mean = lambda k: reduce(
            functools.reduce(jnp.add, [sums_ref[k, pl.ds(row, cols, stride=8), :] for row in range(8)])
        ) * (1.0 / area)
        own_sum, own_square, prev_sum, prev_square = (mean(k) for k in range(4))
        spread = jnp.sqrt(
            (jnp.maximum(own_square - own_sum * own_sum, 0.0) + 1e-5)
            * (jnp.maximum(prev_square - prev_sum * prev_sum, 0.0) + 1e-5)
        )
        scale = sharpness / area / spread
        level = corner_ref[0] * prev_sum + corner_ref[1] * own_sum + own_sum * prev_sum
        level = jnp.concatenate([level, level], axis=1) * area
        third, row_lag = lag_layout((cols, 2 * LANES), 1)
        inside = (jnp.abs(row_lag - row_offset) <= HALF) & (third < THIRD)
        weight = row_moment = col_moment = 0.0
        for i in range(THIRD):
            score = (band_sum(band_ref, 8 * cols * i, cols) - level) * scale
            weights = jnp.where(inside, jnp.exp(jnp.where(inside, score, 0.0)), 0.0)
            col_lag = i + THIRD * third - HALF + col_offset
            weight = weight + weights
            row_moment = row_moment + weights * row_lag.astype(f32)
            col_moment = col_moment + weights * col_lag.astype(f32)
        inverse = 1.0 / reduce(weight)
        flow_row = reduce(row_moment) * inverse
        flow_col = reduce(col_moment) * inverse
        shape = (cols, LANES)
        node, lane = iota(shape, 0) + first, iota(shape, 1)
        sent = jnp.where(lane == node, flow_row, jnp.where(lane == node + nodes, flow_col, 0.0))
        sent = jnp.sum(sent, axis=0, keepdims=True)
        masks = mask_ref[...].astype(f32)
        gap = jnp.zeros((1, MASK_LANE - 2 * nodes), f32)
        masks = jnp.concatenate([gap, jnp.zeros((1, 2 * nodes), f32), masks, masks, gap], axis=1)
        sent = sent + jnp.where(is_upper, masks, 0.0)
        out_ref[...] = jnp.broadcast_to(sent, out_ref.shape)


def home_kernel(rows, nodes, own_ref, *refs):
    out_ref, shift_ref, base_ref, swing_ref = refs[-4:]
    count = lax.axis_size("tile")
    rotated = (lax.axis_index("tile") + count - rows // 2) % count
    group, row_index = rotated // rows, rotated % rows
    grid = None
    for step in range(1, SECTIONS):
        part = section_grid(refs[step - 1][...], step, rows)
        grid = part if grid is None else jnp.where(group == step, part, grid)
    row_shift = own_row(relax(grid, rows, nodes), row_index)
    row_shift = jnp.where(group == 0, 0.0, row_shift)
    shift_ref[0, :, :] = row_shift[:, :nodes]
    shift_ref[1, :, :] = pltpu.roll(row_shift, LANES - nodes, 1)[:, :nodes]
    base_ref[...], swing_ref[...] = kernels_of(row_shift, 0, nodes, nodes)

    def one(index, slot):
        here = columns(index)
        out_ref[:, here] = warp_indexed(own_ref[:, here], base_ref, swing_ref, index, nodes)

    looped(nodes, one)


def shards(sections, valid_mask, coarse_offsets):
    count = lax.axis_size("tile")
    rows = count // SECTIONS
    nodes = valid_mask.shape[1]
    place = lambda group, row: (group * rows + row + rows // 2) % count
    group = (lax.axis_index("tile") + count - rows // 2) % count // rows
    moved = lambda value, pairs: lax.ppermute(value, "tile", pairs)

    def half_of(source, lower):
        start = jnp.where(group == lower, half * PATCH, 0)
        return lax.dynamic_slice_in_dim(source, start, half * PATCH, 1)

    def swapped(sent, lower):
        ends = [(place(lower, i), place(lower + 1, i)) for i in range(rows)]
        return moved(sent, ends + [(d, s) for s, d in ends])

    half = nodes // 2
    first_half = half_of(sections, 0)
    source, first_half = lax.optimization_barrier((sections, first_half))
    others = [swapped(first_half, 0)]
    others += [swapped(half_of(source, lower), lower) for lower in range(1, SECTIONS - 1)]

    vmem = pl.BlockSpec(memory_space=pltpu.VMEM)
    params = pltpu.CompilerParams(vmem_limit_bytes=16 * 2**20)
    gathered = []
    for step in range(1, SECTIONS):
        extra = gathered[-1:]
        sent = pl.pallas_call(
            functools.partial(chain_kernel, step, rows, nodes),
            out_shape=jax.ShapeDtypeStruct((count, LANES), f32),
            in_specs=[vmem] * (4 + len(extra)),
            out_specs=vmem,
            scratch_shapes=[
                pltpu.VMEM((2, THIRD * half * 8, LANES), f32),
                pltpu.VMEM((4, half * 8, LANES), f32),
                pltpu.VMEM((2, half, LANES), f32),
                pltpu.VMEM((half, PATCH, PATCH), bf16),
                pltpu.VMEM((2 * half, LANES), f32),
                pltpu.VMEM((2 * half, LANES), f32),
            ],
            compiler_params=params,
            name=f"chain{step}",
        )(coarse_offsets, sections, others[step - 1], valid_mask, *extra)
        if 1 < step < SECTIONS - 1:
            sent, others[step] = lax.optimization_barrier((sent, others[step]))
        gathered.append(lax.all_to_all(sent, "tile", 0, 0, tiled=True))
    return pl.pallas_call(
        functools.partial(home_kernel, rows, nodes),
        out_shape=(
            jax.ShapeDtypeStruct(sections.shape, bf16),
            jax.ShapeDtypeStruct((2, 1, nodes), f32),
        ),
        in_specs=[vmem] * SECTIONS,
        out_specs=(vmem, vmem),
        scratch_shapes=[pltpu.VMEM((2 * nodes, LANES), f32)] * 2,
        compiler_params=params,
        name="home",
    )(sections, *gathered)


def solution(mesh):
    placed = (P(("parts", "tile"), None), P(("parts", "tile"), None), P("parts", None))
    return jax.shard_map(
        shards,
        mesh=mesh,
        in_specs=placed,
        out_specs=(P(("parts", "tile"), None), P(None, ("parts", "tile"), None)),
        check_vma=False,
    )
```

```python
import functools
import math

import jax
import jax.numpy as jnp
from jax import lax
from jax.experimental import pallas as pl
from jax.experimental.pallas import tpu as pltpu
from jax.sharding import PartitionSpec as P

SECTIONS = 4
PATCH = 128
HALF = 4
SWEEPS = 3
LANES = 128
WIDTH = 2 * HALF + 1
MASK_LANE = 64
GROUP = 16
THIRD = WIDTH // 3
SPAN = PATCH // 2 + 16

sharpness = 12.0
anchor_weight = 2.0
f32 = jnp.float32
bf16 = jnp.bfloat16


def iota(shape, axis):
    return lax.broadcasted_iota(jnp.int32, shape, axis)


def split(value):
    high = value.astype(bf16)
    return high, (value - high.astype(f32)).astype(bf16)


def dot(lhs, rhs):
    return jnp.dot(lhs, rhs, preferred_element_type=f32)


def dot_t(lhs, rhs):
    return lax.dot_general(lhs, rhs, (((1,), (1,)), ((), ())), preferred_element_type=f32)


def sine(x):
    y = x * x
    acc = jnp.full_like(x, 1.0 / math.factorial(13))
    for order in (11, 9, 7, 5, 3, 1):
        acc = (-1.0 if order % 4 == 3 else 1.0) / math.factorial(order) + y * acc
    return x * acc


def cosine(x):
    y = x * x
    acc = jnp.full_like(x, 1.0 / math.factorial(12))
    for order in (10, 8, 6, 4, 2, 0):
        acc = (-1.0 if order % 4 == 2 else 1.0) / math.factorial(order) + y * acc
    return acc


def total(value):
    return jnp.sum(jnp.sum(value, axis=0, keepdims=True), axis=1, keepdims=True)


def tile_sum(value):
    parts = [value[r : r + 8] for r in range(0, value.shape[0], 8)]
    while len(parts) > 1:
        parts = [x + y for x, y in zip(parts[::2], parts[1::2])]
    return parts[0]


def sign_tile(shape):
    return (1 - 2 * ((iota(shape, 0) + iota(shape, 1)) % 2)).astype(f32)


def section_grid(gathered, step, rows):
    count = gathered.shape[0]
    out = None
    for group in (step - 1, step):
        start = (group * rows + rows // 2) % count
        part = jnp.concatenate([gathered[start:], gathered[:start]], axis=0)[:rows]
        out = part if out is None else out + part
    return jnp.concatenate([out, jnp.zeros((8 - rows % 8, LANES), f32)], axis=0)


def relax(grid, rows, nodes):
    shape = grid.shape
    row, lane = iota(shape, 0), iota(shape, 1)
    col = lane % nodes
    valid = (row < rows) & (lane < 2 * nodes)
    mask = pltpu.roll(grid, LANES - MASK_LANE, 1)
    one = lambda cond: jnp.where(cond, 1.0, 0.0)
    count = one(row > 0) + one(row < rows - 1) + one(col > 0) + one(col < nodes - 1)
    weight = anchor_weight * mask
    inverse = 1.0 / jnp.where(valid, weight + count, 1.0)
    pulled = weight * grid
    shift = jnp.where(valid, grid * mask, 0.0)
    for _ in range(SWEEPS):
        near = pltpu.roll(shift, 1, 0) + pltpu.roll(shift, shape[0] - 1, 0)
        near += jnp.where(col > 0, pltpu.roll(shift, 1, 1), 0.0)
        near += jnp.where(col < nodes - 1, pltpu.roll(shift, LANES - 1, 1), 0.0)
        shift = jnp.where(valid, (pulled + near) * inverse, 0.0)
    return shift


def own_row(shift, index):
    return jnp.sum(jnp.where(iota(shift.shape, 0) == index, shift, 0.0), axis=0, keepdims=True)


def kernels_of(row_shift, first, cols, nodes):
    shape = (2 * cols, LANES)
    sub, lane = iota(shape, 0), iota(shape, 1)
    is_row = sub < cols
    target = first + jnp.where(is_row, sub, sub - cols + nodes)
    shift = jnp.sum(jnp.where(lane == target, row_shift, 0.0), axis=1, keepdims=True)
    shift = jnp.broadcast_to(shift, shape)
    whole = jnp.floor(shift + 0.5)
    part = shift - whole
    steps = jnp.where(is_row, -lane, lane).astype(f32) + whole
    steps = steps - LANES * jnp.floor((steps + LANES // 2) * (1.0 / LANES))
    sign = lambda n: 1.0 - 2.0 * (n - 2.0 * jnp.floor(n * 0.5))
    swing = sine(part * math.pi)
    angle = (steps + part) * (math.pi / LANES)
    centre = (steps == 0.0) & (jnp.abs(part) < 1e-20)
    below = jnp.where(centre, 1.0, sine(angle))
    base = swing * sign(steps) * (1.0 / LANES) * cosine(angle) / below
    return jnp.where(centre, 1.0, base), swing * sign(whole)


def circulant(row):
    return pltpu.roll(jnp.broadcast_to(row, (PATCH, LANES)), 0, 1, stride=1, stride_axis=0)


def warp(patch, row_base, col_base, row_swing, col_swing, nyquist):
    row_high, row_low = split(circulant(row_base))
    col_high, col_low = split(circulant(col_base))
    inner = dot(
        jnp.concatenate([patch, patch], axis=1), jnp.concatenate([col_high, col_low], axis=0)
    )
    in_high, in_low = split(inner)
    upper = jnp.concatenate([in_high, in_low], axis=1)
    lower = jnp.concatenate([in_high, jnp.zeros_like(in_low)], axis=1)
    out = dot(
        jnp.concatenate([row_high, row_low], axis=1), jnp.concatenate([upper, lower], axis=0)
    )
    out = out[:, :LANES] + out[:, LANES:]
    factor = row_swing * col_swing * nyquist * (1.0 / (PATCH * PATCH))
    return out - factor * sign_tile((PATCH, LANES))


def lag_layout(shape, axis):
    spot = (iota(shape, axis) + 16) % (2 * LANES)
    return spot // SPAN, 8 - spot % SPAN


def correlate(own, prev, level, column_offset, put):
    own32, prev32 = own.astype(f32), prev.astype(f32)
    half = PATCH // 2
    left, right = [], []
    for i in range(THIRD):
        amount = (PATCH + HALF - i - column_offset) % PATCH
        turned = pltpu.roll(own32, amount, 1)
        low = jnp.concatenate([turned[PATCH - 8 :], turned[: half + 8]], axis=0)
        high = jnp.concatenate([turned[half - 8 :], turned[:8]], axis=0)
        left.append(jnp.concatenate([low, high], axis=1).astype(bf16))
    for j in range(THIRD):
        turned = pltpu.roll(prev32, THIRD * j, 1).astype(bf16) if j else prev
        right.append(jnp.concatenate([turned[:half], turned[half:]], axis=1))
        right.append(jnp.zeros((SPAN - half, 2 * LANES), bf16))
    right.append(jnp.zeros((2 * LANES - THIRD * SPAN, 2 * LANES), bf16))
    product = dot_t(jnp.concatenate(left, axis=0), jnp.concatenate(right, axis=0))
    spot = iota((8, 2 * LANES), 1) % SPAN
    base = jnp.where((spot < half) & (iota((8, 2 * LANES), 1) < THIRD * SPAN), level * (2.0 * LANES), 0.0)
    unused = lag_layout(spot.shape, 1)[1] >= 8 - iota(spot.shape, 0)
    for i in range(THIRD):
        tile = lambda r: product[i * SPAN + 8 * r : i * SPAN + 8 * r + 8]
        band = None
        for k in range(3):
            kept = tile(k)
            for m in range(1, 4 if k == 0 else 3):
                kept = jnp.where(spot >= 8 * k + 24 * m - 16, tile(k + 3 * m), kept)
            kept = kept - base
            kept = pltpu.roll(kept, 2 * LANES - 8 * k, 1) if k else kept
            band = kept if band is None else band + kept
        band = jnp.where(unused, 0.0, band)
        put(i, band)


def band_sum(band_ref, first, cols):
    out = None
    for row in range(8):
        rows = pl.ds(first + row, cols, stride=8)
        part = jnp.concatenate([band_ref[side, rows, :] for side in range(2)], axis=1)
        part = pltpu.roll(part, 2 * LANES - row, 1) if row else part
        out = part if out is None else out + part
    back = lambda lanes: pltpu.roll(out, 2 * LANES - lanes, 1)
    _, row_lag = lag_layout(out.shape, 1)
    return out + back(24) + back(48) + jnp.where(row_lag > 0, back(72), 0.0)


def moments(values, corner):
    values = values.astype(f32) - corner
    return tile_sum(values), tile_sum(values * values)


def looped(count, one):
    width = min(GROUP, count)

    def body(turn, carry):
        for k in range(width):
            one(turn * width + k, k)
        return carry

    if count == width:
        body(0, 0)
    else:
        lax.fori_loop(0, count // width, body, 0)


def rows_of(index):
    return pl.ds(index * 8 if isinstance(index, int) else pl.multiple_of(index * 8, 8), 8)


def columns(index):
    start = index * PATCH
    return pl.ds(start if isinstance(start, int) else pl.multiple_of(start, PATCH), PATCH)


def warp_indexed(patch, base_ref, swing_ref, index, cols):
    nyquist = total(tile_sum(patch.astype(f32)) * sign_tile((8, LANES)))
    return warp(
        patch,
        base_ref[pl.ds(index, 1), :],
        base_ref[pl.ds(index + cols, 1), :],
        swing_ref[pl.ds(index, 1), :],
        swing_ref[pl.ds(index + cols, 1), :],
        nyquist,
    ).astype(bf16)


def chain_kernel(step, rows, nodes, offsets_ref, own_ref, other_ref, mask_ref, *refs):
    out_ref, band_ref, sums_ref, corner_ref, prev_ref, base_ref, swing_ref = refs[-7:]
    cols = nodes // 2
    count = lax.axis_size("tile")
    rotated = (lax.axis_index("tile") + count - rows // 2) % count
    group, row_index = rotated // rows, rotated % rows
    is_upper = group == step
    first = jnp.where(is_upper, cols, 0)

    @pl.when(is_upper | (group == step - 1) | (step == 1))
    def _():
        row_offset, col_offset = offsets_ref[step, 0], offsets_ref[step, 1]
        area = float(PATCH * PATCH)

        if step > 1:
            row_shift = own_row(relax(refs[0][...], rows, nodes), row_index)
            base_ref[...], swing_ref[...] = kernels_of(row_shift, first, cols, nodes)

        def stage(index, slot):
            patch = jnp.where(is_upper, other_ref[:, columns(index)], own_ref[:, columns(index)])
            if step > 1:
                patch = warp_indexed(patch, base_ref, swing_ref, index, cols)
            prev_ref[index] = patch

        looped(cols, stage)

        def one(index, slot):
            own = jnp.where(is_upper, own_ref[:, columns(index + cols)], other_ref[:, columns(index)])
            prev = prev_ref[index]
            own_corner, prev_corner = (x[0:1, 0:1].astype(f32) for x in (own, prev))
            corner_ref[0, pl.ds(index, 1), :] = jnp.broadcast_to(own_corner, (1, LANES))
            corner_ref[1, pl.ds(index, 1), :] = jnp.broadcast_to(prev_corner, (1, LANES))
            sums = moments(own, own_corner) + moments(prev, prev_corner)
            for k, value in enumerate(sums):
                sums_ref[k, rows_of(index), :] = value
            level = own_corner * prev_corner

            def put(third, band):
                for side in range(2):
                    band_ref[side, rows_of(third * cols + index), :] = band[:, side * LANES : (side + 1) * LANES]

            correlate(own, prev, level, col_offset, put)

        looped(cols, one)
        reduce = lambda value: jnp.sum(value, axis=1, keepdims=True)
        mean = lambda k: reduce(
            functools.reduce(jnp.add, [sums_ref[k, pl.ds(row, cols, stride=8), :] for row in range(8)])
        ) * (1.0 / area)
        own_sum, own_square, prev_sum, prev_square = (mean(k) for k in range(4))
        spread = jnp.sqrt(
            (jnp.maximum(own_square - own_sum * own_sum, 0.0) + 1e-5)
            * (jnp.maximum(prev_square - prev_sum * prev_sum, 0.0) + 1e-5)
        )
        scale = sharpness / area / spread
        level = corner_ref[0] * prev_sum + corner_ref[1] * own_sum + own_sum * prev_sum
        level = jnp.concatenate([level, level], axis=1) * area
        third, row_lag = lag_layout((cols, 2 * LANES), 1)
        inside = (jnp.abs(row_lag - row_offset) <= HALF) & (third < THIRD)
        weight = row_moment = col_moment = 0.0
        for i in range(THIRD):
            score = (band_sum(band_ref, 8 * cols * i, cols) - level) * scale
            weights = jnp.where(inside, jnp.exp(jnp.where(inside, score, 0.0)), 0.0)
            col_lag = i + THIRD * third - HALF + col_offset
            weight = weight + weights
            row_moment = row_moment + weights * row_lag.astype(f32)
            col_moment = col_moment + weights * col_lag.astype(f32)
        inverse = 1.0 / reduce(weight)
        flow_row = reduce(row_moment) * inverse
        flow_col = reduce(col_moment) * inverse
        shape = (cols, LANES)
        node, lane = iota(shape, 0) + first, iota(shape, 1)
        sent = jnp.where(lane == node, flow_row, jnp.where(lane == node + nodes, flow_col, 0.0))
        sent = jnp.sum(sent, axis=0, keepdims=True)
        masks = mask_ref[...].astype(f32)
        gap = jnp.zeros((1, MASK_LANE - 2 * nodes), f32)
        masks = jnp.concatenate([gap, jnp.zeros((1, 2 * nodes), f32), masks, masks, gap], axis=1)
        sent = sent + jnp.where(is_upper, masks, 0.0)
        out_ref[...] = jnp.broadcast_to(sent, out_ref.shape)


def home_kernel(rows, nodes, own_ref, *refs):
    out_ref, shift_ref, base_ref, swing_ref = refs[-4:]
    count = lax.axis_size("tile")
    rotated = (lax.axis_index("tile") + count - rows // 2) % count
    group, row_index = rotated // rows, rotated % rows
    grid = None
    for step in range(1, SECTIONS):
        part = section_grid(refs[step - 1][...], step, rows)
        grid = part if grid is None else jnp.where(group == step, part, grid)
    row_shift = own_row(relax(grid, rows, nodes), row_index)
    row_shift = jnp.where(group == 0, 0.0, row_shift)
    shift_ref[0, :, :] = row_shift[:, :nodes]
    shift_ref[1, :, :] = pltpu.roll(row_shift, LANES - nodes, 1)[:, :nodes]
    base_ref[...], swing_ref[...] = kernels_of(row_shift, 0, nodes, nodes)

    def one(index, slot):
        here = columns(index)
        out_ref[:, here] = warp_indexed(own_ref[:, here], base_ref, swing_ref, index, nodes)

    looped(nodes, one)


def shards(sections, valid_mask, coarse_offsets):
    count = lax.axis_size("tile")
    rows = count // SECTIONS
    nodes = valid_mask.shape[1]
    place = lambda group, row: (group * rows + row + rows // 2) % count
    group = (lax.axis_index("tile") + count - rows // 2) % count // rows
    moved = lambda value, pairs: lax.ppermute(value, "tile", pairs)

    def half_of(source, lower):
        start = jnp.where(group == lower, half * PATCH, 0)
        return lax.dynamic_slice_in_dim(source, start, half * PATCH, 1)

    def swapped(sent, lower):
        ends = [(place(lower, i), place(lower + 1, i)) for i in range(rows)]
        return moved(sent, ends + [(d, s) for s, d in ends])

    half = nodes // 2
    first_half = half_of(sections, 0)
    source, first_half = lax.optimization_barrier((sections, first_half))
    others = [swapped(first_half, 0)]
    others += [swapped(half_of(source, lower), lower) for lower in range(1, SECTIONS - 1)]

    vmem = pl.BlockSpec(memory_space=pltpu.VMEM)
    params = pltpu.CompilerParams(vmem_limit_bytes=16 * 2**20)
    gathered = []
    for step in range(1, SECTIONS):
        extra = [section_grid(gathered[-1], step - 1, rows)] if gathered else []
        sent = pl.pallas_call(
            functools.partial(chain_kernel, step, rows, nodes),
            out_shape=jax.ShapeDtypeStruct((count, LANES), f32),
            in_specs=[vmem] * (4 + len(extra)),
            out_specs=vmem,
            scratch_shapes=[
                pltpu.VMEM((2, THIRD * half * 8, LANES), f32),
                pltpu.VMEM((4, half * 8, LANES), f32),
                pltpu.VMEM((2, half, LANES), f32),
                pltpu.VMEM((half, PATCH, PATCH), bf16),
                pltpu.VMEM((2 * half, LANES), f32),
                pltpu.VMEM((2 * half, LANES), f32),
            ],
            compiler_params=params,
            name=f"chain{step}",
        )(coarse_offsets, sections, others[step - 1], valid_mask, *extra)
        if 1 < step < SECTIONS - 1:
            sent, others[step] = lax.optimization_barrier((sent, others[step]))
        gathered.append(lax.all_to_all(sent, "tile", 0, 0, tiled=True))
    return pl.pallas_call(
        functools.partial(home_kernel, rows, nodes),
        out_shape=(
            jax.ShapeDtypeStruct(sections.shape, bf16),
            jax.ShapeDtypeStruct((2, 1, nodes), f32),
        ),
        in_specs=[vmem] * SECTIONS,
        out_specs=(vmem, vmem),
        scratch_shapes=[pltpu.VMEM((2 * nodes, LANES), f32)] * 2,
        compiler_params=params,
        name="home",
    )(sections, *gathered)


def solution(mesh):
    placed = (P(("parts", "tile"), None), P(("parts", "tile"), None), P("parts", None))
    return jax.shard_map(
        shards,
        mesh=mesh,
        in_specs=placed,
        out_specs=(P(("parts", "tile"), None), P(None, ("parts", "tile"), None)),
        check_vma=False,
    )
```

```python
import functools
import math

import jax
import jax.numpy as jnp
from jax import lax
from jax.experimental import pallas as pl
from jax.experimental.pallas import tpu as pltpu
from jax.sharding import PartitionSpec as P

SECTIONS = 4
PATCH = 128
HALF = 4
SWEEPS = 3
LANES = 128
WIDTH = 2 * HALF + 1
MASK_LANE = 64
GROUP = 16
THIRD = WIDTH // 3
SPAN = PATCH // 2 + 16

sharpness = 12.0
anchor_weight = 2.0
f32 = jnp.float32
bf16 = jnp.bfloat16


def iota(shape, axis):
    return lax.broadcasted_iota(jnp.int32, shape, axis)


def split(value):
    high = value.astype(bf16)
    return high, (value - high.astype(f32)).astype(bf16)


def dot(lhs, rhs):
    return jnp.dot(lhs, rhs, preferred_element_type=f32)


def dot_t(lhs, rhs):
    return lax.dot_general(lhs, rhs, (((1,), (1,)), ((), ())), preferred_element_type=f32)


def sine(x):
    y = x * x
    acc = jnp.full_like(x, 1.0 / math.factorial(13))
    for order in (11, 9, 7, 5, 3, 1):
        acc = (-1.0 if order % 4 == 3 else 1.0) / math.factorial(order) + y * acc
    return x * acc


def cosine(x):
    y = x * x
    acc = jnp.full_like(x, 1.0 / math.factorial(12))
    for order in (10, 8, 6, 4, 2, 0):
        acc = (-1.0 if order % 4 == 2 else 1.0) / math.factorial(order) + y * acc
    return acc


def total(value):
    return jnp.sum(jnp.sum(value, axis=0, keepdims=True), axis=1, keepdims=True)


def tile_sum(value):
    parts = [value[r : r + 8] for r in range(0, value.shape[0], 8)]
    while len(parts) > 1:
        parts = [x + y for x, y in zip(parts[::2], parts[1::2])]
    return parts[0]


def sign_tile(shape):
    return (1 - 2 * ((iota(shape, 0) + iota(shape, 1)) % 2)).astype(f32)


def section_grid(gathered, step, rows):
    count = gathered.shape[0]
    out = None
    for group in (step - 1, step):
        start = (group * rows + rows // 2) % count
        part = jnp.concatenate([gathered[start:], gathered[:start]], axis=0)[:rows]
        out = part if out is None else out + part
    return jnp.concatenate([out, jnp.zeros((8 - rows % 8, LANES), f32)], axis=0)


def relax(grid, rows, nodes):
    shape = grid.shape
    row, lane = iota(shape, 0), iota(shape, 1)
    col = lane % nodes
    valid = (row < rows) & (lane < 2 * nodes)
    mask = pltpu.roll(grid, LANES - MASK_LANE, 1)
    one = lambda cond: jnp.where(cond, 1.0, 0.0)
    count = one(row > 0) + one(row < rows - 1) + one(col > 0) + one(col < nodes - 1)
    weight = anchor_weight * mask
    inverse = 1.0 / jnp.where(valid, weight + count, 1.0)
    pulled = weight * grid
    shift = jnp.where(valid, grid * mask, 0.0)
    for _ in range(SWEEPS):
        near = pltpu.roll(shift, 1, 0) + pltpu.roll(shift, shape[0] - 1, 0)
        near += jnp.where(col > 0, pltpu.roll(shift, 1, 1), 0.0)
        near += jnp.where(col < nodes - 1, pltpu.roll(shift, LANES - 1, 1), 0.0)
        shift = jnp.where(valid, (pulled + near) * inverse, 0.0)
    return shift


def own_row(shift, index):
    return jnp.sum(jnp.where(iota(shift.shape, 0) == index, shift, 0.0), axis=0, keepdims=True)


def kernels_of(row_shift, first, cols, nodes):
    shape = (2 * cols, LANES)
    sub, lane = iota(shape, 0), iota(shape, 1)
    is_row = sub < cols
    target = first + jnp.where(is_row, sub, sub - cols + nodes)
    shift = jnp.sum(jnp.where(lane == target, row_shift, 0.0), axis=1, keepdims=True)
    shift = jnp.broadcast_to(shift, shape)
    whole = jnp.floor(shift + 0.5)
    part = shift - whole
    steps = jnp.where(is_row, -lane, lane).astype(f32) + whole
    steps = steps - LANES * jnp.floor((steps + LANES // 2) * (1.0 / LANES))
    sign = lambda n: 1.0 - 2.0 * (n - 2.0 * jnp.floor(n * 0.5))
    swing = sine(part * math.pi)
    angle = (steps + part) * (math.pi / LANES)
    centre = (steps == 0.0) & (jnp.abs(part) < 1e-20)
    below = jnp.where(centre, 1.0, sine(angle))
    base = swing * sign(steps) * (1.0 / LANES) * cosine(angle) / below
    return jnp.where(centre, 1.0, base), swing * sign(whole)


def circulant(row):
    return pltpu.roll(jnp.broadcast_to(row, (PATCH, LANES)), 0, 1, stride=1, stride_axis=0)


def warp(patch, row_base, col_base, row_swing, col_swing, nyquist):
    row_high, row_low = split(circulant(row_base))
    col_high, col_low = split(circulant(col_base))
    inner = dot(
        jnp.concatenate([patch, patch], axis=1), jnp.concatenate([col_high, col_low], axis=0)
    )
    in_high, in_low = split(inner)
    upper = jnp.concatenate([in_high, in_low], axis=1)
    lower = jnp.concatenate([in_high, jnp.zeros_like(in_low)], axis=1)
    out = dot(
        jnp.concatenate([row_high, row_low], axis=1), jnp.concatenate([upper, lower], axis=0)
    )
    out = out[:, :LANES] + out[:, LANES:]
    factor = row_swing * col_swing * nyquist * (1.0 / (PATCH * PATCH))
    return out - factor * sign_tile((PATCH, LANES))


def lag_layout(shape, axis):
    spot = (iota(shape, axis) + 16) % (2 * LANES)
    return spot // SPAN, 8 - spot % SPAN


def correlate(own, prev, level, column_offset, put):
    own32, prev32 = own.astype(f32), prev.astype(f32)
    half = PATCH // 2
    left, right = [], []
    for i in range(THIRD):
        amount = (PATCH + HALF - i - column_offset) % PATCH
        turned = pltpu.roll(own32, amount, 1)
        low = jnp.concatenate([turned[PATCH - 8 :], turned[: half + 8]], axis=0)
        high = jnp.concatenate([turned[half - 8 :], turned[:8]], axis=0)
        left.append(jnp.concatenate([low, high], axis=1).astype(bf16))
    for j in range(THIRD):
        turned = pltpu.roll(prev32, THIRD * j, 1).astype(bf16) if j else prev
        right.append(jnp.concatenate([turned[:half], turned[half:]], axis=1))
        right.append(jnp.zeros((SPAN - half, 2 * LANES), bf16))
    right.append(jnp.zeros((2 * LANES - THIRD * SPAN, 2 * LANES), bf16))
    product = dot_t(jnp.concatenate(left, axis=0), jnp.concatenate(right, axis=0))
    spot = iota((8, 2 * LANES), 1) % SPAN
    base = jnp.where((spot < half) & (iota((8, 2 * LANES), 1) < THIRD * SPAN), level * (2.0 * LANES), 0.0)
    unused = lag_layout(spot.shape, 1)[1] >= 8 - iota(spot.shape, 0)
    for i in range(THIRD):
        tile = lambda r: product[i * SPAN + 8 * r : i * SPAN + 8 * r + 8]
        band = None
        for k in range(3):
            kept = tile(k)
            for m in range(1, 4 if k == 0 else 3):
                kept = jnp.where(spot >= 8 * k + 24 * m - 16, tile(k + 3 * m), kept)
            kept = kept - base
            kept = pltpu.roll(kept, 2 * LANES - 8 * k, 1) if k else kept
            band = kept if band is None else band + kept
        band = jnp.where(unused, 0.0, band)
        put(i, band)


def band_sum(band_ref, first, cols):
    out = None
    for row in range(8):
        rows = pl.ds(first + row, cols, stride=8)
        part = jnp.concatenate([band_ref[side, rows, :] for side in range(2)], axis=1)
        part = pltpu.roll(part, 2 * LANES - row, 1) if row else part
        out = part if out is None else out + part
    back = lambda lanes: pltpu.roll(out, 2 * LANES - lanes, 1)
    _, row_lag = lag_layout(out.shape, 1)
    return out + back(24) + back(48) + jnp.where(row_lag > 0, back(72), 0.0)


def moments(values, corner):
    values = values.astype(f32) - corner
    return tile_sum(values), tile_sum(values * values)


def looped(count, one):
    width = min(GROUP, count)

    def body(turn, carry):
        for k in range(width):
            one(turn * width + k, k)
        return carry

    if count == width:
        body(0, 0)
    else:
        lax.fori_loop(0, count // width, body, 0)


def rows_of(index):
    return pl.ds(index * 8 if isinstance(index, int) else pl.multiple_of(index * 8, 8), 8)


def columns(index):
    start = index * PATCH
    return pl.ds(start if isinstance(start, int) else pl.multiple_of(start, PATCH), PATCH)


def warp_indexed(patch, base_ref, swing_ref, index, cols):
    nyquist = total(tile_sum(patch.astype(f32)) * sign_tile((8, LANES)))
    return warp(
        patch,
        base_ref[pl.ds(index, 1), :],
        base_ref[pl.ds(index + cols, 1), :],
        swing_ref[pl.ds(index, 1), :],
        swing_ref[pl.ds(index + cols, 1), :],
        nyquist,
    ).astype(bf16)


def chain_kernel(step, rows, nodes, offsets_ref, own_ref, other_ref, mask_ref, *refs):
    out_ref, band_ref, sums_ref, corner_ref, prev_ref, base_ref, swing_ref = refs[-7:]
    cols = nodes // 2
    count = lax.axis_size("tile")
    rotated = (lax.axis_index("tile") + count - rows // 2) % count
    group, row_index = rotated // rows, rotated % rows
    is_upper = group == step
    first = jnp.where(is_upper, cols, 0)

    @pl.when(is_upper | (group == step - 1) | (step == 1))
    def _():
        row_offset, col_offset = offsets_ref[step, 0], offsets_ref[step, 1]
        area = float(PATCH * PATCH)

        if step > 1:
            row_shift = own_row(relax(refs[0][...], rows, nodes), row_index)
            base_ref[...], swing_ref[...] = kernels_of(row_shift, first, cols, nodes)

        def stage(index, slot):
            patch = jnp.where(is_upper, other_ref[:, columns(index)], own_ref[:, columns(index)])
            if step > 1:
                patch = warp_indexed(patch, base_ref, swing_ref, index, cols)
            prev_ref[index] = patch

        looped(cols, stage)

        def one(index, slot):
            own = jnp.where(is_upper, own_ref[:, columns(index + cols)], other_ref[:, columns(index)])
            prev = prev_ref[index]
            own_corner, prev_corner = (x[0:1, 0:1].astype(f32) for x in (own, prev))
            corner_ref[0, pl.ds(index, 1), :] = jnp.broadcast_to(own_corner, (1, LANES))
            corner_ref[1, pl.ds(index, 1), :] = jnp.broadcast_to(prev_corner, (1, LANES))
            sums = moments(own, own_corner) + moments(prev, prev_corner)
            for k, value in enumerate(sums):
                sums_ref[k, rows_of(index), :] = value
            level = own_corner * prev_corner

            def put(third, band):
                for side in range(2):
                    band_ref[side, rows_of(third * cols + index), :] = band[:, side * LANES : (side + 1) * LANES]

            correlate(own, prev, level, col_offset, put)

        looped(cols, one)
        reduce = lambda value: jnp.sum(value, axis=1, keepdims=True)
        mean = lambda k: reduce(
            functools.reduce(jnp.add, [sums_ref[k, pl.ds(row, cols, stride=8), :] for row in range(8)])
        ) * (1.0 / area)
        own_sum, own_square, prev_sum, prev_square = (mean(k) for k in range(4))
        spread = jnp.sqrt(
            (jnp.maximum(own_square - own_sum * own_sum, 0.0) + 1e-5)
            * (jnp.maximum(prev_square - prev_sum * prev_sum, 0.0) + 1e-5)
        )
        scale = sharpness / area / spread
        level = corner_ref[0] * prev_sum + corner_ref[1] * own_sum + own_sum * prev_sum
        level = jnp.concatenate([level, level], axis=1) * area
        third, row_lag = lag_layout((cols, 2 * LANES), 1)
        inside = (jnp.abs(row_lag - row_offset) <= HALF) & (third < THIRD)
        weight = row_moment = col_moment = 0.0
        for i in range(THIRD):
            score = (band_sum(band_ref, 8 * cols * i, cols) - level) * scale
            weights = jnp.where(inside, jnp.exp(jnp.where(inside, score, 0.0)), 0.0)
            col_lag = i + THIRD * third - HALF + col_offset
            weight = weight + weights
            row_moment = row_moment + weights * row_lag.astype(f32)
            col_moment = col_moment + weights * col_lag.astype(f32)
        inverse = 1.0 / reduce(weight)
        flow_row = reduce(row_moment) * inverse
        flow_col = reduce(col_moment) * inverse
        shape = (cols, LANES)
        node, lane = iota(shape, 0) + first, iota(shape, 1)
        sent = jnp.where(lane == node, flow_row, jnp.where(lane == node + nodes, flow_col, 0.0))
        sent = jnp.sum(sent, axis=0, keepdims=True)
        masks = mask_ref[...].astype(f32)
        gap = jnp.zeros((1, MASK_LANE - 2 * nodes), f32)
        masks = jnp.concatenate([gap, jnp.zeros((1, 2 * nodes), f32), masks, masks, gap], axis=1)
        sent = sent + jnp.where(is_upper, masks, 0.0)
        out_ref[...] = jnp.broadcast_to(sent, out_ref.shape)


def home_kernel(rows, nodes, own_ref, *refs):
    out_ref, shift_ref, base_ref, swing_ref = refs[-4:]
    count = lax.axis_size("tile")
    rotated = (lax.axis_index("tile") + count - rows // 2) % count
    group, row_index = rotated // rows, rotated % rows
    grid = None
    for step in range(1, SECTIONS):
        part = refs[step - 1][...]
        grid = part if grid is None else jnp.where(group == step, part, grid)
    row_shift = own_row(relax(grid, rows, nodes), row_index)
    row_shift = jnp.where(group == 0, 0.0, row_shift)
    shift_ref[0, :, :] = row_shift[:, :nodes]
    shift_ref[1, :, :] = pltpu.roll(row_shift, LANES - nodes, 1)[:, :nodes]
    base_ref[...], swing_ref[...] = kernels_of(row_shift, 0, nodes, nodes)

    def one(index, slot):
        here = columns(index)
        out_ref[:, here] = warp_indexed(own_ref[:, here], base_ref, swing_ref, index, nodes)

    looped(nodes, one)


def shards(sections, valid_mask, coarse_offsets):
    count = lax.axis_size("tile")
    rows = count // SECTIONS
    nodes = valid_mask.shape[1]
    place = lambda group, row: (group * rows + row + rows // 2) % count
    group = (lax.axis_index("tile") + count - rows // 2) % count // rows
    moved = lambda value, pairs: lax.ppermute(value, "tile", pairs)

    def half_of(source, lower):
        start = jnp.where(group == lower, half * PATCH, 0)
        return lax.dynamic_slice_in_dim(source, start, half * PATCH, 1)

    def swapped(sent, lower):
        ends = [(place(lower, i), place(lower + 1, i)) for i in range(rows)]
        return moved(sent, ends + [(d, s) for s, d in ends])

    half = nodes // 2
    first_half = half_of(sections, 0)
    source, first_half = lax.optimization_barrier((sections, first_half))
    others = [swapped(first_half, 0)]
    others += [swapped(half_of(source, lower), lower) for lower in range(1, SECTIONS - 1)]

    vmem = pl.BlockSpec(memory_space=pltpu.VMEM)
    params = pltpu.CompilerParams(vmem_limit_bytes=16 * 2**20)
    gathered = []
    for step in range(1, SECTIONS):
        extra = gathered[-1:]
        sent = pl.pallas_call(
            functools.partial(chain_kernel, step, rows, nodes),
            out_shape=jax.ShapeDtypeStruct((count, LANES), f32),
            in_specs=[vmem] * (4 + len(extra)),
            out_specs=vmem,
            scratch_shapes=[
                pltpu.VMEM((2, THIRD * half * 8, LANES), f32),
                pltpu.VMEM((4, half * 8, LANES), f32),
                pltpu.VMEM((2, half, LANES), f32),
                pltpu.VMEM((half, PATCH, PATCH), bf16),
                pltpu.VMEM((2 * half, LANES), f32),
                pltpu.VMEM((2 * half, LANES), f32),
            ],
            compiler_params=params,
            name=f"chain{step}",
        )(coarse_offsets, sections, others[step - 1], valid_mask, *extra)
        if 1 < step < SECTIONS - 1:
            sent, others[step] = lax.optimization_barrier((sent, others[step]))
        gathered.append(section_grid(lax.all_to_all(sent, "tile", 0, 0, tiled=True), step, rows))
    return pl.pallas_call(
        functools.partial(home_kernel, rows, nodes),
        out_shape=(
            jax.ShapeDtypeStruct(sections.shape, bf16),
            jax.ShapeDtypeStruct((2, 1, nodes), f32),
        ),
        in_specs=[vmem] * SECTIONS,
        out_specs=(vmem, vmem),
        scratch_shapes=[pltpu.VMEM((2 * nodes, LANES), f32)] * 2,
        compiler_params=params,
        name="home",
    )(sections, *gathered)


def solution(mesh):
    placed = (P(("parts", "tile"), None), P(("parts", "tile"), None), P("parts", None))
    return jax.shard_map(
        shards,
        mesh=mesh,
        in_specs=placed,
        out_specs=(P(("parts", "tile"), None), P(None, ("parts", "tile"), None)),
        check_vma=False,
    )
```
